32 devices in a mesh: ctx: 8 (over z, y), wa: 4 (over x, core).
Axes of the slice: x: 2, y: 2, z: 4, core: 2. Of those that a mesh axis runs over, the one named last changes fastest.
Arguments:
- tokens: bfloat16 [4, 1024, 2048], P('wa', 'ctx'), may hold values from -6 to 6
- cotangent: bfloat16 [4, 1024, 2048], P('wa', 'ctx'), may hold values from -6 to 6
- deal: int32 [16], replicated, may hold values from 0 to 15, each once
- doc_lengths: int32 [4, 16], P('wa'), may hold values from 1 to 512, 1024 in all within a row
- doc_adapter: int32 [4, 16], P('wa'), may hold values from 0 to 7
- ln1_gain: float32 [2048], replicated, may hold values from 0.5 to 1.5
- ln1_bias: float32 [2048], replicated, may hold values from -1 to 1
- ln2_gain: float32 [2048], replicated, may hold values from 0.5 to 1.5
- ln2_bias: float32 [2048], replicated, may hold values from -1 to 1
- qkv_weight: bfloat16 [2048, 6144], P('wa'), may hold values from -0.125 to 0.125
- qkv_bias: float32 [6144], replicated, may hold values from -1 to 1
- dense_weight: bfloat16 [2048, 2048], P('wa'), may hold values from -0.5 to 0.5
- dense_bias: float32 [2048], replicated, may hold values from -1 to 1
- in_weight: bfloat16 [2048, 8192], P('wa'), may hold values from -0.125 to 0.125
- in_bias: float32 [8192], replicated, may hold values from -1 to 1
- out_weight: bfloat16 [8192, 2048], P('wa'), may hold values from -0.0625 to 0.0625
- out_bias: float32 [2048], replicated, may hold values from -1 to 1
- qkv_down: bfloat16 [2048, 128], P('wa'), may hold values from -0.125 to 0.125
- qkv_up: bfloat16 [128, 6144], P('wa'), may hold values from -1.5 to 1.5
- dense_down: bfloat16 [2048, 128], P('wa'), may hold values from -0.125 to 0.125
- dense_up: bfloat16 [128, 2048], P('wa'), may hold values from -1.5 to 1.5
- in_down: bfloat16 [2048, 128], P('wa'), may hold values from -0.125 to 0.125
- in_up: bfloat16 [128, 8192], P('wa'), may hold values from -1.5 to 1.5
- out_down: bfloat16 [8192, 128], P('wa'), may hold values from -0.0625 to 0.0625
- out_up: bfloat16 [128, 2048], P('wa'), may hold values from -1.5 to 1.5
Outputs:
- output: bfloat16 [4, 1024, 2048], P('wa', 'ctx')
- tokens_grad: float32 [4, 1024, 2048], P('wa', 'ctx')
- qkv_down_grad: float32 [2048, 128], P('wa')
- qkv_up_grad: float32 [128, 6144], P('wa')
- dense_down_grad: float32 [2048, 128], P('wa')
- dense_up_grad: float32 [128, 2048], P('wa')
- in_down_grad: float32 [2048, 128], P('wa')
- in_up_grad: float32 [128, 8192], P('wa')
- out_down_grad: float32 [8192, 128], P('wa')
- out_up_grad: float32 [128, 2048], P('wa')
The draws below stay inside these ranges and needn't reach their ends.
Inputs may be any that keep to these rules, and one draw needn't show every extreme that they name: `deal`: every block number appears once. `doc_lengths`: the lengths of each pack sum to 1024; the largest of each pack is exactly 512.
All inputs are finite; a program needn't handle non-finite values.
Results may differ from the reference program's by a relative error of at most 0.017.
Values may be sent and summed in bfloat16 or wider, within the bound.
No kernel may reach another device: no remote copies, remote signals or barrier semaphores. Data moves between devices by JAX's collectives and lax.ppermute only.
A program may use at most 448 MiB of HBM per device.

```python
import math
import jax
import jax.numpy as jnp
import numpy as np
from jax import lax

D = 2048
HEADS = 8
HEAD = 256
FF = 8192
ROT = 64
RANK = 16
ADAPTERS = 8
DOCS = 16
PACK = 1024
PACKS = 4
BLOCK = 64
BLOCKS = 16
MAXDOC = 512
ADAPT_COLS = 128


def touch_ends(values, own_key, smallest, high):
    longest = values.shape.index(max(values.shape))
    spots = []
    for shift in (0, 1):
        where = [jax.random.randint(jax.random.fold_in(own_key, axis), (), 0, length) for axis, length in enumerate(values.shape)]
        where[longest] = (where[longest] + shift) % values.shape[longest]
        spots.append(tuple(where))
    return values.at[spots[0]].set(smallest).at[spots[1]].set(high)


def level_of(own_key, shape, pieces, least, largest):
    level = 1.0
    for position, blocks in pieces:
        draws = jax.random.uniform(jax.random.fold_in(jax.random.fold_in(own_key, 6), position), (blocks,), jnp.float32, least / len(pieces), largest / len(pieces))
        level = level * jnp.repeat(jnp.exp(draws), shape[position] // blocks).reshape((-1,) + (1,) * (len(shape) - 1 - position))
    return level


def split_up(count, total, bound, lean):
    weights = [(1 << 20) // math.isqrt(grade ** lean) + 1 for grade in range(2, count + 1)]
    surplus, given = total - bound - (count - 1), [1] * (count - 1)
    while surplus > 0:
        free = [i for i in range(count - 1) if given[i] < bound]
        mass, budget = sum([weights[i] for i in free]), surplus
        for i in free:
            addition = min(bound - given[i], max(1, budget * weights[i] // mass), surplus)
            given[i] = given[i] + addition
            surplus = surplus - addition
    return np.array([bound] + given)


def uneven(own_key, amount, total, bound, slope):
    if amount == 2:
        one = jax.random.randint(own_key, (), max(1, total - bound), min(bound, total - 1) + 1)
        return jnp.stack([one, total - one])
    tallies = jnp.asarray(split_up(amount, total, bound, slope), jnp.int32)
    pairs = (amount - 1) // 2
    donor, sink = tallies[1:1 + 2 * pairs:2], tallies[2:2 + 2 * pairs:2]
    room = jnp.minimum(donor - 1, bound - sink)
    passed = jax.random.randint(jax.random.fold_in(own_key, 1), (pairs,), 0, 1 << 20) % (room + 1)
    tallies = tallies.at[1:1 + 2 * pairs:2].set(donor - passed).at[2:2 + 2 * pairs:2].set(sink + passed)
    return tallies[jax.random.permutation(jax.random.fold_in(own_key, 2), amount)]


def scatter_about(rng, extent, deviation, bound, pieces=(), held_as=jnp.bfloat16):
    factor_of = level_of(rng, extent, pieces, -0.22, 0.18) if pieces else 1.0
    values = jax.random.normal(rng, extent, jnp.float32) * deviation * factor_of
    return jnp.minimum(jnp.maximum(values, -bound), bound).astype(held_as)


def setup_inputs(seed: int = 0) -> dict:
    keys = jax.random.split(jax.random.key(seed), 26)
    return {
        "tokens": scatter_about(keys[0], (PACKS, PACK, D), 1.0, 6.0, ((0, 4), (1, 8))),
        "cotangent": scatter_about(keys[1], (PACKS, PACK, D), 1.0, 6.0, ((0, 4), (1, 8))),
        "deal": jax.random.permutation(keys[2], BLOCKS).astype(jnp.int32),
        "doc_lengths": jax.vmap(lambda own: uneven(own, DOCS, PACK, MAXDOC, 2))(jax.random.split(keys[3], PACKS)).reshape((PACKS, DOCS)).astype(jnp.int32),
        "doc_adapter": touch_ends(jax.random.randint(keys[4], (PACKS, DOCS), 0, ADAPTERS), jax.random.fold_in(keys[4], 1), 0, ADAPTERS - 1).astype(jnp.int32),
        "ln1_gain": jnp.clip(1.0 + 0.1 * jax.random.normal(keys[5], (D,), jnp.float32), 0.5, 1.5),
        "ln1_bias": scatter_about(keys[6], (D,), 0.2, 1.0, (), jnp.float32),
        "ln2_gain": jnp.clip(1.0 + 0.1 * jax.random.normal(keys[7], (D,), jnp.float32), 0.5, 1.5),
        "ln2_bias": scatter_about(keys[8], (D,), 0.2, 1.0, (), jnp.float32),
        "qkv_weight": scatter_about(keys[9], (D, 3 * D), D ** -0.5, 0.125, ((0, 4),)),
        "qkv_bias": scatter_about(keys[10], (3 * D,), 0.2, 1.0, (), jnp.float32),
        "dense_weight": scatter_about(keys[11], (D, D), (D // 16) ** -0.5, 0.5, ((0, 4),)),
        "dense_bias": scatter_about(keys[12], (D,), 0.2, 1.0, (), jnp.float32),
        "in_weight": scatter_about(keys[13], (D, FF), D ** -0.5, 0.125, ((0, 4),)),
        "in_bias": scatter_about(keys[14], (FF,), 0.2, 1.0, (), jnp.float32),
        "out_weight": scatter_about(keys[15], (FF, D), FF ** -0.5, 0.0625, ((0, 4),)),
        "out_bias": scatter_about(keys[16], (D,), 0.2, 1.0, (), jnp.float32),
        "qkv_down": scatter_about(keys[17], (D, ADAPT_COLS), D ** -0.5, 0.125, ((0, 4),)),
        "qkv_up": scatter_about(keys[18], (ADAPT_COLS, 3 * D), RANK ** -0.5, 1.5, ((0, 4),)),
        "dense_down": scatter_about(keys[19], (D, ADAPT_COLS), D ** -0.5, 0.125, ((0, 4),)),
        "dense_up": scatter_about(keys[20], (ADAPT_COLS, D), RANK ** -0.5, 1.5, ((0, 4),)),
        "in_down": scatter_about(keys[21], (D, ADAPT_COLS), D ** -0.5, 0.125, ((0, 4),)),
        "in_up": scatter_about(keys[22], (ADAPT_COLS, FF), RANK ** -0.5, 1.5, ((0, 4),)),
        "out_down": scatter_about(keys[23], (FF, ADAPT_COLS), FF ** -0.5, 0.0625, ((0, 4),)),
        "out_up": scatter_about(keys[24], (ADAPT_COLS, D), RANK ** -0.5, 1.5, ((0, 4),)),
    }


@jax.custom_vjp
def low(v):
    return lax.optimization_barrier(v.astype(jnp.bfloat16)).astype(jnp.float32)

@jax.custom_vjp
def low_back(v):
    return v

def low_keep(v):
    return (low(v), None)

def low_pass(kept, grad):
    return (grad,)

def back_keep(v):
    return (v, None)

def back_low(kept, grad):
    return (low(grad),)
low.defvjp(low_keep, low_pass)
low_back.defvjp(back_keep, back_low)
epsilon = 1e-05
masked_score = -1e+30

def matmul(left, right):
    return jnp.dot(left, right, precision=lax.Precision.HIGHEST, preferred_element_type=jnp.float32)

def layer_norm(values, gain, shift):
    centered = values - lax.optimization_barrier(jnp.mean(values, axis=-1, keepdims=True))
    spread = lax.optimization_barrier(jnp.mean(centered * centered, axis=-1, keepdims=True))
    return centered * lax.rsqrt(spread + epsilon) * gain + shift

def rotate(values, offset):
    half = ROT // 2
    freq = 10000.0 ** (-2.0 * jnp.arange(half, dtype=jnp.float32) / ROT)
    angle = offset.astype(jnp.float32)[:, None] * freq[None, :]
    cosine = jnp.cos(angle)[:, None, :]
    sine = jnp.sin(angle)[:, None, :]
    first = values[..., :half]
    second = values[..., half:ROT]
    return jnp.concatenate([first * cosine - second * sine, second * cosine + first * sine, values[..., ROT:]], axis=-1)

def adapted(inputs, weight, bias, down, up, mask):
    inner = low(low_back(matmul(inputs, down) * mask))
    return matmul(inputs, weight) + bias + matmul(inner, up)

def attention(query, key, value, place, docs):
    count = min(512, PACK)
    scale = 1.0 / math.sqrt(HEAD)

    def block(first):
        part = lax.dynamic_slice_in_dim(query, first, count, 0)
        part_place = lax.dynamic_slice_in_dim(place, first, count, 0)
        part_docs = lax.dynamic_slice_in_dim(docs, first, count, 0)
        scores = jnp.einsum('qhd,khd->hqk', part, key, precision=lax.Precision.HIGHEST) * scale
        allowed = (part_docs[:, None] == docs[None, :]) & (place[None, :] <= part_place[:, None])
        scores = low_back(jnp.where(allowed[None], scores, masked_score))
        top = lax.optimization_barrier(jnp.max(scores, axis=2, keepdims=True))
        weights = jnp.exp(scores - top)
        prob = low(weights / lax.optimization_barrier(jnp.sum(weights, axis=2, keepdims=True)))
        return jnp.einsum('hqk,khd->qhd', prob, value, precision=lax.Precision.HIGHEST).reshape(count, D)
    firsts = jnp.arange(PACK // count, dtype=jnp.int32) * count
    return lax.map(jax.checkpoint(block), firsts).reshape(PACK, D)

def layer(tokens, adapters, weights, place, docs, offset, mask):
    ln1_gain, ln1_bias, ln2_gain, ln2_bias, qkv_weight, qkv_bias, dense_weight, dense_bias, in_weight, in_bias, out_weight, out_bias = weights
    qkv_down, qkv_up, dense_down, dense_up, in_down, in_up, out_down, out_up = adapters
    first_norm = low(layer_norm(tokens, ln1_gain, ln1_bias))
    mixed = low_back(adapted(first_norm, qkv_weight, qkv_bias, qkv_down, qkv_up, mask))
    shape = (PACK, HEADS, HEAD)
    query = low(rotate(mixed[:, :D].reshape(shape), offset))
    key = low(rotate(mixed[:, D:2 * D].reshape(shape), offset))
    value = low(mixed[:, 2 * D:].reshape(shape))
    attended = low(low_back(attention(query, key, value, place, docs)))
    dense = adapted(attended, dense_weight, dense_bias, dense_down, dense_up, mask)
    second_norm = low(layer_norm(tokens, ln2_gain, ln2_bias))
    hidden_pre = low_back(adapted(second_norm, in_weight, in_bias, in_down, in_up, mask))
    hidden = low(jax.nn.gelu(hidden_pre, approximate=False))
    return tokens + dense + adapted(hidden, out_weight, out_bias, out_down, out_up, mask)

def reference(tokens, cotangent, deal, doc_lengths, doc_adapter, ln1_gain, ln1_bias, ln2_gain, ln2_bias, qkv_weight, qkv_bias, dense_weight, dense_bias, in_weight, in_bias, out_weight, out_bias, qkv_down, qkv_up, dense_down, dense_up, in_down, in_up, out_down, out_up):
    weights = tuple((item.astype(jnp.float32) for item in (ln1_gain, ln1_bias, ln2_gain, ln2_bias, qkv_weight, qkv_bias, dense_weight, dense_bias, in_weight, in_bias, out_weight, out_bias)))
    adapters = tuple((item.astype(jnp.float32) for item in (qkv_down, qkv_up, dense_down, dense_up, in_down, in_up, out_down, out_up)))
    positions = jnp.arange(PACK, dtype=jnp.int32)
    place = deal[positions // BLOCK] * BLOCK + positions % BLOCK
    columns = jnp.arange(ADAPT_COLS, dtype=jnp.int32) // RANK
    outputs = []
    input_grads = []
    totals = tuple((jnp.zeros(item.shape, jnp.float32) for item in adapters))
    for member in range(PACKS):
        lengths = doc_lengths[member]
        starts = jnp.cumsum(lengths) - lengths
        inside = (starts[None, :] <= place[:, None]).astype(jnp.int32)
        docs = lax.optimization_barrier(jnp.sum(inside, axis=1)) - 1
        offset = place - starts[docs]
        chosen = doc_adapter[member][docs]
        mask = (columns[None, :] == chosen[:, None]).astype(jnp.float32)

        def local_layer(values, adapter_set):
            return layer(values, adapter_set, weights, place, docs, offset, mask)
        result, pull = jax.vjp(local_layer, tokens[member].astype(jnp.float32), adapters)
        grad_tokens, grad_adapters = pull(cotangent[member].astype(jnp.float32))
        outputs.append(result.astype(jnp.bfloat16))
        input_grads.append(grad_tokens)
        totals = tuple((total + extra for total, extra in zip(totals, grad_adapters)))
    return (jnp.stack(outputs), jnp.stack(input_grads), totals[0], totals[1], totals[2], totals[3], totals[4], totals[5], totals[6], totals[7])
```

```python
import functools
import math

import jax
import jax.numpy as jnp
from jax import lax
from jax.experimental import pallas as pl
from jax.experimental.pallas import tpu as pltpu
from jax.sharding import PartitionSpec as P

HEADS = 8
HEAD = 256
ROT = 64
RANK = 16
BLOCK = 64
ADAPT_COLS = 128
WA = 4
PAIRS = 8

epsilon = 1e-05
masked_score = -1e30
f32 = jnp.float32
bf16 = jnp.bfloat16


def product(left, right):
    return jnp.dot(left, right, preferred_element_type=f32)


def times_t(left, right):
    return lax.dot_general(left, right, (((1,), (1,)), ((), ())), preferred_element_type=f32)


def t_times(left, right):
    return lax.dot_general(left, right, (((0,), (0,)), ((), ())), preferred_element_type=f32)


def swap(value, bits):
    return lax.ppermute(value, "wa", [(i, i ^ bits) for i in range(WA)])


def gather_relative(value):
    mate = swap(value, 1)
    peer = swap(value, 2)
    return [value, mate, peer, swap(peer, 1)]


def absolute(pieces, wa):
    low = wa % 2 == 1
    high = wa >= 2
    p = [
        jnp.where(low, pieces[1], pieces[0]),
        jnp.where(low, pieces[0], pieces[1]),
        jnp.where(low, pieces[3], pieces[2]),
        jnp.where(low, pieces[2], pieces[3]),
    ]
    return [
        jnp.where(high, p[2], p[0]),
        jnp.where(high, p[3], p[1]),
        jnp.where(high, p[0], p[2]),
        jnp.where(high, p[1], p[3]),
    ]


def rotary_tables(offset):
    half = ROT // 2
    freq = 10000.0 ** (-2.0 * jnp.arange(half, dtype=f32) / ROT)
    angle = offset.astype(f32)[:, None] * freq[None, :]
    cosine = jnp.cos(angle)
    sine = jnp.sin(angle)
    rest = jnp.zeros((offset.shape[0], 128 - ROT), f32)
    return (
        jnp.concatenate([cosine, cosine, rest + 1.0], axis=1),
        jnp.concatenate([-sine, sine, rest], axis=1),
    )


def turn_first(values, cosine, sine):
    lane = lax.broadcasted_iota(jnp.int32, values.shape, 1)
    partner = jnp.where(
        lane < ROT // 2, pltpu.roll(values, 128 - ROT // 2, 1), pltpu.roll(values, ROT // 2, 1)
    )
    return values * cosine + partner * sine


def rotate_kernel(value_ref, cos_ref, sin_ref, out_ref):
    for head in range(2):
        first = head * HEAD
        turned = turn_first(value_ref[:, first : first + 128], cos_ref[...], sin_ref[...])
        out_ref[head, :, :128] = turned.astype(bf16)
        out_ref[head, :, 128:] = value_ref[:, first + 128 : first + HEAD].astype(bf16)


def rotate_heads(values, cosine, sine):
    total = values.shape[0]
    rows = total // WA
    return pl.pallas_call(
        rotate_kernel,
        grid=(WA,),
        in_specs=[
            pl.BlockSpec((rows, 2 * HEAD), lambda i: (i, 0)),
            pl.BlockSpec((rows, 128), lambda i: (i, 0)),
            pl.BlockSpec((rows, 128), lambda i: (i, 0)),
        ],
        out_specs=pl.BlockSpec((None, 2, rows, HEAD), lambda i: (i, 0, 0, 0)),
        out_shape=jax.ShapeDtypeStruct((WA, 2, rows, HEAD), bf16),
        cost_estimate=pl.CostEstimate(
            flops=4 * total * 512, bytes_accessed=total * 512 * 6, transcendentals=0
        ),
    )(values, cosine, sine)


def attention_kernel(
    query_ref,
    key_ref,
    value_ref,
    grad_ref,
    begin_ref,
    place_ref,
    key_place_ref,
    q_cos_ref,
    q_sin_ref,
    k_cos_ref,
    k_sin_ref,
    out_ref,
    dq_ref,
    dk_ref,
    dv_ref,
    dk_sum,
    dv_sum,
):
    step = pl.program_id(0)
    scale = 1.0 / math.sqrt(HEAD)

    @pl.when(step == 0)
    def _():
        dk_sum[...] = jnp.zeros_like(dk_sum)
        dv_sum[...] = jnp.zeros_like(dv_sum)

    query = query_ref[...]
    key = key_ref[...]
    value = value_ref[...]
    grad = grad_ref[...]
    key_place = key_place_ref[...]
    allowed = (key_place >= begin_ref[...]) & (key_place <= place_ref[...])
    scores = jnp.where(allowed, times_t(query, key) * scale, masked_score)
    top = jnp.max(scores, axis=1, keepdims=True)
    weights = jnp.exp(scores - top)
    prob = weights * (1.0 / jnp.sum(weights, axis=1, keepdims=True))
    prob_low = prob.astype(bf16)
    out_ref[...] = product(prob_low, value).astype(bf16)
    prob_grad = times_t(grad, value)
    delta = jnp.sum(prob * prob_grad, axis=1, keepdims=True)
    score_grad = (prob * (prob_grad - delta)).astype(bf16)
    dq = product(score_grad, key) * scale
    dq_ref[:, :128] = turn_first(dq[:, :128], q_cos_ref[...], -q_sin_ref[...]).astype(bf16)
    dq_ref[:, 128:] = dq[:, 128:].astype(bf16)
    dk_sum[...] += t_times(score_grad, query)
    dv_sum[...] += t_times(prob_low, grad)

    @pl.when(step == pl.num_programs(0) - 1)
    def _():
        dk = dk_sum[...] * scale
        dk_ref[:, :128] = turn_first(dk[:, :128], k_cos_ref[...], -k_sin_ref[...]).astype(bf16)
        dk_ref[:, 128:] = dk[:, 128:].astype(bf16)
        dv_ref[...] = dv_sum[...].astype(bf16)


def attend(query, key, value, grad, begin, place, key_place, q_tables, k_tables):
    rows = query.shape[0]
    keys = key.shape[0]
    part = min(256, rows)
    by_rows = lambda i: (i, 0)
    whole = lambda i: (0, 0)
    return pl.pallas_call(
        attention_kernel,
        grid=(rows // part,),
        in_specs=[
            pl.BlockSpec((part, HEAD), by_rows),
            pl.BlockSpec((keys, HEAD), whole),
            pl.BlockSpec((keys, HEAD), whole),
            pl.BlockSpec((part, HEAD), by_rows),
            pl.BlockSpec((part, 1), by_rows),
            pl.BlockSpec((part, 1), by_rows),
            pl.BlockSpec((1, keys), whole),
            pl.BlockSpec((part, 128), by_rows),
            pl.BlockSpec((part, 128), by_rows),
            pl.BlockSpec((keys, 128), whole),
            pl.BlockSpec((keys, 128), whole),
        ],
        out_specs=[
            pl.BlockSpec((part, HEAD), by_rows),
            pl.BlockSpec((part, HEAD), by_rows),
            pl.BlockSpec((keys, HEAD), whole),
            pl.BlockSpec((keys, HEAD), whole),
        ],
        out_shape=[
            jax.ShapeDtypeStruct((rows, HEAD), bf16),
            jax.ShapeDtypeStruct((rows, HEAD), bf16),
            jax.ShapeDtypeStruct((keys, HEAD), bf16),
            jax.ShapeDtypeStruct((keys, HEAD), bf16),
        ],
        scratch_shapes=[pltpu.VMEM((keys, HEAD), f32), pltpu.VMEM((keys, HEAD), f32)],
        compiler_params=pltpu.CompilerParams(vmem_limit_bytes=56 * 1024 * 1024),
        cost_estimate=pl.CostEstimate(
            flops=14 * rows * keys * HEAD,
            bytes_accessed=16 * keys * HEAD,
            transcendentals=rows * keys,
        ),
    )(query, key, value, grad, begin, place, key_place, *q_tables, *k_tables)


def body(
    contexts,
    tokens,
    cotangent,
    deal,
    doc_lengths,
    doc_adapter,
    ln1_gain,
    ln1_bias,
    ln2_gain,
    ln2_bias,
    qkv_weight,
    qkv_bias,
    dense_weight,
    dense_bias,
    in_weight,
    in_bias,
    out_weight,
    out_bias,
    qkv_down,
    qkv_up,
    dense_down,
    dense_up,
    in_down,
    in_up,
    out_down,
    out_up,
):
    rows = tokens.shape[1]
    width = tokens.shape[2]
    wa = lax.axis_index("wa")
    ctx = lax.axis_index("ctx")
    mate, peer, far = wa ^ 1, wa ^ 2, wa ^ 3
    total = WA * rows
    own_width = width // WA
    hidden_width = in_weight.shape[1] // WA
    part_cols = ADAPT_COLS // WA
    groups = contexts // PAIRS

    def columns(value, index, size):
        return lax.dynamic_slice_in_dim(value, index * size, size, axis=1)

    def part_rows(value, index, size):
        return lax.dynamic_slice_in_dim(value, index * size, size, axis=0)

    tables = lax.all_gather(
        jnp.concatenate([doc_lengths, doc_adapter], axis=1), "wa", axis=0, tiled=True
    )
    docs_per_pack = doc_lengths.shape[1]
    lengths = tables[:, :docs_per_pack]
    adapters = tables[:, docs_per_pack:]
    starts = jnp.cumsum(lengths, axis=1) - lengths

    def places(first, size):
        slots = first + jnp.arange(size, dtype=jnp.int32)
        blocks = slots // BLOCK
        table = jnp.arange(deal.shape[0], dtype=jnp.int32)
        block = jnp.sum(jnp.where(table[None, :] == blocks[:, None], deal[None, :], 0), axis=1)
        return block * BLOCK + slots % BLOCK

    place = places(ctx * rows, rows)
    inside = starts[:, None, :] <= place[None, :, None]
    docs = jnp.sum(inside.astype(jnp.int32), axis=2) - 1
    begin = jnp.max(jnp.where(inside, starts[:, None, :], 0), axis=2)
    offset = (place[None, :] - begin).reshape(total)
    doc_table = jnp.arange(docs_per_pack, dtype=jnp.int32)
    chosen = jnp.sum(
        jnp.where(docs[:, :, None] == doc_table, adapters[:, None, :], 0), axis=2
    ).reshape(total)
    adapter_of = jnp.arange(ADAPT_COLS, dtype=jnp.int32) // RANK
    mask = (adapter_of[None, :] == chosen[:, None]).astype(f32)
    mask_t = (adapter_of[:, None] == chosen[None, :]).astype(f32)
    own_mask_t = part_rows(mask_t, wa, part_cols)
    cosine, sine = rotary_tables(offset)

    def gather_rows(value):
        full = jnp.zeros((WA, rows, width), bf16)
        for r, part in enumerate(gather_relative(value)):
            full = lax.dynamic_update_index_in_dim(full, part, wa ^ r, 0)
        return full.reshape(total, width)

    token_rows = gather_rows(tokens[0])
    downs = gather_relative(jnp.concatenate([qkv_down, in_down], axis=1))
    downs = jnp.concatenate(absolute(downs, wa), axis=0)
    qkv_down_all = downs[:, :ADAPT_COLS]
    in_down_all = downs[:, ADAPT_COLS:]
    grad = gather_rows(cotangent[0])

    qkv_split = qkv_weight.reshape(own_width, 3, WA, own_width)

    def qkv_columns(index):
        return lax.dynamic_index_in_dim(qkv_split, index, axis=2, keepdims=False).reshape(
            own_width, 3 * own_width
        )

    qkv_own = [qkv_columns(wa), swap(qkv_columns(mate), 1)]
    qkv_peer = [qkv_columns(peer), swap(qkv_columns(far), 1)]
    in_own = [columns(in_weight, wa, hidden_width), swap(columns(in_weight, mate, hidden_width), 1)]
    in_peer = [
        columns(in_weight, peer, hidden_width),
        swap(columns(in_weight, far, hidden_width), 1),
    ]

    def up_columns(index):
        qkv_part = lax.dynamic_index_in_dim(
            qkv_up.reshape(part_cols, 3, WA, own_width), index, axis=2, keepdims=False
        ).reshape(part_cols, 3 * own_width)
        return jnp.concatenate([qkv_part, columns(in_up, index, hidden_width)], axis=1)

    ups = [up_columns(wa), swap(up_columns(mate), 1), swap(up_columns(peer), 2), swap(up_columns(far), 3)]
    ups = jnp.concatenate(absolute(ups, wa), axis=0)
    qkv_up_own = ups[:, : 3 * own_width]
    in_up_own = ups[:, 3 * own_width :]

    values = token_rows.astype(f32)
    centered = values - jnp.mean(values, axis=1, keepdims=True)
    normal = centered * lax.rsqrt(jnp.mean(centered * centered, axis=1, keepdims=True) + epsilon)
    first_norm = (normal * ln1_gain + ln1_bias).astype(bf16)
    second_norm = (normal * ln2_gain + ln2_bias).astype(bf16)
    first_inner = (product(first_norm, qkv_down_all) * mask).astype(bf16)
    second_inner = (product(second_norm, in_down_all) * mask).astype(bf16)
    first_pair = [columns(first_norm, wa, own_width), columns(first_norm, mate, own_width)]
    second_pair = [columns(second_norm, wa, own_width), columns(second_norm, mate, own_width)]

    def both(left, right):
        return product(left[0], right[0]) + product(left[1], right[1])

    mixed = []
    for kind in (2, 1, 0):
        cut = slice(kind * own_width, (kind + 1) * own_width)
        sent = both(first_pair, [item[:, cut] for item in qkv_peer]).astype(bf16)
        arrived = swap(sent, 2)
        bias = lax.dynamic_slice_in_dim(
            qkv_bias, kind * width + wa * own_width, own_width, axis=0
        )
        mixed.append(
            both(first_pair, [item[:, cut] for item in qkv_own])
            + product(first_inner, qkv_up_own[:, cut])
            + bias
            + arrived.astype(f32)
        )
    value, key, query = mixed

    def to_pairs(item):
        item = item.reshape(PAIRS, rows, HEAD)
        if groups == 1:
            return lax.all_to_all(item, "ctx", 0, 0, tiled=True)
        names = [[g * PAIRS + j for j in range(PAIRS)] for g in range(groups)]
        return lax.all_to_all(item, "ctx", 0, 0, axis_index_groups=names, tiled=True)

    def split_heads(item):
        return jnp.transpose(item.reshape(WA, rows, 2, HEAD), (0, 2, 1, 3))

    def join_heads(item):
        return jnp.transpose(item.reshape(WA, 2, rows, HEAD), (0, 2, 1, 3)).reshape(
            total, own_width
        )

    query = to_pairs(rotate_heads(query, cosine, sine))
    key = to_pairs(rotate_heads(key, cosine, sine))
    value = to_pairs(split_heads(value.astype(bf16)))

    inner_grads_t = times_t(jnp.concatenate([dense_up, out_up], axis=0), grad)
    inner_grads_t = (inner_grads_t.reshape(2, part_cols, total) * own_mask_t).astype(bf16)
    inner_grads_t = jnp.concatenate(
        absolute(gather_relative(inner_grads_t), wa), axis=1
    )
    dense_inner_grad = inner_grads_t[0]
    out_inner_grad = inner_grads_t[1]
    attended_grad = times_t(grad, dense_weight) + lax.dot_general(
        dense_inner_grad, dense_down, (((0,), (1,)), ((), ())), preferred_element_type=f32
    )
    attended_grad = to_pairs(split_heads(attended_grad.astype(bf16)))

    pair_rows = PAIRS * rows
    group = ctx // PAIRS
    own_pack = (ctx % PAIRS) // 2
    own_starts = jnp.sum(
        jnp.where(jnp.arange(WA)[:, None] == own_pack, starts, 0), axis=0
    )
    all_places = places(0, groups * pair_rows)
    all_inside = own_starts[None, :] <= all_places[:, None]
    all_begins = jnp.max(jnp.where(all_inside, own_starts[None, :], 0), axis=1)
    k_tables = rotary_tables(all_places - all_begins)
    if groups == 1:
        q_place, q_begin, q_tables = all_places, all_begins, k_tables
    else:
        q_place = part_rows(all_places, group, pair_rows)
        q_begin = part_rows(all_begins, group, pair_rows)
        q_tables = [part_rows(item, group, pair_rows) for item in k_tables]
    query, key, value, attended_grad = [
        item.reshape(pair_rows, HEAD) for item in (query, key, value, attended_grad)
    ]
    sets = [[g * PAIRS + j for g in range(groups)] for j in range(PAIRS)]
    if groups > 1:
        key, value = [
            lax.all_gather(item, "ctx", axis=0, axis_index_groups=sets, tiled=True)
            for item in (key, value)
        ]
    attended, dq, dk, dv = attend(
        query,
        key,
        value,
        attended_grad,
        q_begin[:, None],
        q_place[:, None],
        all_places[None, :],
        q_tables,
        k_tables,
    )
    if groups > 1:
        dk, dv = [
            lax.psum_scatter(
                item, "ctx", scatter_dimension=0, axis_index_groups=sets, tiled=True
            )
            for item in (dk, dv)
        ]
    dv, dk, dq, attended = [join_heads(to_pairs(item)) for item in (dv, dk, dq, attended)]

    hidden_sent = both(second_pair, in_peer).astype(bf16)
    hidden_arrived = swap(hidden_sent, 2)
    hidden_pre = (
        both(second_pair, in_own)
        + product(second_inner, in_up_own)
        + lax.dynamic_slice_in_dim(in_bias, wa * hidden_width, hidden_width, axis=0)
        + hidden_arrived.astype(f32)
    )
    hidden, gelu_pull = jax.vjp(lambda v: jax.nn.gelu(v, approximate=False), hidden_pre)
    hidden = hidden.astype(bf16)
    hidden_grad = times_t(grad, out_weight) + lax.dot_general(
        out_inner_grad, out_down, (((0,), (1,)), ((), ())), preferred_element_type=f32
    )
    pre_grad = gelu_pull(hidden_grad)[0].astype(bf16)
    pre_peer = swap(pre_grad, 2)

    def scatter_inner(partial):
        own = [part_rows(partial, wa, part_cols), part_rows(partial, peer, part_cols)]
        sent = [part_rows(partial, mate, part_cols), part_rows(partial, far, part_cols)]
        arrived = swap(jnp.concatenate(sent, axis=0), 1)
        crossing = swap(own[1] + arrived[part_cols:], 2)
        return ((own[0] + arrived[:part_cols] + crossing) * own_mask_t).astype(bf16)

    out_inner_t = scatter_inner(
        lax.dot_general(out_down, hidden, (((0,), (1,)), ((), ())), preferred_element_type=f32)
    )
    dense_inner_t = scatter_inner(
        lax.dot_general(
            dense_down, attended, (((0,), (1,)), ((), ())), preferred_element_type=f32
        )
    )
    branches = (
        product(hidden, out_weight)
        + product(attended, dense_weight)
        + t_times(out_inner_t, out_up)
        + t_times(dense_inner_t, dense_up)
    ).reshape(WA, rows, width)

    def pack_of(value, index):
        return lax.dynamic_index_in_dim(value, index, axis=0, keepdims=False)

    arrived = swap(jnp.stack([pack_of(branches, mate), pack_of(branches, far)]).astype(bf16), 1)
    crossing = swap((pack_of(branches, peer) + arrived[1].astype(f32)).astype(bf16), 2)
    output = (
        pack_of(branches, wa)
        + arrived[0].astype(f32)
        + crossing.astype(f32)
        + dense_bias
        + out_bias
        + tokens[0].astype(f32)
    ).astype(bf16)[None]

    def sum_inner(partial):
        partial = partial + swap(partial, 1)
        partial = partial + swap(partial, 2)
        return (partial * mask_t).astype(bf16)

    mixed_grad = jnp.concatenate([dq, dk, dv], axis=1)
    mixed_peer = jnp.concatenate([swap(item, 2) for item in (dq, dk, dv)], axis=1)
    first_inner_grad = sum_inner(times_t(qkv_up_own, mixed_grad))
    second_inner_grad = sum_inner(times_t(in_up_own, pre_grad))

    def norm_grad(own, other, own_weight, other_weight):
        return times_t(own, own_weight) + times_t(other, other_weight)

    combined = []
    for row, index in ((0, wa), (1, mate)):
        gain1 = lax.dynamic_slice_in_dim(ln1_gain, index * own_width, own_width, axis=0)
        gain2 = lax.dynamic_slice_in_dim(ln2_gain, index * own_width, own_width, axis=0)
        combined.append(
            norm_grad(mixed_grad, mixed_peer, qkv_own[row], qkv_peer[row]) * gain1
            + norm_grad(pre_grad, pre_peer, in_own[row], in_peer[row]) * gain2
        )
    combined = [item.reshape(WA, rows, own_width) for item in combined]

    def both_columns(first, index):
        return jnp.concatenate(
            [pack_of(combined[first], index), pack_of(combined[1 - first], index)], axis=1
        )

    sent = jnp.stack([both_columns(1, mate), both_columns(1, far)]).astype(bf16)
    arrived = swap(sent, 1).astype(f32)
    near = both_columns(0, wa) + arrived[0]
    away = both_columns(0, peer) + arrived[1]
    away = swap(away.astype(bf16), 2).astype(f32)
    combined = jnp.concatenate(
        absolute(
            [near[:, :own_width], near[:, own_width:], away[:, :own_width], away[:, own_width:]],
            wa,
        ),
        axis=1,
    )
    combined = (
        combined
        + lax.dot_general(
            columns(first_inner_grad, wa, rows),
            qkv_down_all,
            (((0,), (1,)), ((), ())),
            preferred_element_type=f32,
        )
        * ln1_gain
        + lax.dot_general(
            columns(second_inner_grad, wa, rows),
            in_down_all,
            (((0,), (1,)), ((), ())),
            preferred_element_type=f32,
        )
        * ln2_gain
    )
    own_values = tokens[0].astype(f32)
    own_centered = own_values - jnp.mean(own_values, axis=1, keepdims=True)
    own_rstd = lax.rsqrt(jnp.mean(own_centered * own_centered, axis=1, keepdims=True) + epsilon)
    own_normal = own_centered * own_rstd
    tokens_grad = (
        cotangent[0].astype(f32)
        + own_rstd
        * (
            combined
            - jnp.mean(combined, axis=1, keepdims=True)
            - own_normal * jnp.mean(combined * own_normal, axis=1, keepdims=True)
        )
    )[None]

    def up_grad(inner, own, other):
        def block(index):
            part = columns(inner, index, part_cols)
            return [t_times(part, own).astype(bf16), t_times(part, other).astype(bf16)]

        mine = block(wa)
        arrived = swap(jnp.stack(block(mate)), 1)
        return [mine[0], arrived[0], mine[1], arrived[1]]

    out_down_grad = t_times(hidden, out_inner_grad.T).astype(bf16)
    out_up_grad = product(out_inner_t, grad).astype(bf16)
    in_down_grad = lax.dot_general(
        second_pair[0], second_inner_grad, (((0,), (1,)), ((), ())), preferred_element_type=f32
    ).astype(bf16)
    in_up_grad = jnp.concatenate(up_grad(second_inner, pre_grad, pre_peer), axis=1)
    out_down_grad, out_up_grad, in_down_grad, in_up_grad = lax.psum(
        (out_down_grad, out_up_grad, in_down_grad, in_up_grad), "ctx"
    )
    dense_down_grad = t_times(attended, dense_inner_grad.T).astype(bf16)
    dense_up_grad = product(dense_inner_t, grad).astype(bf16)
    qkv_down_grad = lax.dot_general(
        first_pair[0], first_inner_grad, (((0,), (1,)), ((), ())), preferred_element_type=f32
    ).astype(bf16)
    qkv_up_grad = jnp.concatenate(up_grad(first_inner, mixed_grad, mixed_peer), axis=1)
    dense_down_grad, dense_up_grad, qkv_down_grad, qkv_up_grad = lax.psum(
        (dense_down_grad, dense_up_grad, qkv_down_grad, qkv_up_grad), "ctx"
    )
    in_up_grad = jnp.concatenate(absolute(jnp.split(in_up_grad, WA, axis=1), wa), axis=1)
    qkv_parts = absolute(jnp.split(qkv_up_grad, WA, axis=1), wa)
    qkv_up_grad = jnp.stack(
        [item.reshape(part_cols, 3, own_width) for item in qkv_parts], axis=2
    ).reshape(part_cols, 3 * width)
    return (
        output,
        tokens_grad,
        qkv_down_grad.astype(f32),
        qkv_up_grad.astype(f32),
        dense_down_grad.astype(f32),
        dense_up_grad.astype(f32),
        in_down_grad.astype(f32),
        in_up_grad.astype(f32),
        out_down_grad.astype(f32),
        out_up_grad.astype(f32),
    )


def solution(mesh):
    rows = P("wa", "ctx", None)
    shard = P("wa", None)
    in_specs = (
        (rows, rows, P(), shard, shard)
        + (P(),) * 4
        + (shard, P()) * 4
        + (shard,) * 8
    )
    out_specs = (rows, rows) + (shard,) * 8
    return jax.shard_map(
        functools.partial(body, mesh.shape["ctx"]),
        mesh=mesh,
        in_specs=in_specs,
        out_specs=out_specs,
        check_vma=False,
    )
```

```python
import functools
import math

import jax
import jax.numpy as jnp
from jax import lax
from jax.experimental import pallas as pl
from jax.experimental.pallas import tpu as pltpu
from jax.sharding import PartitionSpec as P

HEADS = 8
HEAD = 256
ROT = 64
RANK = 16
BLOCK = 64
ADAPT_COLS = 128
WA = 4
PAIRS = 8
VMEM_BYTES = 58 * 1024 * 1024

epsilon = 1e-05
masked_score = -1e30
f32 = jnp.float32
bf16 = jnp.bfloat16


def product(left, right):
    return jnp.dot(left, right, preferred_element_type=f32)


def times_t(left, right):
    return lax.dot_general(left, right, (((1,), (1,)), ((), ())), preferred_element_type=f32)


def t_times(left, right):
    return lax.dot_general(left, right, (((0,), (0,)), ((), ())), preferred_element_type=f32)


def swap(value, bits):
    return lax.ppermute(value, "wa", [(i, i ^ bits) for i in range(WA)])


def after(value, *earlier):
    return lax.optimization_barrier((value, *earlier))[0]


def absolute(pieces, wa):
    low = wa % 2 == 1
    high = wa >= 2
    p = [
        jnp.where(low, pieces[1], pieces[0]),
        jnp.where(low, pieces[0], pieces[1]),
        jnp.where(low, pieces[3], pieces[2]),
        jnp.where(low, pieces[2], pieces[3]),
    ]
    return [
        jnp.where(high, p[2], p[0]),
        jnp.where(high, p[3], p[1]),
        jnp.where(high, p[0], p[2]),
        jnp.where(high, p[1], p[3]),
    ]


def rotary_tables(offset):
    half = ROT // 2
    lane = jnp.arange(128, dtype=jnp.int32)
    freq = 10000.0 ** (-2.0 * (lane % half).astype(f32) / ROT)
    freq = jnp.where(lane < ROT, freq, 0.0)
    angle = offset.astype(f32)[:, None] * freq[None, :]
    sign = jnp.where(lane < half, -1.0, 1.0)
    return jnp.cos(angle), jnp.sin(angle) * sign[None, :]


def turn_first(values, cosine, sine):
    lane = lax.broadcasted_iota(jnp.int32, values.shape, 1)
    partner = jnp.where(
        lane < ROT // 2, pltpu.roll(values, 128 - ROT // 2, 1), pltpu.roll(values, ROT // 2, 1)
    )
    return values * cosine + partner * sine


def call(kernel, index, inputs, outputs, grid=(1,), scratch=(), flops=0, name=None):
    def spec(shape, block, where):
        if where is None:
            zeros = (0,) * len(shape)
            return pl.BlockSpec(shape, lambda *_: zeros)
        return pl.BlockSpec(block, where)

    size = sum(a.size * a.dtype.itemsize if w is None else math.prod(i or 1 for i in b) * 2 * math.prod(grid)
               for a, b, w in inputs)
    return pl.pallas_call(
        kernel,
        grid_spec=pltpu.PrefetchScalarGridSpec(
            num_scalar_prefetch=1,
            grid=grid,
            in_specs=[spec(a.shape, b, w) for a, b, w in inputs],
            out_specs=[spec(s, b, w) for s, _, b, w in outputs],
            scratch_shapes=list(scratch),
        ),
        out_shape=[jax.ShapeDtypeStruct(s, d) for s, d, _, _ in outputs],
        compiler_params=pltpu.CompilerParams(vmem_limit_bytes=VMEM_BYTES),
        cost_estimate=pl.CostEstimate(flops=flops, bytes_accessed=size, transcendentals=0),
    )(index, *[a for a, _, _ in inputs])


def whole(array):
    return (array, None, None)


def copy_kernel(index_ref, *refs):
    count = len(refs) // 2
    for source, target in zip(refs[:count], refs[count:]):
        target[...] = source[...].reshape(target.shape)


def cut_columns(index, weight, size, kinds, cuts, parts=1):
    rows = weight.shape[0]
    part = size // parts
    inputs, outputs = [], []
    for r, halved in cuts:
        height = rows // 2 if halved else rows

        def where(slot, t, ref, r=r, halved=halved):
            kind = sum(kind * (slot == i) for i, kind in enumerate(kinds))
            return (ref[4] if halved else 0, (kind * WA + ref[r]) * parts + t)

        inputs.append((weight, (height, part), where))
        outputs.append(
            (
                (len(kinds), height, size),
                weight.dtype,
                (1, height, part),
                lambda slot, t, ref: (slot, 0, t),
            )
        )
    return call(copy_kernel, index, inputs, outputs, grid=(len(kinds), parts))


def strips(value):
    return [value[:, i : i + 128] for i in range(0, value.shape[1], 128)]


def store_strips(target, first, value):
    for item in strips(value):
        target[first : first + item.shape[0], :] = item
        first += item.shape[0]
    return first


def pack_kernel(index_ref, *refs):
    plain, last_ref = refs[:-6], refs[-6]
    (ups_mate, ups_peer, ups_far), (away_ref, near_ref) = refs[-5:-2], refs[-2:]
    first = 0
    for ref in plain:
        store_strips(away_ref, first, ref)
        first = store_strips(near_ref, first, ref)
    blank = ups_peer.shape[0] * ups_peer.shape[1] // 128
    store_strips(near_ref, first, ups_mate)
    store_strips(near_ref, first + blank, ups_mate)
    store_strips(away_ref, first, ups_peer)
    store_strips(away_ref, first + blank, ups_far)
    store_strips(near_ref, first + 2 * blank, last_ref)
    store_strips(away_ref, first + 2 * blank, last_ref)


def pack_small(index, plain, up, kinds, last):
    block = up.shape[1] // len(kinds) // WA
    items = [whole(item) for item in plain + [last]]
    size = sum(item.size for item in plain) // 128
    ups = up.shape[0] * block * len(kinds) // 128
    cut = jnp.concatenate if len(kinds) > 1 else (lambda v, axis: v[0])
    for r in (1, 2, 3):
        items.append(
            whole(
                cut(
                    [
                        lax.dynamic_slice_in_dim(up, (kind * WA + index[r]) * block, block, axis=1)
                        for kind in kinds
                    ],
                    axis=1,
                )
            )
        )
    shape = (size + 2 * ups + last.shape[0], 128)
    return call(pack_kernel, index, items, [(shape, bf16, None, None)] * 2)


def front_kernel(index_ref, *refs):
    token_ref, down_ref = refs[:2]
    packs = refs[2:5]
    mask_ref, g1, b1, g2, b2, first_ref, second_ref, inner_ref = refs[5:]
    rows, width = token_ref.shape
    wide = down_ref.shape[0]
    step = 32
    for r in range(WA):
        base = pl.multiple_of(index_ref[r] * rows, rows)
        for start in range(0, rows, step):
            if r == 0:
                values = token_ref[start : start + step, :]
            else:
                values = jnp.concatenate(
                    [
                        packs[r - 1][i * rows + start : i * rows + start + step, :]
                        for i in range(width // 128)
                    ],
                    axis=1,
                )
            values = values.astype(f32)
            centered = values - jnp.mean(values, axis=1, keepdims=True)
            spread = jnp.mean(centered * centered, axis=1, keepdims=True)
            normal = centered * lax.rsqrt(spread + epsilon)
            first_ref[pl.ds(base + start, step), :] = (normal * g1[...] + b1[...]).astype(bf16)
            second_ref[pl.ds(base + start, step), :] = (normal * g2[...] + b2[...]).astype(bf16)
    total = 0.0
    first = rows * width // 128
    for r in range(WA):
        columns = pl.ds(pl.multiple_of(index_ref[r] * wide, wide), wide)
        down = down_ref[...] if r == 0 else packs[r - 1][first : first + wide, :]
        total += product(first_ref[:, columns], down)
    inner_ref[...] = (total * mask_ref[...]).astype(bf16)


def pieces_of(index_ref, refs):
    wide = refs[0].shape[-2]
    half = wide // 2
    y = index_ref[4]
    firsts = [
        index_ref[0] * wide,
        index_ref[1] * wide,
        index_ref[2] * wide + y * half,
        index_ref[2] * wide + (1 - y) * half,
        index_ref[3] * wide + y * half,
        index_ref[3] * wide + (1 - y) * half,
    ]
    return [
        (pl.ds(pl.multiple_of(first, half), ref.shape[-2]), ref) for first, ref in zip(firsts, refs)
    ]


def read(ref):
    return ref[...].reshape(ref.shape[-2:])


def join_ups(index_ref, ups, joined):
    size = ADAPT_COLS // WA
    for r, ref in enumerate(ups):
        first = pl.multiple_of(index_ref[r] * size, size)
        if ref.shape[-1] == joined.shape[-1]:
            joined[pl.ds(first, size), :] = read(ref)
        else:
            for i in range(joined.shape[-1] // 128):
                joined[pl.ds(first, size), i * 128 : (i + 1) * 128] = ref[
                    i * size : (i + 1) * size, :
                ]


def qkv_kernel(turned, index_ref, hidden_ref, *refs):
    weights, ups = refs[:6], refs[6:10]
    inner_ref, bias_ref, cos_ref, sin_ref, out_ref, joined = refs[10:]
    join_ups(index_ref, ups, joined)
    total = product(inner_ref[...], joined[...]) + bias_ref[...]
    for columns, ref in pieces_of(index_ref, weights):
        total += product(hidden_ref[:, columns], read(ref))
    shape = out_ref.shape
    if turned:
        first = turn_first(total[:, :128], cos_ref[...], sin_ref[...])
        out_ref[..., :128] = first.astype(bf16).reshape(shape[:-1] + (128,))
        out_ref[..., 128:] = total[:, 128:].astype(bf16).reshape(shape[:-1] + (HEAD - 128,))
    else:
        out_ref[...] = total.astype(bf16).reshape(shape)


def grad_kernel(index_ref, *refs):
    parts = refs[:WA]
    mask_ref, weight_ref, down_ref = refs[WA : WA + 3]
    grad_ref, dense_ref, out_ref, heads_ref, ups_ref, dense_joined, out_joined = refs[WA + 3 :]
    size = ADAPT_COLS // WA
    rows = parts[0].shape[0] - 2 * size
    for r in range(WA):
        first = pl.ds(pl.multiple_of(index_ref[r] * size, size), size)
        dense_joined[first, :] = parts[r][rows : rows + size, :]
        out_joined[first, :] = parts[r][rows + size :, :]
        grad_ref[pl.ds(pl.multiple_of(index_ref[r] * rows, rows), rows), :] = parts[r][:rows, :]
    ups_ref[0] = dense_joined[...]
    ups_ref[1] = out_joined[...]
    grad = grad_ref[...]
    dense = (times_t(grad, dense_joined[...]) * mask_ref[...]).astype(bf16)
    dense_ref[...] = dense
    out_ref[...] = (times_t(grad, out_joined[...]) * mask_ref[...]).astype(bf16)
    for head in range(2):
        span = slice(head * HEAD, (head + 1) * HEAD)
        total = times_t(grad, weight_ref[span, :]) + times_t(dense, down_ref[span, :])
        heads_ref[:, head] = total.astype(bf16).reshape(WA, rows, HEAD)


def gelu_parts(values):
    bell = jnp.exp(-0.5 * values * values)
    t = 1.0 / (1.0 + (0.3275911 * math.sqrt(0.5)) * jnp.abs(values))
    series = 1.061405429 * 0.5
    for factor in (-1.453152027, 1.421413741, -0.284496736, 0.254829592):
        series = series * t + 0.5 * factor
    tail = series * t * bell
    below = jnp.where(values > 0, 1.0 - tail, tail)
    return values * below, below + values * bell * (1.0 / math.sqrt(2.0 * math.pi))


def feed_kernel(index_ref, hidden_ref, grad_ref, *refs):
    weights, ups, downs = refs[:6], refs[6:10], refs[10:14]
    mask_ref, bias_ref, gain_ref, out_w_ref, out_down_ref, out_inner_grad_ref = refs[14:20]
    (
        out_ref,
        norm_grad_ref,
        out_inner_ref,
        inner_grad_ref,
        out_down_grad_ref,
        in_up_grad_ref,
        inner_ref,
        joined,
    ) = refs[20:]
    step = pl.program_id(0)

    @pl.when(step == 0)
    def _():
        wide = downs[0].shape[0]
        total = 0.0
        for r in range(WA):
            columns = pl.ds(pl.multiple_of(index_ref[r] * wide, wide), wide)
            total += product(hidden_ref[:, columns], downs[r][...])
        inner_ref[...] = (total * mask_ref[...]).astype(bf16)
        out_ref[...] = jnp.zeros_like(out_ref)
        norm_grad_ref[...] = jnp.zeros_like(norm_grad_ref)
        out_inner_ref[...] = jnp.zeros_like(out_inner_ref)
        inner_grad_ref[...] = jnp.zeros_like(inner_grad_ref)

    join_ups(index_ref, ups, joined)
    pre = product(inner_ref[...], joined[...]) + bias_ref[...]
    for columns, ref in pieces_of(index_ref, weights):
        pre += product(hidden_ref[:, columns], read(ref))
    units, slope = gelu_parts(pre)
    units = units.astype(bf16)
    pre_grad = times_t(grad_ref[...], out_w_ref[...]) + times_t(
        out_inner_grad_ref[...], out_down_ref[...]
    )
    pre_grad = (pre_grad * slope).astype(bf16)
    out_ref[...] += product(units, out_w_ref[...])
    for columns, ref in pieces_of(index_ref, weights):
        norm_grad_ref[:, columns] += times_t(pre_grad, read(ref))
    out_inner_ref[...] += product(units, out_down_ref[...])
    inner_grad_ref[...] += times_t(pre_grad, joined[...])
    out_down_grad_ref[...] = t_times(units, out_inner_grad_ref[...]).astype(bf16)
    in_up_grad_ref[...] = t_times(inner_ref[...], pre_grad).astype(bf16)

    @pl.when(step == pl.num_programs(0) - 1)
    def _():
        norm_grad_ref[...] = norm_grad_ref[...] * gain_ref[...]


def scatter_rows(index_ref, total_ref, keep_ref, send_ref):
    rows = keep_ref.shape[1]
    for r, (ref, slot) in enumerate(((keep_ref, 0), (send_ref, 0), (keep_ref, 1), (send_ref, 1))):
        part = total_ref[pl.ds(pl.multiple_of(index_ref[r] * rows, rows), rows), :]
        ref[slot] = part.astype(ref.dtype)


def head_rows(ref, head):
    return ref[:, head, 0].reshape(-1, HEAD)


def dense_kernel(
    index_ref,
    heads_ref,
    sum_ref,
    weight_ref,
    down_ref,
    inner_grad_ref,
    keep_ref,
    send_ref,
    inner_ref,
    down_grad_ref,
    total,
):
    result = sum_ref[...]
    inner = 0.0
    for head in range(2):
        span = slice(head * HEAD, (head + 1) * HEAD)
        heads = head_rows(heads_ref, head)
        result += product(heads, weight_ref[span, :])
        inner += product(heads, down_ref[span, :])
        down_grad_ref[span, :] = t_times(heads, inner_grad_ref[...]).astype(bf16)
    inner_ref[...] = inner
    total[...] = result
    scatter_rows(index_ref, total, keep_ref, send_ref)


def mixed_rows(query_grad_ref, key_grad_ref, kind, head):
    if kind == 0:
        return query_grad_ref[:, head, 1].reshape(-1, HEAD)
    return key_grad_ref[:, head, kind + 1].reshape(-1, HEAD)


def mix_kernel(index_ref, *refs):
    grads, ups = refs[:2], refs[2 : 2 + 3 * WA]
    inner_ref, inner_grad_ref, up_grad_ref, joined = refs[2 + 3 * WA :]
    width = 2 * HEAD
    for kind in range(3):
        for r in range(WA):
            size = ADAPT_COLS // WA
            first = pl.multiple_of(index_ref[r] * size, size)
            ref = ups[kind * WA + r]
            if r == 0:
                joined[kind, pl.ds(first, size), :] = ref[...]
            else:
                for i in range(width // 128):
                    joined[kind, pl.ds(first, size), i * 128 : (i + 1) * 128] = ref[
                        i * size : (i + 1) * size, :
                    ]
    total = 0.0
    for kind in range(3):
        for head in range(2):
            span = slice(head * HEAD, (head + 1) * HEAD)
            rows = mixed_rows(*grads, kind, head)
            total += times_t(rows, joined[kind, :, span])
            out = slice(kind * width + head * HEAD, kind * width + (head + 1) * HEAD)
            up_grad_ref[:, out] = t_times(inner_ref[...], rows).astype(bf16)
    inner_grad_ref[...] = total


def norm_grad_kernel(index_ref, *refs):
    grads, weights = refs[:2], refs[2:20]
    gain_ref, sum_ref, keep_ref, send_ref, total = refs[20:]
    sets = [pieces_of(index_ref, weights[6 * kind : 6 * kind + 6]) for kind in range(3)]
    rows = [[mixed_rows(*grads, kind, head) for head in range(2)] for kind in range(3)]
    for piece in range(6):
        columns = sets[0][piece][0]
        part = 0.0
        for kind in range(3):
            weight = read(sets[kind][piece][1])
            for head in range(2):
                part += times_t(rows[kind][head], weight[:, head * HEAD : (head + 1) * HEAD])
        total[:, columns] = part * gain_ref[:, columns] + sum_ref[:, columns]
    scatter_rows(index_ref, total, keep_ref, send_ref)


def finish_kernel(index_ref, *refs):
    keep_ref, near_ref, away_ref, first_ref, second_ref = refs[:5]
    first_downs, second_downs = refs[5:9], refs[9:13]
    g1, g2, token_ref, grad_ref, out_ref, total = refs[13:]
    total[...] = keep_ref[0] + near_ref[0].astype(f32) + away_ref[...].astype(f32)
    wide = first_downs[0].shape[0]
    for r in range(WA):
        columns = pl.ds(pl.multiple_of(index_ref[r] * wide, wide), wide)
        total[:, columns] += (
            times_t(first_ref[...], first_downs[r][...]) * g1[:, columns]
            + times_t(second_ref[...], second_downs[r][...]) * g2[:, columns]
        )
    step = 32
    for start in range(0, total.shape[0], step):
        span = slice(start, start + step)
        values = token_ref[span, :].astype(f32)
        centered = values - jnp.mean(values, axis=1, keepdims=True)
        rstd = lax.rsqrt(jnp.mean(centered * centered, axis=1, keepdims=True) + epsilon)
        normal = centered * rstd
        part = total[span, :]
        part = (
            part
            - jnp.mean(part, axis=1, keepdims=True)
            - normal * jnp.mean(part * normal, axis=1, keepdims=True)
        )
        out_ref[span, :] = grad_ref[span, :].astype(f32) + rstd * part


def attention_kernel(
    joint,
    query_ref,
    key_ref,
    value_ref,
    grad_ref,
    begin_ref,
    place_ref,
    key_place_ref,
    q_cos_ref,
    q_sin_ref,
    k_cos_ref,
    k_sin_ref,
    rows_ref,
    *refs,
):
    keys_ref, dk_sum, dv_sum = (rows_ref, *refs) if joint else refs
    step = pl.program_id(0)
    scale = 1.0 / math.sqrt(HEAD)

    @pl.when(step == 0)
    def _():
        dk_sum[...] = jnp.zeros_like(dk_sum)
        dv_sum[...] = jnp.zeros_like(dv_sum)

    query = query_ref[...]
    key = key_ref[...]
    value = value_ref[...]
    grad = grad_ref[...]
    key_place = key_place_ref[...]
    allowed = (key_place >= begin_ref[...]) & (key_place <= place_ref[...])
    scores = jnp.where(allowed, times_t(query, key) * scale, masked_score)
    top = jnp.max(scores, axis=1, keepdims=True)
    weights = jnp.exp(scores - top)
    prob = weights * (1.0 / jnp.sum(weights, axis=1, keepdims=True))
    prob_low = prob.astype(bf16)
    part, block = query.shape[0], rows_ref.shape[2]
    shape = (part // block, block)
    own = pl.ds(step * shape[0], shape[0]) if joint else slice(None)
    rows_ref[own, 0] = product(prob_low, value).astype(bf16).reshape(shape + (HEAD,))
    prob_grad = times_t(grad, value)
    delta = jnp.sum(prob * prob_grad, axis=1, keepdims=True)
    score_grad = (prob * (prob_grad - delta)).astype(bf16)
    dq = product(score_grad, key) * scale
    first = turn_first(dq[:, :128], q_cos_ref[...], -q_sin_ref[...])
    rows_ref[own, 1, :, :128] = first.astype(bf16).reshape(shape + (128,))
    rows_ref[own, 1, :, 128:] = dq[:, 128:].astype(bf16).reshape(shape + (HEAD - 128,))
    dk_sum[...] += t_times(score_grad, query)
    dv_sum[...] += t_times(prob_low, grad)

    @pl.when(step == pl.num_programs(0) - 1)
    def _():
        base = 2 if joint else 0
        shape = keys_ref.shape[:1] + keys_ref.shape[2:3]
        dk = dk_sum[...] * scale
        first = turn_first(dk[:, :128], k_cos_ref[...], -k_sin_ref[...])
        keys_ref[:, base, :, :128] = first.astype(bf16).reshape(shape + (128,))
        keys_ref[:, base, :, 128:] = dk[:, 128:].astype(bf16).reshape(shape + (HEAD - 128,))
        keys_ref[:, base + 1] = dv_sum[...].astype(bf16).reshape(shape + (HEAD,))


def attend(query, key, value, grad, begin, place, key_place, q_tables, k_tables, block):
    rows = query.shape[0]
    keys = key.shape[0]
    part = min(256, rows)
    joint = rows == keys
    by_rows = lambda i: (i, 0)
    all_rows = lambda i: (0, 0)
    fixed = lambda i: (0, 0, 0, 0)
    if joint:
        shapes = [(keys // block, 4, block, HEAD)]
        out_specs = [pl.BlockSpec(shapes[0], fixed)]
    else:
        shapes = [(rows // block, 2, block, HEAD), (keys // block, 2, block, HEAD)]
        out_specs = [
            pl.BlockSpec((part // block, 2, block, HEAD), lambda i: (i, 0, 0, 0)),
            pl.BlockSpec(shapes[1], fixed),
        ]
    return pl.pallas_call(
        functools.partial(attention_kernel, joint),
        grid=(rows // part,),
        in_specs=[
            pl.BlockSpec((part, HEAD), by_rows),
            pl.BlockSpec((keys, HEAD), all_rows),
            pl.BlockSpec((keys, HEAD), all_rows),
            pl.BlockSpec((part, HEAD), by_rows),
            pl.BlockSpec((part, 1), by_rows),
            pl.BlockSpec((part, 1), by_rows),
            pl.BlockSpec((1, keys), all_rows),
            pl.BlockSpec((part, 128), by_rows),
            pl.BlockSpec((part, 128), by_rows),
            pl.BlockSpec((keys, 128), all_rows),
            pl.BlockSpec((keys, 128), all_rows),
        ],
        out_specs=out_specs,
        out_shape=[jax.ShapeDtypeStruct(shape, bf16) for shape in shapes],
        scratch_shapes=[pltpu.VMEM((keys, HEAD), f32), pltpu.VMEM((keys, HEAD), f32)],
        compiler_params=pltpu.CompilerParams(vmem_limit_bytes=VMEM_BYTES),
        cost_estimate=pl.CostEstimate(
            flops=14 * rows * keys * HEAD,
            bytes_accessed=16 * keys * HEAD,
            transcendentals=rows * keys,
        ),
    )(query, key, value, grad, begin, place, key_place, *q_tables, *k_tables)


def body(
    contexts,
    tokens,
    cotangent,
    deal,
    doc_lengths,
    doc_adapter,
    ln1_gain,
    ln1_bias,
    ln2_gain,
    ln2_bias,
    qkv_weight,
    qkv_bias,
    dense_weight,
    dense_bias,
    in_weight,
    in_bias,
    out_weight,
    out_bias,
    qkv_down,
    qkv_up,
    dense_down,
    dense_up,
    in_down,
    in_up,
    out_down,
    out_up,
):
    rows = tokens.shape[1]
    width = tokens.shape[2]
    wa = lax.axis_index("wa")
    ctx = lax.axis_index("ctx")
    total = WA * rows
    own_width = width // WA
    hidden_width = in_weight.shape[1] // WA
    part_cols = ADAPT_COLS // WA
    groups = contexts // PAIRS
    half = own_width // 2
    relative = [wa, wa ^ 1, wa ^ 2, wa ^ 3]
    index = jnp.stack(relative + [ctx % 2]).astype(jnp.int32)

    def columns(value, which, size):
        return lax.dynamic_slice_in_dim(value, which * size, size, axis=1)

    def part_rows(value, which, size):
        return lax.dynamic_slice_in_dim(value, which * size, size, axis=0)

    def swap_y(value):
        return lax.ppermute(value, "ctx", [(i, i ^ 1) for i in range(contexts)])

    def gather(value, peer=None):
        peer = swap(value, 2) if peer is None else peer
        return [value, swap(value, 1), peer, swap(peer, 1)]

    value_cuts = cut_columns(index, qkv_weight, own_width, [2], [(2, True), (3, True)])
    limit = 64
    numbers = jnp.concatenate(
        [doc_lengths // limit, doc_lengths % limit, doc_adapter], axis=1
    ).astype(bf16)
    numbers = jnp.pad(numbers, ((0, 15), (0, 128 - numbers.shape[1])))
    first_pack = pack_small(index, [tokens[0], qkv_down], qkv_up, [0, 1, 2], numbers)

    def cross(value, *earlier):
        peer = swap(after(value[0], *earlier), 2)
        far = swap(after(value[1], *earlier), 3)
        return [peer, swap_y(peer), far, swap_y(far)]

    def hand_on(away, near, *earlier):
        peer = swap(after(away, *earlier), 2)
        return [swap(near, 1), peer, swap(peer, 1)]

    first_packs = hand_on(*first_pack)
    value_halves = cross(value_cuts)
    mate_cuts = cut_columns(index, qkv_weight, own_width, [0, 1, 2], [(1, False)])[0]
    key_cuts = cut_columns(index, qkv_weight, own_width, [1], [(2, True), (3, True)])
    query_cuts = cut_columns(index, qkv_weight, own_width, [0], [(2, True), (3, True)])
    in_cuts = cut_columns(
        index, in_weight, hidden_width, [0], [(2, True), (3, True), (1, False)], 4
    )
    feed_pack = pack_small(index, [in_down], in_up, [0], numbers)
    value_there = (value_halves[0], value_halves[2])
    mate_weights = swap(mate_cuts, 1)
    grad_pack = jnp.concatenate([cotangent[0], dense_up, out_up], axis=0)
    grad_packs = hand_on(grad_pack, grad_pack, *value_there)
    key_halves = cross(key_cuts, *value_there)
    key_there = (key_halves[0], key_halves[2])
    query_halves = cross(query_cuts, grad_packs[1])
    query_there = (query_halves[0], query_halves[2])
    in_mate = swap(after(in_cuts[2], mate_weights), 1)
    in_peer = swap(after(in_cuts[0], *key_there), 2)
    in_far = swap(after(in_cuts[1], *query_there), 3)
    in_halves = [in_peer, swap_y(in_peer), in_far, swap_y(in_far)]
    feed_packs = hand_on(*feed_pack, in_peer)

    docs_per_pack = doc_lengths.shape[1]
    tables = [numbers] + [item[-16:] for item in first_packs]
    tables = jnp.stack(absolute([item[0] for item in tables], wa)).astype(jnp.int32)
    lengths = tables[:, :docs_per_pack] * limit + tables[:, docs_per_pack : 2 * docs_per_pack]
    adapters = tables[:, 2 * docs_per_pack : 3 * docs_per_pack]
    starts = jnp.cumsum(lengths, axis=1) - lengths

    def places(first, size):
        slots = first + jnp.arange(size, dtype=jnp.int32)
        blocks = slots // BLOCK
        table = jnp.arange(deal.shape[0], dtype=jnp.int32)
        block = jnp.sum(jnp.where(table[None, :] == blocks[:, None], deal[None, :], 0), axis=1)
        return block * BLOCK + slots % BLOCK

    place = places(ctx * rows, rows)
    inside = starts[:, None, :] <= place[None, :, None]
    docs = jnp.sum(inside.astype(jnp.int32), axis=2) - 1
    begin = jnp.max(jnp.where(inside, starts[:, None, :], 0), axis=2)
    offset = (place[None, :] - begin).reshape(total)
    doc_table = jnp.arange(docs_per_pack, dtype=jnp.int32)
    chosen = jnp.sum(
        jnp.where(docs[:, :, None] == doc_table, adapters[:, None, :], 0), axis=2
    ).reshape(total)
    adapter_of = jnp.arange(ADAPT_COLS, dtype=jnp.int32) // RANK
    mask = (adapter_of[None, :] == chosen[:, None]).astype(f32)
    cosine, sine = rotary_tables(offset)

    gains = [item[None, :] for item in (ln1_gain, ln1_bias, ln2_gain, ln2_bias)]
    first_norm, second_norm, first_inner = call(
        front_kernel,
        index,
        [whole(after(tokens[0], *value_there, *key_cuts, *query_cuts, *in_cuts, *feed_pack))]
        + [whole(item) for item in [qkv_down] + first_packs + [mask] + gains],
        [
            ((total, width), bf16, None, None),
            ((total, width), bf16, None, None),
            ((total, ADAPT_COLS), bf16, None, None),
        ],
        flops=2 * total * width * ADAPT_COLS,
    )

    strip = strip_rows = part_cols * HEAD // 128
    ups_row = (tokens.size + qkv_down.size) // 128
    ups_size = 3 * own_width * part_cols // 128

    def project(kind, halves, turned):
        own_block = lambda head, ref: (0, (kind * WA + ref[0]) * 2 + head)
        items = [whole(first_norm), (qkv_weight, (own_width, HEAD), own_block)]
        items.append((mate_weights, (1, own_width, HEAD), lambda head, ref: (kind, 0, head)))
        items += [
            (item, (1, own_width // 2, HEAD), lambda head, ref: (0, 0, head)) for item in halves
        ]
        items.append((qkv_up, (part_cols, HEAD), own_block))
        for r, item in zip((1, 2, 3), first_packs):
            row = (ups_row + (r == 3) * ups_size) // strip + kind * 2
            items.append((item, (strip, 128), lambda head, ref, row=row: (row + head, 0)))
        items += [
            whole(first_inner),
            (qkv_bias[None, :], (1, HEAD), own_block),
            whole(cosine),
            whole(sine),
        ]
        out = call(
            functools.partial(qkv_kernel, turned),
            index,
            items,
            [
                (
                    (WA, 2, rows, HEAD),
                    bf16,
                    (WA, 1, rows, HEAD),
                    lambda head, ref: (0, head, 0, 0),
                )
            ],
            grid=(2,),
            scratch=[pltpu.VMEM((ADAPT_COLS, HEAD), bf16)],
            flops=2 * total * width * own_width,
        )[0]
        return out.reshape(PAIRS, rows, HEAD)

    def to_pairs(item):
        if groups == 1:
            return lax.all_to_all(item, "ctx", 0, 0, tiled=True)
        names = [[g * PAIRS + j for j in range(PAIRS)] for g in range(groups)]
        return lax.all_to_all(item, "ctx", 0, 0, axis_index_groups=names, tiled=True)

    value_halves[1] = after(value_halves[1], *grad_packs)
    value = to_pairs(project(2, value_halves, False))

    grad_own = after(grad_pack, *key_there, value_halves[1])
    grad, dense_inner_grad, out_inner_grad, attended_grad, all_ups = call(
        grad_kernel,
        index,
        [
            whole(item)
            for item in [grad_own] + grad_packs + [mask, dense_weight, dense_down]
        ],
        [
            ((total, width), bf16, None, None),
            ((total, ADAPT_COLS), bf16, None, None),
            ((total, ADAPT_COLS), bf16, None, None),
            ((WA, 2, rows, HEAD), bf16, None, None),
            ((2, ADAPT_COLS, width), bf16, None, None),
        ],
        scratch=[pltpu.VMEM((ADAPT_COLS, width), bf16), pltpu.VMEM((ADAPT_COLS, width), bf16)],
        flops=2 * total * width * (own_width + 2 * ADAPT_COLS),
    )
    attended_grad = to_pairs(after(attended_grad, value).reshape(PAIRS, rows, HEAD))
    key_halves[1] = after(key_halves[1], *query_there)
    key = to_pairs(after(project(1, key_halves, True), attended_grad))
    query_halves[1] = after(query_halves[1], in_peer)
    query = to_pairs(after(project(0, query_halves, True), key))

    pair_rows = PAIRS * rows
    group = ctx // PAIRS
    own_pack = (ctx % PAIRS) // 2
    own_starts = jnp.sum(
        jnp.where(jnp.arange(WA)[:, None] == own_pack, starts, 0), axis=0
    )
    all_places = places(0, groups * pair_rows)
    all_inside = own_starts[None, :] <= all_places[:, None]
    all_begins = jnp.max(jnp.where(all_inside, own_starts[None, :], 0), axis=1)
    k_tables = rotary_tables(all_places - all_begins)
    if groups == 1:
        q_place, q_begin, q_tables = all_places, all_begins, k_tables
    else:
        q_place = part_rows(all_places, group, pair_rows)
        q_begin = part_rows(all_begins, group, pair_rows)
        q_tables = [part_rows(item, group, pair_rows) for item in k_tables]
    query, key, value, attended_grad = [
        item.reshape(pair_rows, HEAD) for item in (query, key, value, attended_grad)
    ]
    sets = [[g * PAIRS + j for g in range(groups)] for j in range(PAIRS)]
    if groups > 1:
        key, value = [
            lax.all_gather(item, "ctx", axis=0, axis_index_groups=sets, tiled=True)
            for item in (key, value)
        ]
    both = attend(
        after(query, in_far, in_halves[1], feed_packs[2]),
        key,
        value,
        attended_grad,
        q_begin[:, None],
        q_place[:, None],
        all_places[None, :],
        q_tables,
        k_tables,
        rows,
    )
    if groups > 1:
        dkv = lax.psum_scatter(
            both[1], "ctx", scatter_dimension=0, axis_index_groups=sets, tiled=True
        )
        both = [jnp.concatenate([both[0], dkv], axis=1)]
    both = to_pairs(after(both[0], in_halves[3])).reshape(WA, 2, 4, rows, HEAD)
    odq, dkv = both, both

    tile = min(512, hidden_width)
    tiles = hidden_width // tile
    own_tile = lambda t, ref: (0, ref[0] * tiles + t)
    items = [whole(second_norm), whole(grad), (in_weight, (own_width, tile), own_tile)]
    items += [
        (item, (1, item.shape[1], tile), lambda t, ref: (0, 0, t)) for item in [in_mate] + in_halves
    ]
    items += [(in_up, (part_cols, tile), own_tile)]
    strip = part_cols * tile // 128
    for r, item in zip((1, 2, 3), feed_packs):
        row = (own_width + (r == 3) * part_cols * hidden_width // 128) // strip
        items.append((item, (strip, 128), lambda t, ref, row=row: (row + t, 0)))
    in_downs = [whole(in_down)] + [
        (item, (own_width, ADAPT_COLS), lambda *_: (0, 0)) for item in feed_packs
    ]
    items += in_downs + [whole(mask)]
    items += [
        (in_bias[None, :], (1, tile), own_tile),
        whole(gains[2]),
        (out_weight, (tile, width), lambda t, ref: (t, 0)),
        (out_down, (tile, ADAPT_COLS), lambda t, ref: (t, 0)),
        whole(out_inner_grad),
    ]
    (
        branch_sum,
        norm_grad,
        out_inner,
        second_inner_grad,
        out_down_grad,
        in_up_grad,
        second_inner,
    ) = call(
        feed_kernel,
        index,
        items,
        [
            ((total, width), f32, None, None),
            ((total, width), f32, None, None),
            ((total, ADAPT_COLS), f32, None, None),
            ((total, ADAPT_COLS), f32, None, None),
            ((hidden_width, ADAPT_COLS), bf16, (tile, ADAPT_COLS), lambda t, ref: (t, 0)),
            ((ADAPT_COLS, hidden_width), bf16, (ADAPT_COLS, tile), lambda t, ref: (0, t)),
            ((total, ADAPT_COLS), bf16, None, None),
        ],
        grid=(tiles,),
        scratch=[pltpu.VMEM((ADAPT_COLS, tile), bf16)],
        flops=8 * total * width * hidden_width,
    )

    def sum_inner(partial):
        partial = (partial + swap(partial, 1)).astype(bf16)
        partial = partial.astype(f32) + swap(partial, 2).astype(f32)
        return (partial * mask).astype(bf16)

    def spread_rows(value):
        return [part_rows(value, wa, part_cols)] + [
            swap(part_rows(value, wa ^ r, part_cols), r) for r in (1, 2, 3)
        ]

    def own_columns(left, right):
        return t_times(columns(left, wa, left.shape[1] // WA), right).astype(bf16)

    out_inner = sum_inner(out_inner)
    second_inner_grad = sum_inner(second_inner_grad)
    feed_grads = lax.psum([out_down_grad, in_up_grad], "ctx")

    dense_items = [odq, branch_sum, dense_weight, dense_down, dense_inner_grad]
    reduced = [
        ((2, rows, width), f32, None, None),
        ((2, rows, width), bf16, None, None),
    ]
    keep, send, dense_inner, dense_down_grad = call(
        dense_kernel,
        index,
        [whole(item) for item in dense_items],
        reduced
        + [
            ((total, ADAPT_COLS), f32, None, None),
            ((own_width, ADAPT_COLS), bf16, None, None),
        ],
        scratch=[pltpu.VMEM((total, width), f32)],
        flops=2 * total * width * own_width,
    )
    dense_inner = sum_inner(dense_inner)
    near = swap(send, 1)
    away = swap((keep[1] + near[1].astype(f32)).astype(bf16), 2)
    output = (
        keep[0]
        + near[0].astype(f32)
        + away.astype(f32)
        + product(part_rows(dense_inner, wa, rows), all_ups[0])
        + product(part_rows(out_inner, wa, rows), all_ups[1])
        + dense_bias
        + out_bias
        + tokens[0].astype(f32)
    ).astype(bf16)[None]

    mixed_grads = [odq, dkv]
    up_items = []
    for kind in range(3):
        up_items.append(
            (qkv_up, (part_cols, own_width), lambda _, ref, kind=kind: (0, kind * WA + ref[0]))
        )
        for r, item in zip((1, 2, 3), first_packs):
            row = (ups_row + (r == 3) * ups_size) // (2 * strip_rows) + kind
            up_items.append(
                (item, (2 * strip_rows, 128), lambda _, ref, row=row: (row, 0))
            )
    first_inner_grad, qkv_up_grad = call(
        mix_kernel,
        index,
        [whole(item) for item in mixed_grads] + up_items + [whole(first_inner)],
        [
            ((total, ADAPT_COLS), f32, None, None),
            ((ADAPT_COLS, 3 * own_width), bf16, None, None),
        ],
        scratch=[pltpu.VMEM((3, ADAPT_COLS, own_width), bf16)],
        flops=4 * total * ADAPT_COLS * 3 * own_width,
    )
    first_inner_grad = sum_inner(first_inner_grad)
    weight_items = []
    for kind, halves in ((0, query_halves), (1, key_halves), (2, value_halves)):
        weight_items.append(
            (
                qkv_weight,
                (own_width, own_width),
                lambda _, ref, kind=kind: (0, kind * WA + ref[0]),
            )
        )
        weight_items.append(
            (mate_weights, (1, own_width, own_width), lambda _, ref, kind=kind: (kind, 0, 0))
        )
        weight_items += [whole(item) for item in halves]
    keep, send = call(
        norm_grad_kernel,
        index,
        [whole(item) for item in mixed_grads]
        + weight_items
        + [whole(gains[0]), whole(norm_grad)],
        reduced,
        scratch=[pltpu.VMEM((total, width), f32)],
        flops=2 * total * width * 3 * own_width,
    )
    near = swap(send, 1)
    combined = (keep[1] + near[1].astype(f32)).astype(bf16)
    away = swap(combined, 2)
    down_at = rows * width // 128 // own_width
    down_block = lambda *_: (down_at, 0)
    tokens_grad = call(
        finish_kernel,
        index,
        [
            whole(item)
            for item in [
                keep,
                near,
                away,
                part_rows(first_inner_grad, wa, rows),
                part_rows(second_inner_grad, wa, rows),
            ]
        ]
        + [whole(qkv_down)]
        + [(item, (own_width, ADAPT_COLS), down_block) for item in first_packs]
        + in_downs
        + [whole(item) for item in [gains[0], gains[2], tokens[0], cotangent[0]]],
        [((rows, width), f32, None, None)],
        scratch=[pltpu.VMEM((rows, width), f32)],
    )[0][None]

    attention_grads = [
        dense_down_grad,
        own_columns(dense_inner, grad),
        own_columns(first_norm, first_inner_grad),
        own_columns(out_inner, grad),
        own_columns(second_norm, second_inner_grad),
    ] + spread_rows(qkv_up_grad)
    feed_grads = [after(item, *attention_grads, combined, output) for item in feed_grads]
    out_down_grad, in_up_grad = feed_grads
    in_up_parts = spread_rows(in_up_grad)
    attention_grads = [after(item, *feed_grads) for item in attention_grads]
    attention_grads = lax.psum(attention_grads, "ctx")
    out_down_grad = out_down_grad.astype(f32)
    dense_down_grad, dense_up_grad, qkv_down_grad, out_up_grad, in_down_grad = [
        item.astype(f32) for item in attention_grads[:5]
    ]
    in_up_grad = jnp.concatenate(absolute(in_up_parts, wa), axis=1).astype(f32)
    qkv_parts = absolute(attention_grads[5:], wa)
    qkv_up_grad = jnp.concatenate(
        [
            part[:, kind * own_width : (kind + 1) * own_width]
            for kind in range(3)
            for part in qkv_parts
        ],
        axis=1,
    ).astype(f32)
    return (
        output,
        tokens_grad,
        qkv_down_grad,
        qkv_up_grad,
        dense_down_grad,
        dense_up_grad,
        in_down_grad,
        in_up_grad,
        out_down_grad,
        out_up_grad,
    )


def solution(mesh):
    rows = P("wa", "ctx", None)
    shard = P("wa", None)
    in_specs = (
        (rows, rows, P(), shard, shard)
        + (P(),) * 4
        + (shard, P()) * 4
        + (shard,) * 8
    )
    out_specs = (rows, rows) + (shard,) * 8
    return jax.shard_map(
        functools.partial(body, mesh.shape["ctx"]),
        mesh=mesh,
        in_specs=in_specs,
        out_specs=out_specs,
        check_vma=False,
    )
```

```python
import functools
import math

import jax
import jax.numpy as jnp
from jax import lax
from jax.experimental import pallas as pl
from jax.experimental.pallas import tpu as pltpu
from jax.sharding import PartitionSpec as P

HEADS = 8
HEAD = 256
ROT = 64
RANK = 16
BLOCK = 64
ADAPT_COLS = 128
WA = 4
PAIRS = 8
VMEM_BYTES = 58 * 1024 * 1024

epsilon = 1e-05
masked_score = -1e30
f32 = jnp.float32
bf16 = jnp.bfloat16


def product(left, right):
    return jnp.dot(left, right, preferred_element_type=f32)


def times_t(left, right):
    return lax.dot_general(left, right, (((1,), (1,)), ((), ())), preferred_element_type=f32)


def t_times(left, right):
    return lax.dot_general(left, right, (((0,), (0,)), ((), ())), preferred_element_type=f32)


def swap(value, bits):
    return lax.ppermute(value, "wa", [(i, i ^ bits) for i in range(WA)])


def after(value, *earlier):
    return lax.optimization_barrier((value, *earlier))[0]


def absolute(pieces, wa):
    low = wa % 2 == 1
    high = wa >= 2
    p = [
        jnp.where(low, pieces[1], pieces[0]),
        jnp.where(low, pieces[0], pieces[1]),
        jnp.where(low, pieces[3], pieces[2]),
        jnp.where(low, pieces[2], pieces[3]),
    ]
    return [
        jnp.where(high, p[2], p[0]),
        jnp.where(high, p[3], p[1]),
        jnp.where(high, p[0], p[2]),
        jnp.where(high, p[1], p[3]),
    ]


def rotary_tables(offset):
    half = ROT // 2
    lane = jnp.arange(128, dtype=jnp.int32)
    freq = 10000.0 ** (-2.0 * (lane % half).astype(f32) / ROT)
    freq = jnp.where(lane < ROT, freq, 0.0)
    angle = offset.astype(f32)[:, None] * freq[None, :]
    sign = jnp.where(lane < half, -1.0, 1.0)
    return jnp.cos(angle), jnp.sin(angle) * sign[None, :]


def turn_first(values, cosine, sine):
    lane = lax.broadcasted_iota(jnp.int32, values.shape, 1)
    partner = jnp.where(
        lane < ROT // 2, pltpu.roll(values, 128 - ROT // 2, 1), pltpu.roll(values, ROT // 2, 1)
    )
    return values * cosine + partner * sine


def call(kernel, index, inputs, outputs, grid=(1,), scratch=(), flops=0, name=None):
    def spec(shape, block, where):
        if where is None:
            zeros = (0,) * len(shape)
            return pl.BlockSpec(shape, lambda *_: zeros)
        return pl.BlockSpec(block, where)

    size = sum(a.size * a.dtype.itemsize if w is None else math.prod(i or 1 for i in b) * 2 * math.prod(grid)
               for a, b, w in inputs)
    return pl.pallas_call(
        kernel,
        grid_spec=pltpu.PrefetchScalarGridSpec(
            num_scalar_prefetch=1,
            grid=grid,
            in_specs=[spec(a.shape, b, w) for a, b, w in inputs],
            out_specs=[spec(s, b, w) for s, _, b, w in outputs],
            scratch_shapes=list(scratch),
        ),
        out_shape=[jax.ShapeDtypeStruct(s, d) for s, d, _, _ in outputs],
        compiler_params=pltpu.CompilerParams(vmem_limit_bytes=VMEM_BYTES),
        cost_estimate=pl.CostEstimate(flops=flops, bytes_accessed=size, transcendentals=0),
    )(index, *[a for a, _, _ in inputs])


def whole(array):
    return (array, None, None)


def copy_kernel(index_ref, *refs):
    count = len(refs) // 2
    for source, target in zip(refs[:count], refs[count:]):
        target[...] = source[...].reshape(target.shape)


def cut_columns(index, weight, size, kinds, cuts, parts=1):
    rows = weight.shape[0]
    part = size // parts
    inputs, outputs = [], []
    for r, division, number in cuts:
        height = rows // division

        def where(slot, t, ref, r=r, number=number):
            kind = sum(kind * (slot == i) for i, kind in enumerate(kinds))
            return (0 if number is None else ref[number], (kind * WA + ref[r]) * parts + t)

        inputs.append((weight, (height, part), where))
        outputs.append(
            (
                (height, len(kinds) * size),
                weight.dtype,
                (height, part),
                lambda slot, t, ref: (0, slot * parts + t),
            )
        )
    return call(copy_kernel, index, inputs, outputs, grid=(len(kinds), parts))


def strips(value):
    return [value[:, i : i + 128] for i in range(0, value.shape[1], 128)]


def store_strips(target, first, value):
    for item in strips(value):
        target[first : first + item.shape[0], :] = item
        first += item.shape[0]
    return first


def pack_kernel(index_ref, *refs):
    plain, last_ref = refs[:-6], refs[-6]
    (ups_mate, ups_peer, ups_far), (away_ref, near_ref) = refs[-5:-2], refs[-2:]
    first = 0
    for ref in plain:
        store_strips(away_ref, first, ref)
        first = store_strips(near_ref, first, ref)
    blank = ups_peer.shape[0] * ups_peer.shape[1] // 128
    store_strips(near_ref, first, ups_mate)
    store_strips(near_ref, first + blank, ups_mate)
    store_strips(away_ref, first, ups_peer)
    store_strips(away_ref, first + blank, ups_far)
    store_strips(near_ref, first + 2 * blank, last_ref)
    store_strips(away_ref, first + 2 * blank, last_ref)


def pack_small(index, plain, up, kinds, last):
    block = up.shape[1] // len(kinds) // WA
    items = [whole(item) for item in plain + [last]]
    size = sum(item.size for item in plain) // 128
    ups = up.shape[0] * block * len(kinds) // 128
    cut = jnp.concatenate if len(kinds) > 1 else (lambda v, axis: v[0])
    for r in (1, 2, 3):
        items.append(
            whole(
                cut(
                    [
                        lax.dynamic_slice_in_dim(up, (kind * WA + index[r]) * block, block, axis=1)
                        for kind in kinds
                    ],
                    axis=1,
                )
            )
        )
    shape = (size + 2 * ups + last.shape[0], 128)
    return call(pack_kernel, index, items, [(shape, bf16, None, None)] * 2)


def front_kernel(index_ref, *refs):
    token_ref, down_ref = refs[:2]
    packs = refs[2:5]
    mask_ref, g1, b1, g2, b2, first_ref, second_ref, inner_ref = refs[5:]
    rows, width = token_ref.shape
    wide = down_ref.shape[0]
    step = 32
    for r in range(WA):
        base = pl.multiple_of(index_ref[r] * rows, rows)
        for start in range(0, rows, step):
            if r == 0:
                values = token_ref[start : start + step, :]
            else:
                values = jnp.concatenate(
                    [
                        packs[r - 1][i * rows + start : i * rows + start + step, :]
                        for i in range(width // 128)
                    ],
                    axis=1,
                )
            values = values.astype(f32)
            centered = values - jnp.mean(values, axis=1, keepdims=True)
            spread = jnp.mean(centered * centered, axis=1, keepdims=True)
            normal = centered * lax.rsqrt(spread + epsilon)
            first_ref[pl.ds(base + start, step), :] = (normal * g1[...] + b1[...]).astype(bf16)
            second_ref[pl.ds(base + start, step), :] = (normal * g2[...] + b2[...]).astype(bf16)
    total = 0.0
    first = rows * width // 128
    for r in range(WA):
        columns = pl.ds(pl.multiple_of(index_ref[r] * wide, wide), wide)
        down = down_ref[...] if r == 0 else packs[r - 1][first : first + wide, :]
        total += product(first_ref[:, columns], down)
    inner_ref[...] = (total * mask_ref[...]).astype(bf16)


def pieces_of(index_ref, refs):
    wide = refs[0].shape[0]
    pieces = []
    for r, ref in enumerate(refs):
        size = ref.shape[0]
        first = index_ref[r] * wide
        if len(refs) > WA and r >= 2:
            first = index_ref[2 + (r - 2) // 2] * wide + (r % 2) * size
        pieces.append((pl.ds(pl.multiple_of(first, size), size), ref))
    return pieces


def read(ref):
    return ref[...].reshape(ref.shape[-2:])


def join_ups(index_ref, ups, joined):
    size = ADAPT_COLS // WA
    for r, ref in enumerate(ups):
        first = pl.multiple_of(index_ref[r] * size, size)
        if ref.shape[-1] == joined.shape[-1]:
            joined[pl.ds(first, size), :] = read(ref)
        else:
            for i in range(joined.shape[-1] // 128):
                joined[pl.ds(first, size), i * 128 : (i + 1) * 128] = ref[
                    i * size : (i + 1) * size, :
                ]


def qkv_kernel(turned, index_ref, hidden_ref, *refs):
    weights, ups = refs[:4], refs[4:8]
    inner_ref, bias_ref, cos_ref, sin_ref, out_ref, joined = refs[8:]
    join_ups(index_ref, ups, joined)
    total = product(inner_ref[...], joined[...]) + bias_ref[...]
    for columns, ref in pieces_of(index_ref, weights):
        total += product(hidden_ref[:, columns], read(ref))
    shape = out_ref.shape
    if turned:
        first = turn_first(total[:, :128], cos_ref[...], sin_ref[...])
        out_ref[..., :128] = first.astype(bf16).reshape(shape[:-1] + (128,))
        out_ref[..., 128:] = total[:, 128:].astype(bf16).reshape(shape[:-1] + (HEAD - 128,))
    else:
        out_ref[...] = total.astype(bf16).reshape(shape)


def grad_kernel(index_ref, *refs):
    parts = refs[:WA]
    mask_ref, weight_ref, down_ref = refs[WA : WA + 3]
    grad_ref, dense_ref, out_ref, heads_ref, ups_ref, dense_joined, out_joined = refs[WA + 3 :]
    size = ADAPT_COLS // WA
    rows = parts[0].shape[0] - 2 * size
    for r in range(WA):
        first = pl.ds(pl.multiple_of(index_ref[r] * size, size), size)
        dense_joined[first, :] = parts[r][rows : rows + size, :]
        out_joined[first, :] = parts[r][rows + size :, :]
        grad_ref[pl.ds(pl.multiple_of(index_ref[r] * rows, rows), rows), :] = parts[r][:rows, :]
    ups_ref[0] = dense_joined[...]
    ups_ref[1] = out_joined[...]
    grad = grad_ref[...]
    dense = (times_t(grad, dense_joined[...]) * mask_ref[...]).astype(bf16)
    dense_ref[...] = dense
    out_ref[...] = (times_t(grad, out_joined[...]) * mask_ref[...]).astype(bf16)
    for head in range(2):
        span = slice(head * HEAD, (head + 1) * HEAD)
        total = times_t(grad, weight_ref[span, :]) + times_t(dense, down_ref[span, :])
        heads_ref[:, head] = total.astype(bf16).reshape(WA, rows, HEAD)


def gelu_parts(values):
    bell = jnp.exp(-0.5 * values * values)
    t = 1.0 / (1.0 + (0.3275911 * math.sqrt(0.5)) * jnp.abs(values))
    series = 1.061405429 * 0.5
    for factor in (-1.453152027, 1.421413741, -0.284496736, 0.254829592):
        series = series * t + 0.5 * factor
    tail = series * t * bell
    below = jnp.where(values > 0, 1.0 - tail, tail)
    return values * below, below + values * bell * (1.0 / math.sqrt(2.0 * math.pi))


def feed_kernel(starts, ends, index_ref, hidden_ref, grad_ref, *refs):
    weights, ups, refs = refs[:6], refs[6:10], refs[10:]
    if starts:
        downs, mask_ref, refs = refs[:4], refs[4], refs[5:]
    else:
        known_ref, refs = refs[0], refs[1:]
    bias_ref, gain_ref, out_w_ref, out_down_ref, out_inner_grad_ref = refs[:5]
    (
        out_ref,
        norm_grad_ref,
        out_inner_ref,
        inner_grad_ref,
        out_down_grad_ref,
        in_up_grad_ref,
        inner_ref,
        joined,
    ) = refs[5:]
    step = pl.program_id(0)

    @pl.when(step == 0)
    def _():
        if starts:
            wide = downs[0].shape[0]
            total = 0.0
            for r in range(WA):
                columns = pl.ds(pl.multiple_of(index_ref[r] * wide, wide), wide)
                total += product(hidden_ref[:, columns], downs[r][...])
            inner_ref[...] = (total * mask_ref[...]).astype(bf16)
        else:
            inner_ref[...] = known_ref[...]
        out_ref[...] = jnp.zeros_like(out_ref)
        norm_grad_ref[...] = jnp.zeros_like(norm_grad_ref)
        out_inner_ref[...] = jnp.zeros_like(out_inner_ref)
        inner_grad_ref[...] = jnp.zeros_like(inner_grad_ref)

    join_ups(index_ref, ups, joined)
    pre = product(inner_ref[...], joined[...]) + bias_ref[...]
    for columns, ref in pieces_of(index_ref, weights):
        pre += product(hidden_ref[:, columns], read(ref))
    units, slope = gelu_parts(pre)
    units = units.astype(bf16)
    pre_grad = times_t(grad_ref[...], out_w_ref[...]) + times_t(
        out_inner_grad_ref[...], out_down_ref[...]
    )
    pre_grad = (pre_grad * slope).astype(bf16)
    out_ref[...] += product(units, out_w_ref[...])
    for columns, ref in pieces_of(index_ref, weights):
        norm_grad_ref[:, columns] += times_t(pre_grad, read(ref))
    out_inner_ref[...] += product(units, out_down_ref[...])
    inner_grad_ref[...] += times_t(pre_grad, joined[...])
    out_down_grad_ref[...] = t_times(units, out_inner_grad_ref[...]).astype(bf16)
    in_up_grad_ref[...] = t_times(inner_ref[...], pre_grad).astype(bf16)

    @pl.when(step == pl.num_programs(0) - 1)
    def _():
        norm_grad_ref[...] = norm_grad_ref[...] * gain_ref[...]


def scatter_rows(index_ref, total_ref, keep_ref, send_ref):
    rows = keep_ref.shape[1]
    for r, (ref, slot) in enumerate(((keep_ref, 0), (send_ref, 0), (keep_ref, 1), (send_ref, 1))):
        part = total_ref[pl.ds(pl.multiple_of(index_ref[r] * rows, rows), rows), :]
        ref[slot] = part.astype(ref.dtype)


def head_rows(ref, head):
    return ref[:, head, 0].reshape(-1, HEAD)


def dense_kernel(
    index_ref,
    heads_ref,
    sum_ref,
    weight_ref,
    down_ref,
    inner_grad_ref,
    keep_ref,
    send_ref,
    inner_ref,
    down_grad_ref,
    total,
):
    result = sum_ref[...]
    inner = 0.0
    for head in range(2):
        span = slice(head * HEAD, (head + 1) * HEAD)
        heads = head_rows(heads_ref, head)
        result += product(heads, weight_ref[span, :])
        inner += product(heads, down_ref[span, :])
        down_grad_ref[span, :] = t_times(heads, inner_grad_ref[...]).astype(bf16)
    inner_ref[...] = inner
    total[...] = result
    scatter_rows(index_ref, total, keep_ref, send_ref)


def mixed_rows(query_grad_ref, key_grad_ref, kind, head):
    if kind == 0:
        return query_grad_ref[:, head, 1].reshape(-1, HEAD)
    return key_grad_ref[:, head, kind + 1].reshape(-1, HEAD)


def mix_kernel(index_ref, *refs):
    grads, ups = refs[:2], refs[2 : 2 + 3 * WA]
    inner_ref, inner_grad_ref, up_grad_ref, joined = refs[2 + 3 * WA :]
    width = 2 * HEAD
    for kind in range(3):
        for r in range(WA):
            size = ADAPT_COLS // WA
            first = pl.multiple_of(index_ref[r] * size, size)
            ref = ups[kind * WA + r]
            if r == 0:
                joined[kind, pl.ds(first, size), :] = ref[...]
            else:
                for i in range(width // 128):
                    joined[kind, pl.ds(first, size), i * 128 : (i + 1) * 128] = ref[
                        i * size : (i + 1) * size, :
                    ]
    total = 0.0
    for kind in range(3):
        for head in range(2):
            span = slice(head * HEAD, (head + 1) * HEAD)
            rows = mixed_rows(*grads, kind, head)
            total += times_t(rows, joined[kind, :, span])
            out = slice(kind * width + head * HEAD, kind * width + (head + 1) * HEAD)
            up_grad_ref[:, out] = t_times(inner_ref[...], rows).astype(bf16)
    inner_grad_ref[...] = total


def norm_grad_kernel(index_ref, *refs):
    grads, weights = refs[:2], refs[2:14]
    gain_ref, sum_ref, keep_ref, send_ref, total = refs[14:]
    sets = [pieces_of(index_ref, weights[WA * kind : WA * kind + WA]) for kind in range(3)]
    rows = [[mixed_rows(*grads, kind, head) for head in range(2)] for kind in range(3)]
    for piece in range(WA):
        columns = sets[0][piece][0]
        part = 0.0
        for kind in range(3):
            weight = read(sets[kind][piece][1])
            for head in range(2):
                part += times_t(rows[kind][head], weight[:, head * HEAD : (head + 1) * HEAD])
        total[:, columns] = part * gain_ref[:, columns] + sum_ref[:, columns]
    scatter_rows(index_ref, total, keep_ref, send_ref)


def pack_grads_kernel(index_ref, *refs):
    first_ref, first_grad_ref, second_ref, second_grad_ref = refs[:4]
    dense_ref, out_ref, grad_ref, down_ref = refs[4:8]
    ups, (packed_ref, total) = refs[8:12], refs[12:]
    size = ADAPT_COLS // WA
    at = 0
    for norm, grad in ((first_ref, first_grad_ref), (second_ref, second_grad_ref)):
        part = t_times(norm[...], grad[...]).astype(bf16)
        packed_ref[at : at + part.shape[0], :] = part
        at += part.shape[0]
    packed_ref[at : at + down_ref.shape[0], :] = down_ref[...]
    at += down_ref.shape[0]
    for inner in (dense_ref, out_ref):
        total[...] = t_times(inner[...], grad_ref[...])
        own = total[pl.ds(pl.multiple_of(index_ref[0] * size, size), size), :].astype(bf16)
        at = store_strips(packed_ref, at, own)
    for ref in ups:
        at = store_strips(packed_ref, at, ref)


def pack_feed_kernel(index_ref, down_ref, *refs):
    parts, packed_ref = refs[:WA], refs[WA]
    packed_ref[: down_ref.shape[0], :] = down_ref[...]
    at = down_ref.shape[0]
    for ref in parts:
        at = store_strips(packed_ref, at, ref)


def unpack_feed_kernel(index_ref, source_ref, down_ref, up_ref):
    packed = source_ref[...].reshape(-1, ADAPT_COLS)
    size = ADAPT_COLS // WA
    at = down_ref.shape[0]
    down_ref[...] = packed[:at, :].astype(f32)
    block = up_ref.shape[1] // WA
    for r in range(WA):
        for i in range(block // 128):
            first = index_ref[r] * block + i * 128
            up_ref[:, pl.ds(pl.multiple_of(first, 128), 128)] = packed[at : at + size].astype(f32)
            at += size


def unpack_grads_kernel(index_ref, source_ref, *refs):
    first_ref, second_ref, down_ref, dense_ref, out_ref, up_ref = refs
    packed_ref = source_ref[...].reshape(-1, ADAPT_COLS)
    size = ADAPT_COLS // WA
    at = 0
    for ref in (first_ref, second_ref, down_ref):
        ref[...] = packed_ref[at : at + ref.shape[0], :].astype(f32)
        at += ref.shape[0]
    for ref in (dense_ref, out_ref):
        for i in range(ref.shape[1] // 128):
            ref[:, i * 128 : (i + 1) * 128] = packed_ref[at : at + size, :].astype(f32)
            at += size
    width = up_ref.shape[1] // 3
    block = width // WA
    for r in range(WA):
        for kind in range(3):
            first = kind * width + index_ref[r] * block
            for i in range(block // 128):
                columns = pl.ds(pl.multiple_of(first + i * 128, 128), 128)
                up_ref[:, columns] = packed_ref[at : at + size, :].astype(f32)
                at += size


def finish_kernel(index_ref, *refs):
    keep_ref, near_ref, away_ref, first_ref, second_ref = refs[:5]
    first_downs, second_downs = refs[5:9], refs[9:13]
    g1, g2, token_ref, grad_ref, out_ref, total = refs[13:]
    total[...] = keep_ref[0] + near_ref[0].astype(f32) + away_ref[...].astype(f32)
    wide = first_downs[0].shape[0]
    for r in range(WA):
        columns = pl.ds(pl.multiple_of(index_ref[r] * wide, wide), wide)
        total[:, columns] += (
            times_t(first_ref[...], first_downs[r][...]) * g1[:, columns]
            + times_t(second_ref[...], second_downs[r][...]) * g2[:, columns]
        )
    step = 32
    for start in range(0, total.shape[0], step):
        span = slice(start, start + step)
        values = token_ref[span, :].astype(f32)
        centered = values - jnp.mean(values, axis=1, keepdims=True)
        rstd = lax.rsqrt(jnp.mean(centered * centered, axis=1, keepdims=True) + epsilon)
        normal = centered * rstd
        part = total[span, :]
        part = (
            part
            - jnp.mean(part, axis=1, keepdims=True)
            - normal * jnp.mean(part * normal, axis=1, keepdims=True)
        )
        out_ref[span, :] = grad_ref[span, :].astype(f32) + rstd * part


def attention_kernel(
    joint,
    query_ref,
    key_ref,
    value_ref,
    grad_ref,
    begin_ref,
    place_ref,
    key_place_ref,
    q_cos_ref,
    q_sin_ref,
    k_cos_ref,
    k_sin_ref,
    rows_ref,
    *refs,
):
    keys_ref, dk_sum, dv_sum = (rows_ref, *refs) if joint else refs
    step = pl.program_id(0)
    scale = 1.0 / math.sqrt(HEAD)

    @pl.when(step == 0)
    def _():
        dk_sum[...] = jnp.zeros_like(dk_sum)
        dv_sum[...] = jnp.zeros_like(dv_sum)

    query = query_ref[...].reshape(-1, HEAD)
    key = key_ref[...].reshape(-1, HEAD)
    value = value_ref[...]
    grad = grad_ref[...]
    key_place = key_place_ref[...]
    allowed = (key_place >= begin_ref[...]) & (key_place <= place_ref[...])
    scores = jnp.where(allowed, times_t(query, key) * scale, masked_score)
    top = jnp.max(scores, axis=1, keepdims=True)
    weights = jnp.exp(scores - top)
    prob = weights * (1.0 / jnp.sum(weights, axis=1, keepdims=True))
    prob_low = prob.astype(bf16)
    part, block = query.shape[0], rows_ref.shape[2]
    shape = (part // block, block)
    own = pl.ds(step * shape[0], shape[0]) if joint else slice(None)
    rows_ref[own, 0] = product(prob_low, value).astype(bf16).reshape(shape + (HEAD,))
    prob_grad = times_t(grad, value)
    delta = jnp.sum(prob * prob_grad, axis=1, keepdims=True)
    score_grad = (prob * (prob_grad - delta)).astype(bf16)
    dq = product(score_grad, key) * scale
    first = turn_first(dq[:, :128], q_cos_ref[...], -q_sin_ref[...])
    rows_ref[own, 1, :, :128] = first.astype(bf16).reshape(shape + (128,))
    rows_ref[own, 1, :, 128:] = dq[:, 128:].astype(bf16).reshape(shape + (HEAD - 128,))
    dk_sum[...] += t_times(score_grad, query)
    dv_sum[...] += t_times(prob_low, grad)

    @pl.when(step == pl.num_programs(0) - 1)
    def _():
        base = 2 if joint else 0
        shape = keys_ref.shape[:1] + keys_ref.shape[2:3]
        dk = dk_sum[...] * scale
        first = turn_first(dk[:, :128], k_cos_ref[...], -k_sin_ref[...])
        keys_ref[:, base, :, :128] = first.astype(bf16).reshape(shape + (128,))
        keys_ref[:, base, :, 128:] = dk[:, 128:].astype(bf16).reshape(shape + (HEAD - 128,))
        keys_ref[:, base + 1] = dv_sum[...].astype(bf16).reshape(shape + (HEAD,))


def attend(query, key, value, grad, begin, place, key_place, q_tables, k_tables, block):
    rows = query.shape[0] * block
    keys = key.shape[0] * block
    part = min(256, rows)
    joint = rows == keys
    by_rows = lambda i: (i, 0)
    all_rows = lambda i: (0, 0)
    fixed = lambda i: (0, 0, 0, 0)
    if joint:
        shapes = [(keys // block, 4, block, HEAD)]
        out_specs = [pl.BlockSpec(shapes[0], fixed)]
    else:
        shapes = [(rows // block, 2, block, HEAD), (keys // block, 2, block, HEAD)]
        out_specs = [
            pl.BlockSpec((part // block, 2, block, HEAD), lambda i: (i, 0, 0, 0)),
            pl.BlockSpec(shapes[1], fixed),
        ]
    return pl.pallas_call(
        functools.partial(attention_kernel, joint),
        grid=(rows // part,),
        in_specs=[
            pl.BlockSpec((part // block, 1, block, HEAD), lambda i: (i, 1, 0, 0)),
            pl.BlockSpec((keys // block, 1, block, HEAD), fixed),
            pl.BlockSpec((keys, HEAD), all_rows),
            pl.BlockSpec((part, HEAD), by_rows),
            pl.BlockSpec((part, 1), by_rows),
            pl.BlockSpec((part, 1), by_rows),
            pl.BlockSpec((1, keys), all_rows),
            pl.BlockSpec((part, 128), by_rows),
            pl.BlockSpec((part, 128), by_rows),
            pl.BlockSpec((keys, 128), all_rows),
            pl.BlockSpec((keys, 128), all_rows),
        ],
        out_specs=out_specs,
        out_shape=[jax.ShapeDtypeStruct(shape, bf16) for shape in shapes],
        scratch_shapes=[pltpu.VMEM((keys, HEAD), f32), pltpu.VMEM((keys, HEAD), f32)],
        compiler_params=pltpu.CompilerParams(vmem_limit_bytes=VMEM_BYTES),
        cost_estimate=pl.CostEstimate(
            flops=14 * rows * keys * HEAD,
            bytes_accessed=16 * keys * HEAD,
            transcendentals=rows * keys,
        ),
    )(query, key, value, grad, begin, place, key_place, *q_tables, *k_tables)


def body(
    contexts,
    tokens,
    cotangent,
    deal,
    doc_lengths,
    doc_adapter,
    ln1_gain,
    ln1_bias,
    ln2_gain,
    ln2_bias,
    qkv_weight,
    qkv_bias,
    dense_weight,
    dense_bias,
    in_weight,
    in_bias,
    out_weight,
    out_bias,
    qkv_down,
    qkv_up,
    dense_down,
    dense_up,
    in_down,
    in_up,
    out_down,
    out_up,
):
    rows = tokens.shape[1]
    width = tokens.shape[2]
    wa = lax.axis_index("wa")
    ctx = lax.axis_index("ctx")
    total = WA * rows
    own_width = width // WA
    hidden_width = in_weight.shape[1] // WA
    part_cols = ADAPT_COLS // WA
    groups = contexts // PAIRS
    half = own_width // 2
    relative = [wa, wa ^ 1, wa ^ 2, wa ^ 3]
    index = jnp.stack(relative + [ctx % 2, ctx, wa * 0, wa * 0 + 1]).astype(jnp.int32)

    def columns(value, which, size):
        return lax.dynamic_slice_in_dim(value, which * size, size, axis=1)

    def part_rows(value, which, size):
        return lax.dynamic_slice_in_dim(value, which * size, size, axis=0)

    def gather_rows(weight, size, kinds, *earlier):
        cuts = cut_columns(index, weight, size, kinds, [(2, contexts, 5), (3, contexts, 5)])
        parts = [swap(after(cuts[0], *earlier), 2), swap(after(cuts[1], *earlier), 3)]
        part = jnp.concatenate(parts, axis=1)
        return part, lax.all_gather(part, "ctx", axis=0, tiled=True)

    qkv_others_part, qkv_others = gather_rows(qkv_weight, own_width, [2, 1, 0])
    in_cuts = cut_columns(
        index,
        in_weight,
        hidden_width,
        [0],
        [(2, 2, 6), (2, 2, 7), (3, 2, 6), (3, 2, 7)],
        4,
    )
    in_parts = [swap(after(in_cuts[0], qkv_others_part), 2)]
    limit = 64
    numbers = jnp.concatenate(
        [doc_lengths // limit, doc_lengths % limit, doc_adapter], axis=1
    ).astype(bf16)
    numbers = jnp.pad(numbers, ((0, 15), (0, 128 - numbers.shape[1])))
    first_pack = pack_small(index, [tokens[0], qkv_down], qkv_up, [0, 1, 2], numbers)

    def hand_on(away, near, *earlier):
        peer = swap(after(away, *earlier), 2)
        return [swap(near, 1), peer, swap(peer, 1)]

    mate_cuts = cut_columns(index, qkv_weight, own_width, [2, 1, 0], [(1, 1, None)])[0]
    in_mate_cut = cut_columns(index, in_weight, hidden_width, [0], [(1, 1, None)], 2)[0]
    first_packs = hand_on(*first_pack)
    grad_pack = jnp.concatenate([cotangent[0], dense_up, out_up], axis=0)
    grad_packs = hand_on(grad_pack, grad_pack, first_packs[1])
    mate_weights = swap(after(mate_cuts, first_packs[0]), 1)
    feed_pack = pack_small(index, [in_down], in_up, [0], numbers)
    feed_packs = hand_on(*feed_pack, grad_packs[1])

    docs_per_pack = doc_lengths.shape[1]
    tables = [numbers] + [item[-16:] for item in first_packs]
    tables = jnp.stack(absolute([item[0] for item in tables], wa)).astype(jnp.int32)
    lengths = tables[:, :docs_per_pack] * limit + tables[:, docs_per_pack : 2 * docs_per_pack]
    adapters = tables[:, 2 * docs_per_pack : 3 * docs_per_pack]
    starts = jnp.cumsum(lengths, axis=1) - lengths

    def places(first, size):
        slots = first + jnp.arange(size, dtype=jnp.int32)
        blocks = slots // BLOCK
        table = jnp.arange(deal.shape[0], dtype=jnp.int32)
        block = jnp.sum(jnp.where(table[None, :] == blocks[:, None], deal[None, :], 0), axis=1)
        return block * BLOCK + slots % BLOCK

    place = places(ctx * rows, rows)
    inside = starts[:, None, :] <= place[None, :, None]
    docs = jnp.sum(inside.astype(jnp.int32), axis=2) - 1
    begin = jnp.max(jnp.where(inside, starts[:, None, :], 0), axis=2)
    offset = (place[None, :] - begin).reshape(total)
    doc_table = jnp.arange(docs_per_pack, dtype=jnp.int32)
    chosen = jnp.sum(
        jnp.where(docs[:, :, None] == doc_table, adapters[:, None, :], 0), axis=2
    ).reshape(total)
    adapter_of = jnp.arange(ADAPT_COLS, dtype=jnp.int32) // RANK
    mask = (adapter_of[None, :] == chosen[:, None]).astype(f32)
    cosine, sine = rotary_tables(offset)

    gains = [item[None, :] for item in (ln1_gain, ln1_bias, ln2_gain, ln2_bias)]
    first_norm, second_norm, first_inner = call(
        front_kernel,
        index,
        [whole(item) for item in [after(tokens[0], in_parts[0], *feed_pack), qkv_down] + first_packs + [mask] + gains],
        [
            ((total, width), bf16, None, None),
            ((total, width), bf16, None, None),
            ((total, ADAPT_COLS), bf16, None, None),
        ],
        flops=2 * total * width * ADAPT_COLS,
    )

    strip = strip_rows = part_cols * HEAD // 128
    ups_row = (tokens.size + qkv_down.size) // 128
    ups_size = 3 * own_width * part_cols // 128

    def project(last, kinds, turned):
        own_block = lambda i, head, ref: (0, ((last - i) * WA + ref[0]) * 2 + head)
        items = [whole(first_norm), (qkv_weight, (own_width, HEAD), own_block)]
        for item, first in ((mate_weights, 0), (qkv_others, 0), (qkv_others, 3)):
            first = (first + 2 - last) * 2
            items.append(
                (
                    item,
                    (own_width, HEAD),
                    lambda i, head, ref, first=first: (0, first + 2 * i + head),
                )
            )
        items.append((qkv_up, (part_cols, HEAD), own_block))
        for r, item in zip((1, 2, 3), first_packs):
            row = (ups_row + (r == 3) * ups_size) // strip + last * 2
            items.append(
                (item, (strip, 128), lambda i, head, ref, row=row: (row - 2 * i + head, 0))
            )
        items += [
            whole(first_inner),
            (qkv_bias[None, :], (1, HEAD), own_block),
            whole(cosine),
            whole(sine),
        ]
        out = call(
            functools.partial(qkv_kernel, turned),
            index,
            items,
            [
                (
                    (WA, 2, kinds, rows, HEAD),
                    bf16,
                    (WA, 1, 1, rows, HEAD),
                    lambda i, head, ref: (0, head, i, 0, 0),
                )
            ],
            grid=(kinds, 2),
            scratch=[pltpu.VMEM((ADAPT_COLS, HEAD), bf16)],
            flops=2 * total * width * own_width * kinds,
        )[0]
        return out.reshape(PAIRS, kinds, rows, HEAD)

    def to_pairs(item):
        if groups == 1:
            return lax.all_to_all(item, "ctx", 0, 0, tiled=True)
        names = [[g * PAIRS + j for j in range(PAIRS)] for g in range(groups)]
        return lax.all_to_all(item, "ctx", 0, 0, axis_index_groups=names, tiled=True)

    grad, dense_inner_grad, out_inner_grad, attended_grad, all_ups = call(
        grad_kernel,
        index,
        [
            whole(item)
            for item in [after(grad_pack, first_inner)] + grad_packs + [mask, dense_weight, dense_down]
        ],
        [
            ((total, width), bf16, None, None),
            ((total, ADAPT_COLS), bf16, None, None),
            ((total, ADAPT_COLS), bf16, None, None),
            ((WA, 2, rows, HEAD), bf16, None, None),
            ((2, ADAPT_COLS, width), bf16, None, None),
        ],
        scratch=[pltpu.VMEM((ADAPT_COLS, width), bf16), pltpu.VMEM((ADAPT_COLS, width), bf16)],
        flops=2 * total * width * (own_width + 2 * ADAPT_COLS),
    )
    attended_grad = to_pairs(attended_grad.reshape(PAIRS, rows, HEAD))
    in_parts.append(swap(after(in_cuts[1], grad_packs[1]), 2))
    qkv_others = after(qkv_others, first_norm, grad)
    value = to_pairs(after(project(2, 1, False), attended_grad))
    in_parts.append(swap(after(in_cuts[2], in_parts[1]), 3))
    pair_own = after(project(1, 2, True), value, in_parts[2])
    pair = to_pairs(pair_own)
    in_parts.append(swap(after(in_cuts[3], in_parts[2]), 3))

    tile = min(512, hidden_width)
    tiles = hidden_width // tile
    in_downs = [whole(in_down)] + [
        (item, (own_width, ADAPT_COLS), lambda *_: (0, 0)) for item in feed_packs
    ]

    in_mate = swap(after(in_mate_cut, pair_own), 1)

    def feed(part, known, norm, *earlier):
        count = tiles
        first = part * count
        own_tile = lambda t, ref: (0, ref[0] * tiles + first + t)
        strip = part_cols * tile // 128
        items = [whole(after(norm, *earlier)), whole(grad)]
        items += [
            (in_weight, (own_width, tile), own_tile),
            (in_mate, (own_width, tile), lambda t, ref: (0, first + t)),
        ]
        items += [
            (item, (own_width // 2, tile), lambda t, ref: (0, first + t)) for item in in_parts
        ]
        items.append((in_up, (part_cols, tile), own_tile))
        for r, item in zip((1, 2, 3), feed_packs):
            row = (own_width + (r == 3) * part_cols * hidden_width // 128) // strip + first
            items.append((item, (strip, 128), lambda t, ref, row=row: (row + t, 0)))
        items += in_downs + [whole(mask)] if known is None else [whole(known)]
        items += [
            (in_bias[None, :], (1, tile), own_tile),
            whole(gains[2]),
            (out_weight, (tile, width), lambda t, ref: (first + t, 0)),
            (out_down, (tile, ADAPT_COLS), lambda t, ref: (first + t, 0)),
            whole(out_inner_grad),
        ]
        size = count * tile
        return call(
            functools.partial(feed_kernel, known is None, True),
            index,
            items,
            [
                ((total, width), f32, None, None),
                ((total, width), f32, None, None),
                ((total, ADAPT_COLS), f32, None, None),
                ((total, ADAPT_COLS), f32, None, None),
                ((size, ADAPT_COLS), bf16, (tile, ADAPT_COLS), lambda t, ref: (t, 0)),
                ((ADAPT_COLS, size), bf16, (ADAPT_COLS, tile), lambda t, ref: (0, t)),
                ((total, ADAPT_COLS), bf16, None, None),
            ],
            grid=(count,),
            scratch=[pltpu.VMEM((ADAPT_COLS, tile), bf16)],
            flops=8 * total * width * size,
        )

    (
        branch_sum,
        norm_grad,
        out_inner,
        second_inner_grad,
        out_down_grad,
        in_up_grad,
        second_inner,
    ) = feed(0, None, second_norm, pair)

    pair_rows = PAIRS * rows
    group = ctx // PAIRS
    own_pack = (ctx % PAIRS) // 2
    own_starts = jnp.sum(
        jnp.where(jnp.arange(WA)[:, None] == own_pack, starts, 0), axis=0
    )
    all_places = places(0, groups * pair_rows)
    all_inside = own_starts[None, :] <= all_places[:, None]
    all_begins = jnp.max(jnp.where(all_inside, own_starts[None, :], 0), axis=1)
    k_tables = rotary_tables(all_places - all_begins)
    if groups == 1:
        q_place, q_begin, q_tables = all_places, all_begins, k_tables
    else:
        q_place = part_rows(all_places, group, pair_rows)
        q_begin = part_rows(all_begins, group, pair_rows)
        q_tables = [part_rows(item, group, pair_rows) for item in k_tables]
    value, attended_grad = [item.reshape(pair_rows, HEAD) for item in (value, attended_grad)]
    key = pair
    sets = [[g * PAIRS + j for g in range(groups)] for j in range(PAIRS)]
    if groups > 1:
        key, value = [
            lax.all_gather(item, "ctx", axis=0, axis_index_groups=sets, tiled=True)
            for item in (pair[:, :1], value)
        ]
    both = attend(
        after(pair, in_parts[3], in_mate, *feed_packs),
        key,
        value,
        attended_grad,
        q_begin[:, None],
        q_place[:, None],
        all_places[None, :],
        q_tables,
        k_tables,
        rows,
    )
    if groups > 1:
        dkv = lax.psum_scatter(
            both[1], "ctx", scatter_dimension=0, axis_index_groups=sets, tiled=True
        )
        both = [jnp.concatenate([both[0], dkv], axis=1)]
    both = to_pairs(both[0]).reshape(WA, 2, 4, rows, HEAD)
    both = after(both, branch_sum)
    odq, dkv = both, both

    def sum_inner(partial):
        partial = (partial + swap(partial, 1)).astype(bf16)
        partial = partial.astype(f32) + swap(partial, 2).astype(f32)
        return (partial * mask).astype(bf16)

    def spread_rows(value):
        return [part_rows(value, wa, part_cols)] + [
            swap(part_rows(value, wa ^ r, part_cols), r) for r in (1, 2, 3)
        ]

    def exchange_sum(value):
        parts = value.reshape(contexts, -1, ADAPT_COLS)
        parts = lax.all_to_all(parts, "ctx", 0, 0, tiled=True)
        return jnp.sum(parts.astype(f32), axis=0).astype(bf16)

    feed_packed = call(
        pack_feed_kernel,
        index,
        [whole(item) for item in [out_down_grad] + spread_rows(in_up_grad)],
        [((2 * hidden_width, ADAPT_COLS), bf16, None, None)],
    )[0]
    feed_sum = exchange_sum(after(feed_packed, both))
    out_inner = sum_inner(out_inner)
    second_inner_grad = sum_inner(second_inner_grad)

    mixed_grads = [odq, dkv]
    up_items = []
    for kind in range(3):
        up_items.append(
            (qkv_up, (part_cols, own_width), lambda _, ref, kind=kind: (0, kind * WA + ref[0]))
        )
        for r, item in zip((1, 2, 3), first_packs):
            row = (ups_row + (r == 3) * ups_size) // (2 * strip_rows) + kind
            up_items.append(
                (item, (2 * strip_rows, 128), lambda _, ref, row=row: (row, 0))
            )
    mixed_inner, qkv_up_grad = call(
        mix_kernel,
        index,
        [whole(item) for item in mixed_grads] + up_items + [whole(first_inner)],
        [
            ((total, ADAPT_COLS), f32, None, None),
            ((ADAPT_COLS, 3 * own_width), bf16, None, None),
        ],
        scratch=[pltpu.VMEM((3, ADAPT_COLS, own_width), bf16)],
        flops=4 * total * ADAPT_COLS * 3 * own_width,
    )
    first_inner_grad = sum_inner(mixed_inner)
    up_parts = spread_rows(qkv_up_grad)
    dense_items = [after(odq, mixed_inner), branch_sum, dense_weight, dense_down, dense_inner_grad]
    reduced = [
        ((2, rows, width), f32, None, None),
        ((2, rows, width), bf16, None, None),
    ]
    keep, send, dense_inner, dense_down_grad = call(
        dense_kernel,
        index,
        [whole(item) for item in dense_items],
        reduced
        + [
            ((total, ADAPT_COLS), f32, None, None),
            ((own_width, ADAPT_COLS), bf16, None, None),
        ],
        scratch=[pltpu.VMEM((total, width), f32)],
        flops=2 * total * width * own_width,
    )
    dense_inner = sum_inner(dense_inner)
    near = swap(send, 1)
    away = swap((keep[1] + near[1].astype(f32)).astype(bf16), 2)
    output = (
        keep[0]
        + near[0].astype(f32)
        + away.astype(f32)
        + product(part_rows(dense_inner, wa, rows), all_ups[0])
        + product(part_rows(out_inner, wa, rows), all_ups[1])
        + dense_bias
        + out_bias
        + tokens[0].astype(f32)
    ).astype(bf16)[None]

    weight_items = []
    for kind in range(3):
        weight_items.append(
            (
                qkv_weight,
                (own_width, own_width),
                lambda _, ref, kind=kind: (0, kind * WA + ref[0]),
            )
        )
        for item, first in ((mate_weights, 2), (qkv_others, 2), (qkv_others, 5)):
            weight_items.append(
                (item, (own_width, own_width), lambda _, ref, at=first - kind: (0, at))
            )
    keep, send = call(
        norm_grad_kernel,
        index,
        [whole(item) for item in mixed_grads]
        + weight_items
        + [whole(item) for item in [after(gains[0], keep), norm_grad]],
        reduced,
        scratch=[pltpu.VMEM((total, width), f32)],
        flops=2 * total * width * 3 * own_width,
    )
    near = swap(send, 1)
    combined = (keep[1] + near[1].astype(f32)).astype(bf16)
    away = swap(combined, 2)
    down_at = rows * width // 128 // own_width
    down_block = lambda *_: (down_at, 0)
    tokens_grad = call(
        finish_kernel,
        index,
        [
            whole(item)
            for item in [
                keep,
                near,
                away,
                part_rows(first_inner_grad, wa, rows),
                part_rows(second_inner_grad, wa, rows),
            ]
        ]
        + [whole(qkv_down)]
        + [(item, (own_width, ADAPT_COLS), down_block) for item in first_packs]
        + in_downs
        + [whole(item) for item in [gains[0], gains[2], tokens[0], cotangent[0]]],
        [((rows, width), f32, None, None)],
        scratch=[pltpu.VMEM((rows, width), f32)],
    )[0][None]

    own_norm = lambda _, ref: (0, ref[0])
    items = [
        (first_norm, (total, own_width), own_norm),
        whole(first_inner_grad),
    ]
    items += [(second_norm, (total, own_width), own_norm), whole(second_inner_grad)]
    items += [whole(item) for item in [dense_inner, out_inner, grad, dense_down_grad] + up_parts]
    packed = call(
        pack_grads_kernel,
        index,
        items,
        [((8 * own_width, ADAPT_COLS), bf16, None, None)],
        scratch=[pltpu.VMEM((ADAPT_COLS, width), f32)],
    )[0]
    packed = exchange_sum(after(packed, feed_sum))
    packed = jnp.stack([feed_sum, packed])
    packed = lax.all_to_all(
        jnp.broadcast_to(packed[None], (contexts,) + packed.shape), "ctx", 0, 0, tiled=True
    )
    packed = after(packed, tokens_grad, output)
    block = (contexts, 1) + packed.shape[2:]
    out_down_grad, in_up_grad = call(
        unpack_feed_kernel,
        index,
        [(packed, block, lambda *_: (0, 0, 0, 0))],
        [
            ((hidden_width, ADAPT_COLS), f32, None, None),
            ((part_cols, WA * hidden_width), f32, None, None),
        ],
    )
    down_shape = ((own_width, ADAPT_COLS), f32, None, None)
    up_shape = ((part_cols, width), f32, None, None)
    (
        qkv_down_grad,
        in_down_grad,
        dense_down_grad,
        dense_up_grad,
        out_up_grad,
        qkv_up_grad,
    ) = call(
        unpack_grads_kernel,
        index,
        [(packed, block, lambda *_: (0, 1, 0, 0))],
        [down_shape] * 3 + [up_shape] * 2 + [((part_cols, 3 * width), f32, None, None)],
    )
    return (
        output,
        tokens_grad,
        qkv_down_grad,
        qkv_up_grad,
        dense_down_grad,
        dense_up_grad,
        in_down_grad,
        in_up_grad,
        out_down_grad,
        out_up_grad,
    )


def solution(mesh):
    rows = P("wa", "ctx", None)
    shard = P("wa", None)
    in_specs = (
        (rows, rows, P(), shard, shard)
        + (P(),) * 4
        + (shard, P()) * 4
        + (shard,) * 8
    )
    out_specs = (rows, rows) + (shard,) * 8
    return jax.shard_map(
        functools.partial(body, mesh.shape["ctx"]),
        mesh=mesh,
        in_specs=in_specs,
        out_specs=out_specs,
        check_vma=False,
    )
```

```python
import functools
import math

import jax
import jax.numpy as jnp
from jax import lax
from jax.experimental import pallas as pl
from jax.experimental.pallas import tpu as pltpu
from jax.sharding import PartitionSpec as P

HEADS = 8
HEAD = 256
ROT = 64
RANK = 16
BLOCK = 64
ADAPT_COLS = 128
WA = 4
PAIRS = 8
VMEM_BYTES = 58 * 1024 * 1024

epsilon = 1e-05
masked_score = -1e30
f32 = jnp.float32
bf16 = jnp.bfloat16


def product(left, right):
    return jnp.dot(left, right, preferred_element_type=f32)


def times_t(left, right):
    return lax.dot_general(left, right, (((1,), (1,)), ((), ())), preferred_element_type=f32)


def t_times(left, right):
    return lax.dot_general(left, right, (((0,), (0,)), ((), ())), preferred_element_type=f32)


def swap(value, bits):
    return lax.ppermute(value, "wa", [(i, i ^ bits) for i in range(WA)])


def after(value, *earlier):
    return lax.optimization_barrier((value, *earlier))[0]


def absolute(pieces, wa):
    low = wa % 2 == 1
    high = wa >= 2
    p = [
        jnp.where(low, pieces[1], pieces[0]),
        jnp.where(low, pieces[0], pieces[1]),
        jnp.where(low, pieces[3], pieces[2]),
        jnp.where(low, pieces[2], pieces[3]),
    ]
    return [
        jnp.where(high, p[2], p[0]),
        jnp.where(high, p[3], p[1]),
        jnp.where(high, p[0], p[2]),
        jnp.where(high, p[1], p[3]),
    ]


def rotary_tables(offset):
    half = ROT // 2
    lane = jnp.arange(128, dtype=jnp.int32)
    freq = 10000.0 ** (-2.0 * (lane % half).astype(f32) / ROT)
    freq = jnp.where(lane < ROT, freq, 0.0)
    angle = offset.astype(f32)[:, None] * freq[None, :]
    sign = jnp.where(lane < half, -1.0, 1.0)
    return jnp.cos(angle), jnp.sin(angle) * sign[None, :]


def turn_first(values, cosine, sine):
    lane = lax.broadcasted_iota(jnp.int32, values.shape, 1)
    partner = jnp.where(
        lane < ROT // 2, pltpu.roll(values, 128 - ROT // 2, 1), pltpu.roll(values, ROT // 2, 1)
    )
    return values * cosine + partner * sine


def call(kernel, index, inputs, outputs, grid=(1,), scratch=(), flops=0, name=None):
    def spec(shape, block, where):
        if where is None:
            zeros = (0,) * len(shape)
            return pl.BlockSpec(shape, lambda *_: zeros)
        return pl.BlockSpec(block, where)

    size = sum(a.size * a.dtype.itemsize if w is None else math.prod(i or 1 for i in b) * 2 * math.prod(grid)
               for a, b, w in inputs)
    return pl.pallas_call(
        kernel,
        grid_spec=pltpu.PrefetchScalarGridSpec(
            num_scalar_prefetch=1,
            grid=grid,
            in_specs=[spec(a.shape, b, w) for a, b, w in inputs],
            out_specs=[spec(s, b, w) for s, _, b, w in outputs],
            scratch_shapes=list(scratch),
        ),
        out_shape=[jax.ShapeDtypeStruct(s, d) for s, d, _, _ in outputs],
        compiler_params=pltpu.CompilerParams(vmem_limit_bytes=VMEM_BYTES),
        cost_estimate=pl.CostEstimate(flops=flops, bytes_accessed=size, transcendentals=0),
    )(index, *[a for a, _, _ in inputs])


def whole(array):
    return (array, None, None)


def copy_kernel(index_ref, *refs):
    count = len(refs) // 2
    for source, target in zip(refs[:count], refs[count:]):
        target[...] = source[...].reshape(target.shape)


def cut_columns(index, weight, size, kinds, cuts, parts=1):
    rows = weight.shape[0]
    part = size // parts
    inputs, outputs = [], []
    for r, division, number in cuts:
        height = rows // division

        def where(slot, t, ref, r=r, number=number):
            kind = sum(kind * (slot == i) for i, kind in enumerate(kinds))
            return (0 if number is None else ref[number], (kind * WA + ref[r]) * parts + t)

        inputs.append((weight, (height, part), where))
        outputs.append(
            (
                (height, len(kinds) * size),
                weight.dtype,
                (height, part),
                lambda slot, t, ref: (0, slot * parts + t),
            )
        )
    return call(copy_kernel, index, inputs, outputs, grid=(len(kinds), parts))


def strips(value):
    return [value[:, i : i + 128] for i in range(0, value.shape[1], 128)]


def store_strips(target, first, value):
    for item in strips(value):
        target[first : first + item.shape[0], :] = item
        first += item.shape[0]
    return first


def pack_kernel(index_ref, *refs):
    plain, last_ref = refs[:-6], refs[-6]
    (ups_mate, ups_peer, ups_far), (away_ref, near_ref) = refs[-5:-2], refs[-2:]
    first = 0
    for ref in plain:
        store_strips(away_ref, first, ref)
        first = store_strips(near_ref, first, ref)
    blank = ups_peer.shape[0] * ups_peer.shape[1] // 128
    store_strips(near_ref, first, ups_mate)
    store_strips(near_ref, first + blank, ups_mate)
    store_strips(away_ref, first, ups_peer)
    store_strips(away_ref, first + blank, ups_far)
    store_strips(near_ref, first + 2 * blank, last_ref)
    store_strips(away_ref, first + 2 * blank, last_ref)


def pack_small(index, plain, up, kinds, last):
    block = up.shape[1] // len(kinds) // WA
    items = [whole(item) for item in plain + [last]]
    size = sum(item.size for item in plain) // 128
    ups = up.shape[0] * block * len(kinds) // 128
    cut = jnp.concatenate if len(kinds) > 1 else (lambda v, axis: v[0])
    for r in (1, 2, 3):
        items.append(
            whole(
                cut(
                    [
                        lax.dynamic_slice_in_dim(up, (kind * WA + index[r]) * block, block, axis=1)
                        for kind in kinds
                    ],
                    axis=1,
                )
            )
        )
    shape = (size + 2 * ups + last.shape[0], 128)
    return call(pack_kernel, index, items, [(shape, bf16, None, None)] * 2)


def front_kernel(index_ref, *refs):
    token_ref, down_ref = refs[:2]
    packs = refs[2:5]
    mask_ref, g1, b1, g2, b2, first_ref, second_ref, inner_ref = refs[5:]
    rows, width = token_ref.shape
    wide = down_ref.shape[0]
    step = 32
    for r in range(WA):
        base = pl.multiple_of(index_ref[r] * rows, rows)
        for start in range(0, rows, step):
            if r == 0:
                values = token_ref[start : start + step, :]
            else:
                values = jnp.concatenate(
                    [
                        packs[r - 1][i * rows + start : i * rows + start + step, :]
                        for i in range(width // 128)
                    ],
                    axis=1,
                )
            values = values.astype(f32)
            centered = values - jnp.mean(values, axis=1, keepdims=True)
            spread = jnp.mean(centered * centered, axis=1, keepdims=True)
            normal = centered * lax.rsqrt(spread + epsilon)
            first_ref[pl.ds(base + start, step), :] = (normal * g1[...] + b1[...]).astype(bf16)
            second_ref[pl.ds(base + start, step), :] = (normal * g2[...] + b2[...]).astype(bf16)
    total = 0.0
    first = rows * width // 128
    for r in range(WA):
        columns = pl.ds(pl.multiple_of(index_ref[r] * wide, wide), wide)
        down = down_ref[...] if r == 0 else packs[r - 1][first : first + wide, :]
        total += product(first_ref[:, columns], down)
    inner_ref[...] = (total * mask_ref[...]).astype(bf16)


def pieces_of(index_ref, refs):
    wide = refs[0].shape[0]
    pieces = []
    for r, ref in enumerate(refs):
        size = ref.shape[0]
        first = index_ref[r] * wide
        if len(refs) > WA and r >= 2:
            first = index_ref[2 + (r - 2) // 2] * wide + (r % 2) * size
        pieces.append((pl.ds(pl.multiple_of(first, size), size), ref))
    return pieces


def read(ref):
    return ref[...].reshape(ref.shape[-2:])


def join_ups(index_ref, ups, joined):
    size = ADAPT_COLS // WA
    for r, ref in enumerate(ups):
        first = pl.multiple_of(index_ref[r] * size, size)
        if ref.shape[-1] == joined.shape[-1]:
            joined[pl.ds(first, size), :] = read(ref)
        else:
            for i in range(joined.shape[-1] // 128):
                joined[pl.ds(first, size), i * 128 : (i + 1) * 128] = ref[
                    i * size : (i + 1) * size, :
                ]


def qkv_kernel(turned, index_ref, hidden_ref, *refs):
    weights, ups = refs[:4], refs[4:8]
    inner_ref, bias_ref, cos_ref, sin_ref, out_ref, joined = refs[8:]
    join_ups(index_ref, ups, joined)
    total = product(inner_ref[...], joined[...]) + bias_ref[...]
    for columns, ref in pieces_of(index_ref, weights):
        total += product(hidden_ref[:, columns], read(ref))
    shape = out_ref.shape
    if turned:
        first = turn_first(total[:, :128], cos_ref[...], sin_ref[...])
        out_ref[..., :128] = first.astype(bf16).reshape(shape[:-1] + (128,))
        out_ref[..., 128:] = total[:, 128:].astype(bf16).reshape(shape[:-1] + (HEAD - 128,))
    else:
        out_ref[...] = total.astype(bf16).reshape(shape)


def grad_kernel(index_ref, *refs):
    parts = refs[:WA]
    mask_ref, weight_ref, down_ref = refs[WA : WA + 3]
    grad_ref, dense_ref, out_ref, heads_ref, ups_ref, dense_joined, out_joined = refs[WA + 3 :]
    size = ADAPT_COLS // WA
    rows = parts[0].shape[0] - 2 * size
    for r in range(WA):
        first = pl.ds(pl.multiple_of(index_ref[r] * size, size), size)
        dense_joined[first, :] = parts[r][rows : rows + size, :]
        out_joined[first, :] = parts[r][rows + size :, :]
        grad_ref[pl.ds(pl.multiple_of(index_ref[r] * rows, rows), rows), :] = parts[r][:rows, :]
    ups_ref[0] = dense_joined[...]
    ups_ref[1] = out_joined[...]
    grad = grad_ref[...]
    dense = (times_t(grad, dense_joined[...]) * mask_ref[...]).astype(bf16)
    dense_ref[...] = dense
    out_ref[...] = (times_t(grad, out_joined[...]) * mask_ref[...]).astype(bf16)
    for head in range(2):
        span = slice(head * HEAD, (head + 1) * HEAD)
        total = times_t(grad, weight_ref[span, :]) + times_t(dense, down_ref[span, :])
        heads_ref[:, head] = total.astype(bf16).reshape(WA, rows, HEAD)


def gelu_parts(values):
    bell = jnp.exp(-0.5 * values * values)
    t = 1.0 / (1.0 + (0.3275911 * math.sqrt(0.5)) * jnp.abs(values))
    series = 1.061405429 * 0.5
    for factor in (-1.453152027, 1.421413741, -0.284496736, 0.254829592):
        series = series * t + 0.5 * factor
    tail = series * t * bell
    below = jnp.where(values > 0, 1.0 - tail, tail)
    return values * below, below + values * bell * (1.0 / math.sqrt(2.0 * math.pi))


def feed_kernel(starts, ends, index_ref, hidden_ref, grad_ref, *refs):
    weights, ups, refs = refs[:6], refs[6:10], refs[10:]
    if starts:
        downs, mask_ref, refs = refs[:4], refs[4], refs[5:]
    else:
        known_ref, refs = refs[0], refs[1:]
    bias_ref, gain_ref, out_w_ref, out_down_ref, out_inner_grad_ref = refs[:5]
    (
        out_ref,
        norm_grad_ref,
        out_inner_ref,
        inner_grad_ref,
        out_down_grad_ref,
        in_up_grad_ref,
        inner_ref,
        joined,
    ) = refs[5:]
    step = pl.program_id(0)

    @pl.when(step == 0)
    def _():
        if starts:
            wide = downs[0].shape[0]
            total = 0.0
            for r in range(WA):
                columns = pl.ds(pl.multiple_of(index_ref[r] * wide, wide), wide)
                total += product(hidden_ref[:, columns], downs[r][...])
            inner_ref[...] = (total * mask_ref[...]).astype(bf16)
        else:
            inner_ref[...] = known_ref[...]
        out_ref[...] = jnp.zeros_like(out_ref)
        norm_grad_ref[...] = jnp.zeros_like(norm_grad_ref)
        out_inner_ref[...] = jnp.zeros_like(out_inner_ref)
        inner_grad_ref[...] = jnp.zeros_like(inner_grad_ref)

    join_ups(index_ref, ups, joined)
    pre = product(inner_ref[...], joined[...]) + bias_ref[...]
    for columns, ref in pieces_of(index_ref, weights):
        pre += product(hidden_ref[:, columns], read(ref))
    units, slope = gelu_parts(pre)
    units = units.astype(bf16)
    pre_grad = times_t(grad_ref[...], out_w_ref[...]) + times_t(
        out_inner_grad_ref[...], out_down_ref[...]
    )
    pre_grad = (pre_grad * slope).astype(bf16)
    out_ref[...] += product(units, out_w_ref[...])
    for columns, ref in pieces_of(index_ref, weights):
        norm_grad_ref[:, columns] += times_t(pre_grad, read(ref))
    out_inner_ref[...] += product(units, out_down_ref[...])
    inner_grad_ref[...] += times_t(pre_grad, joined[...])
    out_down_grad_ref[...] = t_times(units, out_inner_grad_ref[...]).astype(bf16)
    in_up_grad_ref[...] = t_times(inner_ref[...], pre_grad).astype(bf16)

    @pl.when(step == pl.num_programs(0) - 1)
    def _():
        norm_grad_ref[...] = norm_grad_ref[...] * gain_ref[...]


def scatter_rows(index_ref, total_ref, keep_ref, send_ref):
    rows = keep_ref.shape[1]
    for r, (ref, slot) in enumerate(((keep_ref, 0), (send_ref, 0), (keep_ref, 1), (send_ref, 1))):
        part = total_ref[pl.ds(pl.multiple_of(index_ref[r] * rows, rows), rows), :]
        ref[slot] = part.astype(ref.dtype)


def head_rows(ref, head):
    return ref[:, head, 0].reshape(-1, HEAD)


def dense_kernel(
    index_ref,
    heads_ref,
    sum_ref,
    weight_ref,
    down_ref,
    inner_grad_ref,
    keep_ref,
    send_ref,
    inner_ref,
    down_grad_ref,
    total,
):
    result = sum_ref[...]
    inner = 0.0
    for head in range(2):
        span = slice(head * HEAD, (head + 1) * HEAD)
        heads = head_rows(heads_ref, head)
        result += product(heads, weight_ref[span, :])
        inner += product(heads, down_ref[span, :])
        down_grad_ref[span, :] = t_times(heads, inner_grad_ref[...]).astype(bf16)
    inner_ref[...] = inner
    total[...] = result
    scatter_rows(index_ref, total, keep_ref, send_ref)


def mixed_rows(query_grad_ref, key_grad_ref, kind, head):
    if kind == 0:
        return query_grad_ref[:, head, 1].reshape(-1, HEAD)
    return key_grad_ref[:, head, kind + 1].reshape(-1, HEAD)


def mix_kernel(index_ref, *refs):
    grads, ups = refs[:2], refs[2 : 2 + 3 * WA]
    inner_ref, inner_grad_ref, up_grad_ref, joined = refs[2 + 3 * WA :]
    width = 2 * HEAD
    for kind in range(3):
        for r in range(WA):
            size = ADAPT_COLS // WA
            first = pl.multiple_of(index_ref[r] * size, size)
            ref = ups[kind * WA + r]
            if r == 0:
                joined[kind, pl.ds(first, size), :] = ref[...]
            else:
                for i in range(width // 128):
                    joined[kind, pl.ds(first, size), i * 128 : (i + 1) * 128] = ref[
                        i * size : (i + 1) * size, :
                    ]
    total = 0.0
    for kind in range(3):
        for head in range(2):
            span = slice(head * HEAD, (head + 1) * HEAD)
            rows = mixed_rows(*grads, kind, head)
            total += times_t(rows, joined[kind, :, span])
            out = slice(kind * width + head * HEAD, kind * width + (head + 1) * HEAD)
            up_grad_ref[:, out] = t_times(inner_ref[...], rows).astype(bf16)
    inner_grad_ref[...] = total


def norm_grad_kernel(index_ref, *refs):
    grads, weights = refs[:2], refs[2:14]
    gain_ref, sum_ref, keep_ref, send_ref, total = refs[14:]
    sets = [pieces_of(index_ref, weights[WA * kind : WA * kind + WA]) for kind in range(3)]
    rows = [[mixed_rows(*grads, kind, head) for head in range(2)] for kind in range(3)]
    for piece in range(WA):
        columns = sets[0][piece][0]
        part = 0.0
        for kind in range(3):
            weight = read(sets[kind][piece][1])
            for head in range(2):
                part += times_t(rows[kind][head], weight[:, head * HEAD : (head + 1) * HEAD])
        total[:, columns] = part * gain_ref[:, columns] + sum_ref[:, columns]
    scatter_rows(index_ref, total, keep_ref, send_ref)


def pack_grads_kernel(index_ref, *refs):
    first_ref, first_grad_ref, second_ref, second_grad_ref = refs[:4]
    dense_ref, out_ref, grad_ref, down_ref = refs[4:8]
    ups, (packed_ref, total) = refs[8:12], refs[12:]
    size = ADAPT_COLS // WA
    at = 0
    for norm, grad in ((first_ref, first_grad_ref), (second_ref, second_grad_ref)):
        part = t_times(norm[...], grad[...]).astype(bf16)
        packed_ref[at : at + part.shape[0], :] = part
        at += part.shape[0]
    packed_ref[at : at + down_ref.shape[0], :] = down_ref[...]
    at += down_ref.shape[0]
    for inner in (dense_ref, out_ref):
        total[...] = t_times(inner[...], grad_ref[...])
        own = total[pl.ds(pl.multiple_of(index_ref[0] * size, size), size), :].astype(bf16)
        at = store_strips(packed_ref, at, own)
    for ref in ups:
        at = store_strips(packed_ref, at, ref)


def pack_feed_kernel(index_ref, down_ref, *refs):
    parts, packed_ref = refs[:WA], refs[WA]
    packed_ref[: down_ref.shape[0], :] = down_ref[...]
    at = down_ref.shape[0]
    for ref in parts:
        at = store_strips(packed_ref, at, ref)


def unpack_feed_kernel(index_ref, source_ref, down_ref, up_ref):
    packed = source_ref[...].reshape(-1, ADAPT_COLS)
    size = ADAPT_COLS // WA
    at = down_ref.shape[0]
    down_ref[...] = packed[:at, :].astype(f32)
    block = up_ref.shape[1] // WA
    for r in range(WA):
        for i in range(block // 128):
            first = index_ref[r] * block + i * 128
            up_ref[:, pl.ds(pl.multiple_of(first, 128), 128)] = packed[at : at + size].astype(f32)
            at += size


def unpack_grads_kernel(index_ref, source_ref, *refs):
    first_ref, second_ref, down_ref, dense_ref, out_ref, up_ref = refs
    packed_ref = source_ref[...].reshape(-1, ADAPT_COLS)
    size = ADAPT_COLS // WA
    at = 0
    for ref in (first_ref, second_ref, down_ref):
        ref[...] = packed_ref[at : at + ref.shape[0], :].astype(f32)
        at += ref.shape[0]
    for ref in (dense_ref, out_ref):
        for i in range(ref.shape[1] // 128):
            ref[:, i * 128 : (i + 1) * 128] = packed_ref[at : at + size, :].astype(f32)
            at += size
    width = up_ref.shape[1] // 3
    block = width // WA
    for r in range(WA):
        for kind in range(3):
            first = kind * width + index_ref[r] * block
            for i in range(block // 128):
                columns = pl.ds(pl.multiple_of(first + i * 128, 128), 128)
                up_ref[:, columns] = packed_ref[at : at + size, :].astype(f32)
                at += size


def finish_kernel(index_ref, *refs):
    keep_ref, near_ref, away_ref, first_ref, second_ref = refs[:5]
    first_downs, second_downs = refs[5:9], refs[9:13]
    g1, g2, token_ref, grad_ref, out_ref, total = refs[13:]
    total[...] = keep_ref[0] + near_ref[0].astype(f32) + away_ref[...].astype(f32)
    wide = first_downs[0].shape[0]
    for r in range(WA):
        columns = pl.ds(pl.multiple_of(index_ref[r] * wide, wide), wide)
        total[:, columns] += (
            times_t(first_ref[...], first_downs[r][...]) * g1[:, columns]
            + times_t(second_ref[...], second_downs[r][...]) * g2[:, columns]
        )
    step = 32
    for start in range(0, total.shape[0], step):
        span = slice(start, start + step)
        values = token_ref[span, :].astype(f32)
        centered = values - jnp.mean(values, axis=1, keepdims=True)
        rstd = lax.rsqrt(jnp.mean(centered * centered, axis=1, keepdims=True) + epsilon)
        normal = centered * rstd
        part = total[span, :]
        part = (
            part
            - jnp.mean(part, axis=1, keepdims=True)
            - normal * jnp.mean(part * normal, axis=1, keepdims=True)
        )
        out_ref[span, :] = grad_ref[span, :].astype(f32) + rstd * part


def attention_kernel(
    joint,
    query_ref,
    key_ref,
    value_ref,
    grad_ref,
    begin_ref,
    place_ref,
    key_place_ref,
    q_cos_ref,
    q_sin_ref,
    k_cos_ref,
    k_sin_ref,
    rows_ref,
    *refs,
):
    keys_ref, dk_sum, dv_sum = (rows_ref, *refs) if joint else refs
    step = pl.program_id(0)
    scale = 1.0 / math.sqrt(HEAD)

    @pl.when(step == 0)
    def _():
        dk_sum[...] = jnp.zeros_like(dk_sum)
        dv_sum[...] = jnp.zeros_like(dv_sum)

    query = query_ref[...].reshape(-1, HEAD)
    key = key_ref[...].reshape(-1, HEAD)
    value = value_ref[...]
    grad = grad_ref[...]
    key_place = key_place_ref[...]
    allowed = (key_place >= begin_ref[...]) & (key_place <= place_ref[...])
    scores = jnp.where(allowed, times_t(query, key) * scale, masked_score)
    top = jnp.max(scores, axis=1, keepdims=True)
    weights = jnp.exp(scores - top)
    prob = weights * (1.0 / jnp.sum(weights, axis=1, keepdims=True))
    prob_low = prob.astype(bf16)
    part, block = query.shape[0], rows_ref.shape[2]
    shape = (part // block, block)
    own = pl.ds(step * shape[0], shape[0]) if joint else slice(None)
    rows_ref[own, 0] = product(prob_low, value).astype(bf16).reshape(shape + (HEAD,))
    prob_grad = times_t(grad, value)
    delta = jnp.sum(prob * prob_grad, axis=1, keepdims=True)
    score_grad = (prob * (prob_grad - delta)).astype(bf16)
    dq = product(score_grad, key) * scale
    first = turn_first(dq[:, :128], q_cos_ref[...], -q_sin_ref[...])
    rows_ref[own, 1, :, :128] = first.astype(bf16).reshape(shape + (128,))
    rows_ref[own, 1, :, 128:] = dq[:, 128:].astype(bf16).reshape(shape + (HEAD - 128,))
    dk_sum[...] += t_times(score_grad, query)
    dv_sum[...] += t_times(prob_low, grad)

    @pl.when(step == pl.num_programs(0) - 1)
    def _():
        base = 2 if joint else 0
        shape = keys_ref.shape[:1] + keys_ref.shape[2:3]
        dk = dk_sum[...] * scale
        first = turn_first(dk[:, :128], k_cos_ref[...], -k_sin_ref[...])
        keys_ref[:, base, :, :128] = first.astype(bf16).reshape(shape + (128,))
        keys_ref[:, base, :, 128:] = dk[:, 128:].astype(bf16).reshape(shape + (HEAD - 128,))
        keys_ref[:, base + 1] = dv_sum[...].astype(bf16).reshape(shape + (HEAD,))


def attend(query, key, value, grad, begin, place, key_place, q_tables, k_tables, block):
    rows = query.shape[0] * block
    keys = key.shape[0] * block
    part = min(256, rows)
    joint = rows == keys
    by_rows = lambda i: (i, 0)
    all_rows = lambda i: (0, 0)
    fixed = lambda i: (0, 0, 0, 0)
    if joint:
        shapes = [(keys // block, 4, block, HEAD)]
        out_specs = [pl.BlockSpec(shapes[0], fixed)]
    else:
        shapes = [(rows // block, 2, block, HEAD), (keys // block, 2, block, HEAD)]
        out_specs = [
            pl.BlockSpec((part // block, 2, block, HEAD), lambda i: (i, 0, 0, 0)),
            pl.BlockSpec(shapes[1], fixed),
        ]
    return pl.pallas_call(
        functools.partial(attention_kernel, joint),
        grid=(rows // part,),
        in_specs=[
            pl.BlockSpec((part // block, 1, block, HEAD), lambda i: (i, 1, 0, 0)),
            pl.BlockSpec((keys // block, 1, block, HEAD), fixed),
            pl.BlockSpec((keys, HEAD), all_rows),
            pl.BlockSpec((part, HEAD), by_rows),
            pl.BlockSpec((part, 1), by_rows),
            pl.BlockSpec((part, 1), by_rows),
            pl.BlockSpec((1, keys), all_rows),
            pl.BlockSpec((part, 128), by_rows),
            pl.BlockSpec((part, 128), by_rows),
            pl.BlockSpec((keys, 128), all_rows),
            pl.BlockSpec((keys, 128), all_rows),
        ],
        out_specs=out_specs,
        out_shape=[jax.ShapeDtypeStruct(shape, bf16) for shape in shapes],
        scratch_shapes=[pltpu.VMEM((keys, HEAD), f32), pltpu.VMEM((keys, HEAD), f32)],
        compiler_params=pltpu.CompilerParams(vmem_limit_bytes=VMEM_BYTES),
        cost_estimate=pl.CostEstimate(
            flops=14 * rows * keys * HEAD,
            bytes_accessed=16 * keys * HEAD,
            transcendentals=rows * keys,
        ),
    )(query, key, value, grad, begin, place, key_place, *q_tables, *k_tables)


def body(
    contexts,
    tokens,
    cotangent,
    deal,
    doc_lengths,
    doc_adapter,
    ln1_gain,
    ln1_bias,
    ln2_gain,
    ln2_bias,
    qkv_weight,
    qkv_bias,
    dense_weight,
    dense_bias,
    in_weight,
    in_bias,
    out_weight,
    out_bias,
    qkv_down,
    qkv_up,
    dense_down,
    dense_up,
    in_down,
    in_up,
    out_down,
    out_up,
):
    rows = tokens.shape[1]
    width = tokens.shape[2]
    wa = lax.axis_index("wa")
    ctx = lax.axis_index("ctx")
    total = WA * rows
    own_width = width // WA
    hidden_width = in_weight.shape[1] // WA
    part_cols = ADAPT_COLS // WA
    groups = contexts // PAIRS
    half = own_width // 2
    relative = [wa, wa ^ 1, wa ^ 2, wa ^ 3]
    index = jnp.stack(relative + [ctx % 2, ctx, wa * 0, wa * 0 + 1]).astype(jnp.int32)

    def columns(value, which, size):
        return lax.dynamic_slice_in_dim(value, which * size, size, axis=1)

    def part_rows(value, which, size):
        return lax.dynamic_slice_in_dim(value, which * size, size, axis=0)

    limit = 64
    numbers = jnp.concatenate(
        [doc_lengths // limit, doc_lengths % limit, doc_adapter], axis=1
    ).astype(bf16)
    numbers = jnp.pad(numbers, ((0, 15), (0, 128 - numbers.shape[1])))
    first_pack = pack_small(index, [tokens[0], qkv_down], qkv_up, [0, 1, 2], numbers)

    def gather_rows(weight, size, kinds, *earlier):
        cuts = cut_columns(index, weight, size, kinds, [(2, contexts, 5), (3, contexts, 5)])
        parts = [swap(cuts[0], 2), swap(cuts[1], 3)]
        part = after(jnp.concatenate(parts, axis=1), *earlier)
        return part, lax.all_gather(part, "ctx", axis=0, tiled=True)

    qkv_others_part, qkv_others = gather_rows(qkv_weight, own_width, [2, 1, 0], *first_pack)
    in_cuts = cut_columns(
        index,
        in_weight,
        hidden_width,
        [0],
        [(2, 2, 6), (2, 2, 7), (3, 2, 6), (3, 2, 7)],
        4,
    )
    in_parts = [swap(after(in_cuts[0], qkv_others_part), 2)]
    def hand_on(away, near, *earlier):
        peer = swap(after(away, *earlier), 2)
        return [swap(near, 1), peer, swap(peer, 1)]

    mate_cuts = cut_columns(index, qkv_weight, own_width, [2, 1, 0], [(1, 1, None)])[0]
    in_mate_cut = cut_columns(index, in_weight, hidden_width, [0], [(1, 1, None)], 2)[0]
    first_packs = hand_on(*first_pack)
    grad_pack = jnp.concatenate([cotangent[0], dense_up, out_up], axis=0)
    grad_packs = hand_on(grad_pack, grad_pack, first_packs[1])
    mate_weights = swap(after(mate_cuts, first_packs[0]), 1)
    feed_pack = pack_small(index, [in_down], in_up, [0], numbers)
    feed_packs = hand_on(*feed_pack, grad_packs[1])

    docs_per_pack = doc_lengths.shape[1]
    tables = [numbers] + [item[-16:] for item in first_packs]
    tables = jnp.stack(absolute([item[0] for item in tables], wa)).astype(jnp.int32)
    lengths = tables[:, :docs_per_pack] * limit + tables[:, docs_per_pack : 2 * docs_per_pack]
    adapters = tables[:, 2 * docs_per_pack : 3 * docs_per_pack]
    starts = jnp.cumsum(lengths, axis=1) - lengths

    def places(first, size):
        slots = first + jnp.arange(size, dtype=jnp.int32)
        blocks = slots // BLOCK
        table = jnp.arange(deal.shape[0], dtype=jnp.int32)
        block = jnp.sum(jnp.where(table[None, :] == blocks[:, None], deal[None, :], 0), axis=1)
        return block * BLOCK + slots % BLOCK

    place = places(ctx * rows, rows)
    inside = starts[:, None, :] <= place[None, :, None]
    docs = jnp.sum(inside.astype(jnp.int32), axis=2) - 1
    begin = jnp.max(jnp.where(inside, starts[:, None, :], 0), axis=2)
    offset = (place[None, :] - begin).reshape(total)
    doc_table = jnp.arange(docs_per_pack, dtype=jnp.int32)
    chosen = jnp.sum(
        jnp.where(docs[:, :, None] == doc_table, adapters[:, None, :], 0), axis=2
    ).reshape(total)
    adapter_of = jnp.arange(ADAPT_COLS, dtype=jnp.int32) // RANK
    mask = (adapter_of[None, :] == chosen[:, None]).astype(f32)
    cosine, sine = rotary_tables(offset)

    gains = [item[None, :] for item in (ln1_gain, ln1_bias, ln2_gain, ln2_bias)]
    first_norm, second_norm, first_inner = call(
        front_kernel,
        index,
        [whole(item) for item in [after(tokens[0], in_parts[0], *feed_pack), qkv_down] + first_packs + [mask] + gains],
        [
            ((total, width), bf16, None, None),
            ((total, width), bf16, None, None),
            ((total, ADAPT_COLS), bf16, None, None),
        ],
        flops=2 * total * width * ADAPT_COLS,
    )

    strip = strip_rows = part_cols * HEAD // 128
    ups_row = (tokens.size + qkv_down.size) // 128
    ups_size = 3 * own_width * part_cols // 128

    def project(last, kinds, turned):
        own_block = lambda i, head, ref: (0, ((last - i) * WA + ref[0]) * 2 + head)
        items = [whole(first_norm), (qkv_weight, (own_width, HEAD), own_block)]
        for item, first in ((mate_weights, 0), (qkv_others, 0), (qkv_others, 3)):
            first = (first + 2 - last) * 2
            items.append(
                (
                    item,
                    (own_width, HEAD),
                    lambda i, head, ref, first=first: (0, first + 2 * i + head),
                )
            )
        items.append((qkv_up, (part_cols, HEAD), own_block))
        for r, item in zip((1, 2, 3), first_packs):
            row = (ups_row + (r == 3) * ups_size) // strip + last * 2
            items.append(
                (item, (strip, 128), lambda i, head, ref, row=row: (row - 2 * i + head, 0))
            )
        items += [
            whole(first_inner),
            (qkv_bias[None, :], (1, HEAD), own_block),
            whole(cosine),
            whole(sine),
        ]
        out = call(
            functools.partial(qkv_kernel, turned),
            index,
            items,
            [
                (
                    (WA, 2, kinds, rows, HEAD),
                    bf16,
                    (WA, 1, 1, rows, HEAD),
                    lambda i, head, ref: (0, head, i, 0, 0),
                )
            ],
            grid=(kinds, 2),
            scratch=[pltpu.VMEM((ADAPT_COLS, HEAD), bf16)],
            flops=2 * total * width * own_width * kinds,
        )[0]
        return out.reshape(PAIRS, kinds, rows, HEAD)

    def to_pairs(item):
        if groups == 1:
            return lax.all_to_all(item, "ctx", 0, 0, tiled=True)
        names = [[g * PAIRS + j for j in range(PAIRS)] for g in range(groups)]
        return lax.all_to_all(item, "ctx", 0, 0, axis_index_groups=names, tiled=True)

    grad, dense_inner_grad, out_inner_grad, attended_grad, all_ups = call(
        grad_kernel,
        index,
        [
            whole(item)
            for item in [after(grad_pack, first_inner)] + grad_packs + [mask, dense_weight, dense_down]
        ],
        [
            ((total, width), bf16, None, None),
            ((total, ADAPT_COLS), bf16, None, None),
            ((total, ADAPT_COLS), bf16, None, None),
            ((WA, 2, rows, HEAD), bf16, None, None),
            ((2, ADAPT_COLS, width), bf16, None, None),
        ],
        scratch=[pltpu.VMEM((ADAPT_COLS, width), bf16), pltpu.VMEM((ADAPT_COLS, width), bf16)],
        flops=2 * total * width * (own_width + 2 * ADAPT_COLS),
    )
    attended_grad = to_pairs(attended_grad.reshape(PAIRS, rows, HEAD))
    in_parts.append(swap(after(in_cuts[1], grad_packs[1]), 2))
    qkv_others = after(qkv_others, first_norm, grad)
    value = to_pairs(after(project(2, 1, False), attended_grad))
    in_parts.append(swap(after(in_cuts[2], in_parts[1]), 3))
    pair_own = after(project(1, 2, True), value, in_parts[2])
    pair = to_pairs(pair_own)
    in_parts.append(swap(after(in_cuts[3], in_parts[2]), 3))

    tile = min(512, hidden_width)
    tiles = hidden_width // tile
    in_downs = [whole(in_down)] + [
        (item, (own_width, ADAPT_COLS), lambda *_: (0, 0)) for item in feed_packs
    ]

    in_mate = swap(after(in_mate_cut, pair_own), 1)

    def feed(part, known, norm, *earlier):
        count = tiles
        first = part * count
        own_tile = lambda t, ref: (0, ref[0] * tiles + first + t)
        strip = part_cols * tile // 128
        items = [whole(after(norm, *earlier)), whole(grad)]
        items += [
            (in_weight, (own_width, tile), own_tile),
            (in_mate, (own_width, tile), lambda t, ref: (0, first + t)),
        ]
        items += [
            (item, (own_width // 2, tile), lambda t, ref: (0, first + t)) for item in in_parts
        ]
        items.append((in_up, (part_cols, tile), own_tile))
        for r, item in zip((1, 2, 3), feed_packs):
            row = (own_width + (r == 3) * part_cols * hidden_width // 128) // strip + first
            items.append((item, (strip, 128), lambda t, ref, row=row: (row + t, 0)))
        items += in_downs + [whole(mask)] if known is None else [whole(known)]
        items += [
            (in_bias[None, :], (1, tile), own_tile),
            whole(gains[2]),
            (out_weight, (tile, width), lambda t, ref: (first + t, 0)),
            (out_down, (tile, ADAPT_COLS), lambda t, ref: (first + t, 0)),
            whole(out_inner_grad),
        ]
        size = count * tile
        return call(
            functools.partial(feed_kernel, known is None, True),
            index,
            items,
            [
                ((total, width), f32, None, None),
                ((total, width), f32, None, None),
                ((total, ADAPT_COLS), f32, None, None),
                ((total, ADAPT_COLS), f32, None, None),
                ((size, ADAPT_COLS), bf16, (tile, ADAPT_COLS), lambda t, ref: (t, 0)),
                ((ADAPT_COLS, size), bf16, (ADAPT_COLS, tile), lambda t, ref: (0, t)),
                ((total, ADAPT_COLS), bf16, None, None),
            ],
            grid=(count,),
            scratch=[pltpu.VMEM((ADAPT_COLS, tile), bf16)],
            flops=8 * total * width * size,
        )

    (
        branch_sum,
        norm_grad,
        out_inner,
        second_inner_grad,
        out_down_grad,
        in_up_grad,
        second_inner,
    ) = feed(0, None, second_norm, pair)

    pair_rows = PAIRS * rows
    group = ctx // PAIRS
    own_pack = (ctx % PAIRS) // 2
    own_starts = jnp.sum(
        jnp.where(jnp.arange(WA)[:, None] == own_pack, starts, 0), axis=0
    )
    all_places = places(0, groups * pair_rows)
    all_inside = own_starts[None, :] <= all_places[:, None]
    all_begins = jnp.max(jnp.where(all_inside, own_starts[None, :], 0), axis=1)
    k_tables = rotary_tables(all_places - all_begins)
    if groups == 1:
        q_place, q_begin, q_tables = all_places, all_begins, k_tables
    else:
        q_place = part_rows(all_places, group, pair_rows)
        q_begin = part_rows(all_begins, group, pair_rows)
        q_tables = [part_rows(item, group, pair_rows) for item in k_tables]
    value, attended_grad = [item.reshape(pair_rows, HEAD) for item in (value, attended_grad)]
    key = pair
    sets = [[g * PAIRS + j for g in range(groups)] for j in range(PAIRS)]
    if groups > 1:
        key, value = [
            lax.all_gather(item, "ctx", axis=0, axis_index_groups=sets, tiled=True)
            for item in (pair[:, :1], value)
        ]
    both = attend(
        after(pair, in_parts[3], in_mate, *feed_packs),
        key,
        value,
        attended_grad,
        q_begin[:, None],
        q_place[:, None],
        all_places[None, :],
        q_tables,
        k_tables,
        rows,
    )
    if groups > 1:
        dkv = lax.psum_scatter(
            both[1], "ctx", scatter_dimension=0, axis_index_groups=sets, tiled=True
        )
        both = [jnp.concatenate([both[0], dkv], axis=1)]
    both = to_pairs(both[0]).reshape(WA, 2, 4, rows, HEAD)
    both = after(both, branch_sum)
    odq, dkv = both, both

    def sum_inner(partial):
        partial = (partial + swap(partial, 1)).astype(bf16)
        partial = partial.astype(f32) + swap(partial, 2).astype(f32)
        return (partial * mask).astype(bf16)

    def spread_rows(value):
        return [part_rows(value, wa, part_cols)] + [
            swap(part_rows(value, wa ^ r, part_cols), r) for r in (1, 2, 3)
        ]

    def exchange_sum(value):
        parts = value.reshape(contexts, -1, ADAPT_COLS)
        parts = lax.all_to_all(parts, "ctx", 0, 0, tiled=True)
        return jnp.sum(parts.astype(f32), axis=0).astype(bf16)

    feed_packed = call(
        pack_feed_kernel,
        index,
        [whole(item) for item in [out_down_grad] + spread_rows(in_up_grad)],
        [((2 * hidden_width, ADAPT_COLS), bf16, None, None)],
    )[0]
    feed_sum = exchange_sum(after(feed_packed, both))
    out_inner = sum_inner(out_inner)
    second_inner_grad = sum_inner(second_inner_grad)

    mixed_grads = [odq, dkv]
    up_items = []
    for kind in range(3):
        up_items.append(
            (qkv_up, (part_cols, own_width), lambda _, ref, kind=kind: (0, kind * WA + ref[0]))
        )
        for r, item in zip((1, 2, 3), first_packs):
            row = (ups_row + (r == 3) * ups_size) // (2 * strip_rows) + kind
            up_items.append(
                (item, (2 * strip_rows, 128), lambda _, ref, row=row: (row, 0))
            )
    mixed_inner, qkv_up_grad = call(
        mix_kernel,
        index,
        [whole(item) for item in mixed_grads] + up_items + [whole(first_inner)],
        [
            ((total, ADAPT_COLS), f32, None, None),
            ((ADAPT_COLS, 3 * own_width), bf16, None, None),
        ],
        scratch=[pltpu.VMEM((3, ADAPT_COLS, own_width), bf16)],
        flops=4 * total * ADAPT_COLS * 3 * own_width,
    )
    first_inner_grad = sum_inner(mixed_inner)
    up_parts = spread_rows(qkv_up_grad)
    dense_items = [after(odq, mixed_inner), branch_sum, dense_weight, dense_down, dense_inner_grad]
    reduced = [
        ((2, rows, width), f32, None, None),
        ((2, rows, width), bf16, None, None),
    ]
    keep, send, dense_inner, dense_down_grad = call(
        dense_kernel,
        index,
        [whole(item) for item in dense_items],
        reduced
        + [
            ((total, ADAPT_COLS), f32, None, None),
            ((own_width, ADAPT_COLS), bf16, None, None),
        ],
        scratch=[pltpu.VMEM((total, width), f32)],
        flops=2 * total * width * own_width,
    )
    dense_inner = sum_inner(dense_inner)
    near = swap(send, 1)
    away = swap((keep[1] + near[1].astype(f32)).astype(bf16), 2)
    output = (
        keep[0]
        + near[0].astype(f32)
        + away.astype(f32)
        + product(part_rows(dense_inner, wa, rows), all_ups[0])
        + product(part_rows(out_inner, wa, rows), all_ups[1])
        + dense_bias
        + out_bias
        + tokens[0].astype(f32)
    ).astype(bf16)[None]

    weight_items = []
    for kind in range(3):
        weight_items.append(
            (
                qkv_weight,
                (own_width, own_width),
                lambda _, ref, kind=kind: (0, kind * WA + ref[0]),
            )
        )
        for item, first in ((mate_weights, 2), (qkv_others, 2), (qkv_others, 5)):
            weight_items.append(
                (item, (own_width, own_width), lambda _, ref, at=first - kind: (0, at))
            )
    keep, send = call(
        norm_grad_kernel,
        index,
        [whole(item) for item in mixed_grads]
        + weight_items
        + [whole(item) for item in [after(gains[0], keep), norm_grad]],
        reduced,
        scratch=[pltpu.VMEM((total, width), f32)],
        flops=2 * total * width * 3 * own_width,
    )
    near = swap(send, 1)
    combined = (keep[1] + near[1].astype(f32)).astype(bf16)
    away = swap(combined, 2)
    down_at = rows * width // 128 // own_width
    down_block = lambda *_: (down_at, 0)
    tokens_grad = call(
        finish_kernel,
        index,
        [
            whole(item)
            for item in [
                keep,
                near,
                away,
                part_rows(first_inner_grad, wa, rows),
                part_rows(second_inner_grad, wa, rows),
            ]
        ]
        + [whole(qkv_down)]
        + [(item, (own_width, ADAPT_COLS), down_block) for item in first_packs]
        + in_downs
        + [whole(item) for item in [gains[0], gains[2], tokens[0], cotangent[0]]],
        [((rows, width), f32, None, None)],
        scratch=[pltpu.VMEM((rows, width), f32)],
    )[0][None]

    own_norm = lambda _, ref: (0, ref[0])
    items = [
        (first_norm, (total, own_width), own_norm),
        whole(first_inner_grad),
    ]
    items += [(second_norm, (total, own_width), own_norm), whole(second_inner_grad)]
    items += [whole(item) for item in [dense_inner, out_inner, grad, dense_down_grad] + up_parts]
    packed = call(
        pack_grads_kernel,
        index,
        items,
        [((8 * own_width, ADAPT_COLS), bf16, None, None)],
        scratch=[pltpu.VMEM((ADAPT_COLS, width), f32)],
    )[0]
    packed = exchange_sum(after(packed, feed_sum))
    packed = jnp.stack([feed_sum, packed])
    packed = lax.all_gather(packed, "ctx", axis=0)
    packed = after(packed, tokens_grad, output)
    block = (contexts, 1) + packed.shape[2:]
    out_down_grad, in_up_grad = call(
        unpack_feed_kernel,
        index,
        [(packed, block, lambda *_: (0, 0, 0, 0))],
        [
            ((hidden_width, ADAPT_COLS), f32, None, None),
            ((part_cols, WA * hidden_width), f32, None, None),
        ],
    )
    down_shape = ((own_width, ADAPT_COLS), f32, None, None)
    up_shape = ((part_cols, width), f32, None, None)
    (
        qkv_down_grad,
        in_down_grad,
        dense_down_grad,
        dense_up_grad,
        out_up_grad,
        qkv_up_grad,
    ) = call(
        unpack_grads_kernel,
        index,
        [(packed, block, lambda *_: (0, 1, 0, 0))],
        [down_shape] * 3 + [up_shape] * 2 + [((part_cols, 3 * width), f32, None, None)],
    )
    return (
        output,
        tokens_grad,
        qkv_down_grad,
        qkv_up_grad,
        dense_down_grad,
        dense_up_grad,
        in_down_grad,
        in_up_grad,
        out_down_grad,
        out_up_grad,
    )


def solution(mesh):
    rows = P("wa", "ctx", None)
    shard = P("wa", None)
    in_specs = (
        (rows, rows, P(), shard, shard)
        + (P(),) * 4
        + (shard, P()) * 4
        + (shard,) * 8
    )
    out_specs = (rows, rows) + (shard,) * 8
    return jax.shard_map(
        functools.partial(body, mesh.shape["ctx"]),
        mesh=mesh,
        in_specs=in_specs,
        out_specs=out_specs,
        check_vma=False,
    )
```

```python
import functools
import math

import jax
import jax.numpy as jnp
from jax import lax
from jax.experimental import pallas as pl
from jax.experimental.pallas import tpu as pltpu
from jax.sharding import PartitionSpec as P

HEADS = 8
HEAD = 256
ROT = 64
RANK = 16
BLOCK = 64
ADAPT_COLS = 128
WA = 4
PAIRS = 8
VMEM_BYTES = 58 * 1024 * 1024

epsilon = 1e-05
masked_score = -1e30
f32 = jnp.float32
bf16 = jnp.bfloat16


def product(left, right):
    return jnp.dot(left, right, preferred_element_type=f32)


def times_t(left, right):
    return lax.dot_general(left, right, (((1,), (1,)), ((), ())), preferred_element_type=f32)


def t_times(left, right):
    return lax.dot_general(left, right, (((0,), (0,)), ((), ())), preferred_element_type=f32)


def swap(value, bits):
    return lax.ppermute(value, "wa", [(i, i ^ bits) for i in range(WA)])


def after(value, *earlier):
    return lax.optimization_barrier((value, *earlier))[0]


def absolute(pieces, wa):
    low = wa % 2 == 1
    high = wa >= 2
    p = [
        jnp.where(low, pieces[1], pieces[0]),
        jnp.where(low, pieces[0], pieces[1]),
        jnp.where(low, pieces[3], pieces[2]),
        jnp.where(low, pieces[2], pieces[3]),
    ]
    return [
        jnp.where(high, p[2], p[0]),
        jnp.where(high, p[3], p[1]),
        jnp.where(high, p[0], p[2]),
        jnp.where(high, p[1], p[3]),
    ]


def rotary_tables(offset):
    half = ROT // 2
    lane = jnp.arange(128, dtype=jnp.int32)
    freq = 10000.0 ** (-2.0 * (lane % half).astype(f32) / ROT)
    freq = jnp.where(lane < ROT, freq, 0.0)
    angle = offset.astype(f32)[:, None] * freq[None, :]
    sign = jnp.where(lane < half, -1.0, 1.0)
    return jnp.cos(angle), jnp.sin(angle) * sign[None, :]


def turn_first(values, cosine, sine):
    lane = lax.broadcasted_iota(jnp.int32, values.shape, 1)
    partner = jnp.where(
        lane < ROT // 2, pltpu.roll(values, 128 - ROT // 2, 1), pltpu.roll(values, ROT // 2, 1)
    )
    return values * cosine + partner * sine


def call(kernel, index, inputs, outputs, grid=(1,), scratch=(), flops=0, name=None):
    def spec(shape, block, where):
        if where is None:
            zeros = (0,) * len(shape)
            return pl.BlockSpec(shape, lambda *_: zeros)
        return pl.BlockSpec(block, where)

    size = sum(a.size * a.dtype.itemsize if w is None else math.prod(i or 1 for i in b) * 2 * math.prod(grid)
               for a, b, w in inputs)
    return pl.pallas_call(
        kernel,
        grid_spec=pltpu.PrefetchScalarGridSpec(
            num_scalar_prefetch=1,
            grid=grid,
            in_specs=[spec(a.shape, b, w) for a, b, w in inputs],
            out_specs=[spec(s, b, w) for s, _, b, w in outputs],
            scratch_shapes=list(scratch),
        ),
        out_shape=[jax.ShapeDtypeStruct(s, d) for s, d, _, _ in outputs],
        compiler_params=pltpu.CompilerParams(vmem_limit_bytes=VMEM_BYTES),
        cost_estimate=pl.CostEstimate(flops=flops, bytes_accessed=size, transcendentals=0),
    )(index, *[a for a, _, _ in inputs])


def whole(array):
    return (array, None, None)


def copy_kernel(index_ref, *refs):
    count = len(refs) // 2
    for source, target in zip(refs[:count], refs[count:]):
        target[...] = source[...].reshape(target.shape)


def cut_columns(index, weight, size, kinds, cuts, parts=1):
    rows = weight.shape[0]
    part = size // parts
    inputs, outputs = [], []
    for r, division, number in cuts:
        height = rows // division

        def where(slot, t, ref, r=r, number=number):
            kind = sum(kind * (slot == i) for i, kind in enumerate(kinds))
            return (0 if number is None else ref[number], (kind * WA + ref[r]) * parts + t)

        inputs.append((weight, (height, part), where))
        outputs.append(
            (
                (height, len(kinds) * size),
                weight.dtype,
                (height, part),
                lambda slot, t, ref: (0, slot * parts + t),
            )
        )
    return call(copy_kernel, index, inputs, outputs, grid=(len(kinds), parts))


def strips(value):
    return [value[:, i : i + 128] for i in range(0, value.shape[1], 128)]


def store_strips(target, first, value):
    for item in strips(value):
        target[first : first + item.shape[0], :] = item
        first += item.shape[0]
    return first


def pack_kernel(index_ref, *refs):
    plain, last_ref = refs[:-6], refs[-6]
    (ups_mate, ups_peer, ups_far), (away_ref, near_ref) = refs[-5:-2], refs[-2:]
    first = 0
    for ref in plain:
        store_strips(away_ref, first, ref)
        first = store_strips(near_ref, first, ref)
    blank = ups_peer.shape[0] * ups_peer.shape[1] // 128
    store_strips(near_ref, first, ups_mate)
    store_strips(near_ref, first + blank, ups_mate)
    store_strips(away_ref, first, ups_peer)
    store_strips(away_ref, first + blank, ups_far)
    store_strips(near_ref, first + 2 * blank, last_ref)
    store_strips(away_ref, first + 2 * blank, last_ref)


def pack_small(index, plain, up, kinds, last):
    block = up.shape[1] // len(kinds) // WA
    items = [whole(item) for item in plain + [last]]
    size = sum(item.size for item in plain) // 128
    ups = up.shape[0] * block * len(kinds) // 128
    cut = jnp.concatenate if len(kinds) > 1 else (lambda v, axis: v[0])
    for r in (1, 2, 3):
        items.append(
            whole(
                cut(
                    [
                        lax.dynamic_slice_in_dim(up, (kind * WA + index[r]) * block, block, axis=1)
                        for kind in kinds
                    ],
                    axis=1,
                )
            )
        )
    shape = (size + 2 * ups + last.shape[0], 128)
    return call(pack_kernel, index, items, [(shape, bf16, None, None)] * 2)


def front_kernel(index_ref, *refs):
    token_ref, down_ref = refs[:2]
    packs = refs[2:5]
    mask_ref, g1, b1, g2, b2, first_ref, second_ref, inner_ref = refs[5:]
    rows, width = token_ref.shape
    wide = down_ref.shape[0]
    step = 32
    for r in range(WA):
        base = pl.multiple_of(index_ref[r] * rows, rows)
        for start in range(0, rows, step):
            if r == 0:
                values = token_ref[start : start + step, :]
            else:
                values = jnp.concatenate(
                    [
                        packs[r - 1][i * rows + start : i * rows + start + step, :]
                        for i in range(width // 128)
                    ],
                    axis=1,
                )
            values = values.astype(f32)
            centered = values - jnp.mean(values, axis=1, keepdims=True)
            spread = jnp.mean(centered * centered, axis=1, keepdims=True)
            normal = centered * lax.rsqrt(spread + epsilon)
            first_ref[pl.ds(base + start, step), :] = (normal * g1[...] + b1[...]).astype(bf16)
            second_ref[pl.ds(base + start, step), :] = (normal * g2[...] + b2[...]).astype(bf16)
    total = 0.0
    first = rows * width // 128
    for r in range(WA):
        columns = pl.ds(pl.multiple_of(index_ref[r] * wide, wide), wide)
        down = down_ref[...] if r == 0 else packs[r - 1][first : first + wide, :]
        total += product(first_ref[:, columns], down)
    inner_ref[...] = (total * mask_ref[...]).astype(bf16)


def pieces_of(index_ref, refs):
    wide = refs[0].shape[0]
    pieces = []
    for r, ref in enumerate(refs):
        size = ref.shape[0]
        first = index_ref[r] * wide
        if len(refs) > WA and r >= 2:
            first = index_ref[2 + (r - 2) // 2] * wide + (r % 2) * size
        pieces.append((pl.ds(pl.multiple_of(first, size), size), ref))
    return pieces


def read(ref):
    return ref[...].reshape(ref.shape[-2:])


def join_ups(index_ref, ups, joined):
    size = ADAPT_COLS // WA
    for r, ref in enumerate(ups):
        first = pl.multiple_of(index_ref[r] * size, size)
        if ref.shape[-1] == joined.shape[-1]:
            joined[pl.ds(first, size), :] = read(ref)
        else:
            for i in range(joined.shape[-1] // 128):
                joined[pl.ds(first, size), i * 128 : (i + 1) * 128] = ref[
                    i * size : (i + 1) * size, :
                ]


def qkv_kernel(turned, index_ref, hidden_ref, *refs):
    weights, ups = refs[:4], refs[4:8]
    inner_ref, bias_ref, cos_ref, sin_ref, out_ref, joined = refs[8:]
    join_ups(index_ref, ups, joined)
    total = product(inner_ref[...], joined[...]) + bias_ref[...]
    for columns, ref in pieces_of(index_ref, weights):
        total += product(hidden_ref[:, columns], read(ref))
    shape = out_ref.shape
    if turned:
        first = turn_first(total[:, :128], cos_ref[...], sin_ref[...])
        out_ref[..., :128] = first.astype(bf16).reshape(shape[:-1] + (128,))
        out_ref[..., 128:] = total[:, 128:].astype(bf16).reshape(shape[:-1] + (HEAD - 128,))
    else:
        out_ref[...] = total.astype(bf16).reshape(shape)


def grad_kernel(index_ref, *refs):
    parts = refs[:WA]
    mask_ref, weight_ref, down_ref = refs[WA : WA + 3]
    grad_ref, dense_ref, out_ref, heads_ref, ups_ref, dense_joined, out_joined = refs[WA + 3 :]
    size = ADAPT_COLS // WA
    rows = parts[0].shape[0] - 2 * size
    for r in range(WA):
        first = pl.ds(pl.multiple_of(index_ref[r] * size, size), size)
        dense_joined[first, :] = parts[r][rows : rows + size, :]
        out_joined[first, :] = parts[r][rows + size :, :]
        grad_ref[pl.ds(pl.multiple_of(index_ref[r] * rows, rows), rows), :] = parts[r][:rows, :]
    ups_ref[0] = dense_joined[...]
    ups_ref[1] = out_joined[...]
    grad = grad_ref[...]
    dense = (times_t(grad, dense_joined[...]) * mask_ref[...]).astype(bf16)
    dense_ref[...] = dense
    out_ref[...] = (times_t(grad, out_joined[...]) * mask_ref[...]).astype(bf16)
    for head in range(2):
        span = slice(head * HEAD, (head + 1) * HEAD)
        total = times_t(grad, weight_ref[span, :]) + times_t(dense, down_ref[span, :])
        heads_ref[:, head] = total.astype(bf16).reshape(WA, rows, HEAD)


def gelu_parts(values):
    bell = jnp.exp(-0.5 * values * values)
    t = 1.0 / (1.0 + (0.3275911 * math.sqrt(0.5)) * jnp.abs(values))
    series = 1.061405429 * 0.5
    for factor in (-1.453152027, 1.421413741, -0.284496736, 0.254829592):
        series = series * t + 0.5 * factor
    tail = series * t * bell
    below = jnp.where(values > 0, 1.0 - tail, tail)
    return values * below, below + values * bell * (1.0 / math.sqrt(2.0 * math.pi))


def feed_kernel(starts, ends, index_ref, hidden_ref, grad_ref, *refs):
    weights, ups, refs = refs[:6], refs[6:10], refs[10:]
    if starts:
        downs, mask_ref, refs = refs[:4], refs[4], refs[5:]
    else:
        known_ref, refs = refs[0], refs[1:]
    bias_ref, gain_ref, out_w_ref, out_down_ref, out_inner_grad_ref = refs[:5]
    (
        out_ref,
        norm_grad_ref,
        out_inner_ref,
        inner_grad_ref,
        out_down_grad_ref,
        in_up_grad_ref,
        inner_ref,
        joined,
    ) = refs[5:]
    step = pl.program_id(0)

    @pl.when(step == 0)
    def _():
        if starts:
            wide = downs[0].shape[0]
            total = 0.0
            for r in range(WA):
                columns = pl.ds(pl.multiple_of(index_ref[r] * wide, wide), wide)
                total += product(hidden_ref[:, columns], downs[r][...])
            inner_ref[...] = (total * mask_ref[...]).astype(bf16)
        else:
            inner_ref[...] = known_ref[...]
        out_ref[...] = jnp.zeros_like(out_ref)
        norm_grad_ref[...] = jnp.zeros_like(norm_grad_ref)
        out_inner_ref[...] = jnp.zeros_like(out_inner_ref)
        inner_grad_ref[...] = jnp.zeros_like(inner_grad_ref)

    join_ups(index_ref, ups, joined)
    pre = product(inner_ref[...], joined[...]) + bias_ref[...]
    for columns, ref in pieces_of(index_ref, weights):
        pre += product(hidden_ref[:, columns], read(ref))
    units, slope = gelu_parts(pre)
    units = units.astype(bf16)
    pre_grad = times_t(grad_ref[...], out_w_ref[...]) + times_t(
        out_inner_grad_ref[...], out_down_ref[...]
    )
    pre_grad = (pre_grad * slope).astype(bf16)
    out_ref[...] += product(units, out_w_ref[...])
    for columns, ref in pieces_of(index_ref, weights):
        norm_grad_ref[:, columns] += times_t(pre_grad, read(ref))
    out_inner_ref[...] += product(units, out_down_ref[...])
    inner_grad_ref[...] += times_t(pre_grad, joined[...])
    out_down_grad_ref[...] = t_times(units, out_inner_grad_ref[...]).astype(bf16)
    in_up_grad_ref[...] = t_times(inner_ref[...], pre_grad).astype(bf16)

    @pl.when(step == pl.num_programs(0) - 1)
    def _():
        norm_grad_ref[...] = norm_grad_ref[...] * gain_ref[...]


def scatter_rows(index_ref, total_ref, keep_ref, send_ref):
    rows = keep_ref.shape[1]
    for r, (ref, slot) in enumerate(((keep_ref, 0), (send_ref, 0), (keep_ref, 1), (send_ref, 1))):
        part = total_ref[pl.ds(pl.multiple_of(index_ref[r] * rows, rows), rows), :]
        ref[slot] = part.astype(ref.dtype)


def head_rows(ref, head):
    return ref[:, head, 0].reshape(-1, HEAD)


def dense_kernel(
    index_ref,
    heads_ref,
    sum_ref,
    weight_ref,
    down_ref,
    inner_grad_ref,
    keep_ref,
    send_ref,
    inner_ref,
    down_grad_ref,
    total,
):
    result = sum_ref[...]
    inner = 0.0
    for head in range(2):
        span = slice(head * HEAD, (head + 1) * HEAD)
        heads = head_rows(heads_ref, head)
        result += product(heads, weight_ref[span, :])
        inner += product(heads, down_ref[span, :])
        down_grad_ref[span, :] = t_times(heads, inner_grad_ref[...]).astype(bf16)
    inner_ref[...] = inner
    total[...] = result
    scatter_rows(index_ref, total, keep_ref, send_ref)


def mixed_rows(query_grad_ref, key_grad_ref, kind, head):
    if kind == 0:
        return query_grad_ref[:, head, 1].reshape(-1, HEAD)
    return key_grad_ref[:, head, kind + 1].reshape(-1, HEAD)


def mix_kernel(index_ref, *refs):
    grads, ups = refs[:2], refs[2 : 2 + 3 * WA]
    inner_ref, inner_grad_ref, up_grad_ref, joined = refs[2 + 3 * WA :]
    width = 2 * HEAD
    for kind in range(3):
        for r in range(WA):
            size = ADAPT_COLS // WA
            first = pl.multiple_of(index_ref[r] * size, size)
            ref = ups[kind * WA + r]
            if r == 0:
                joined[kind, pl.ds(first, size), :] = ref[...]
            else:
                for i in range(width // 128):
                    joined[kind, pl.ds(first, size), i * 128 : (i + 1) * 128] = ref[
                        i * size : (i + 1) * size, :
                    ]
    total = 0.0
    for kind in range(3):
        for head in range(2):
            span = slice(head * HEAD, (head + 1) * HEAD)
            rows = mixed_rows(*grads, kind, head)
            total += times_t(rows, joined[kind, :, span])
            out = slice(kind * width + head * HEAD, kind * width + (head + 1) * HEAD)
            up_grad_ref[:, out] = t_times(inner_ref[...], rows).astype(bf16)
    inner_grad_ref[...] = total


def norm_grad_kernel(index_ref, *refs):
    grads, weights = refs[:2], refs[2:14]
    gain_ref, sum_ref, keep_ref, send_ref, total = refs[14:]
    sets = [pieces_of(index_ref, weights[WA * kind : WA * kind + WA]) for kind in range(3)]
    rows = [[mixed_rows(*grads, kind, head) for head in range(2)] for kind in range(3)]
    for piece in range(WA):
        columns = sets[0][piece][0]
        part = 0.0
        for kind in range(3):
            weight = read(sets[kind][piece][1])
            for head in range(2):
                part += times_t(rows[kind][head], weight[:, head * HEAD : (head + 1) * HEAD])
        total[:, columns] = part * gain_ref[:, columns] + sum_ref[:, columns]
    scatter_rows(index_ref, total, keep_ref, send_ref)


def own_rows_of(inner, grad, index_ref, total):
    size = ADAPT_COLS // WA
    total[...] = t_times(inner, grad)
    return total[pl.ds(pl.multiple_of(index_ref[0] * size, size), size), :].astype(bf16)


def pack_grads_kernel(index_ref, *refs):
    down_ref, norm_ref, norm_grad_ref, inner_ref, grad_ref = refs[:5]
    ups, (packed_ref, total) = refs[5:9], refs[9:]
    at = down_ref.shape[0]
    packed_ref[:at, :] = down_ref[...]
    part = t_times(norm_ref[...], norm_grad_ref[...]).astype(bf16)
    packed_ref[at : at + part.shape[0], :] = part
    at += part.shape[0]
    at = store_strips(packed_ref, at, own_rows_of(inner_ref[...], grad_ref[...], index_ref, total))
    for ref in ups:
        at = store_strips(packed_ref, at, ref)


def unpack_grads_kernel(feed_size, index_ref, source_ref, *refs):
    packed = source_ref[...]
    size = ADAPT_COLS // WA
    for outs, start, end in ((refs[:4], 0, feed_size), (refs[4:], feed_size, packed.shape[1])):
        part = packed[:, start:end].reshape(-1, ADAPT_COLS)
        down_ref, norm_ref, inner_ref, up_ref = outs
        at = 0
        for ref in (down_ref, norm_ref):
            ref[...] = part[at : at + ref.shape[0], :].astype(f32)
            at += ref.shape[0]
        for i in range(inner_ref.shape[1] // 128):
            inner_ref[:, i * 128 : (i + 1) * 128] = part[at : at + size, :].astype(f32)
            at += size
        kinds = 3 if start else 1
        width = up_ref.shape[1] // kinds
        block = width // WA
        for r in range(WA):
            for kind in range(kinds):
                for i in range(block // 128):
                    first = kind * width + index_ref[r] * block + i * 128
                    columns = pl.ds(pl.multiple_of(first, 128), 128)
                    up_ref[:, columns] = part[at : at + size, :].astype(f32)
                    at += size


def finish_kernel(index_ref, *refs):
    keep_ref, near_ref, away_ref, first_ref, second_ref = refs[:5]
    first_downs, second_downs = refs[5:9], refs[9:13]
    g1, g2, token_ref, grad_ref, out_ref, total = refs[13:]
    total[...] = keep_ref[0] + near_ref[0].astype(f32) + away_ref[...].astype(f32)
    wide = first_downs[0].shape[0]
    for r in range(WA):
        columns = pl.ds(pl.multiple_of(index_ref[r] * wide, wide), wide)
        total[:, columns] += (
            times_t(first_ref[...], first_downs[r][...]) * g1[:, columns]
            + times_t(second_ref[...], second_downs[r][...]) * g2[:, columns]
        )
    step = 32
    for start in range(0, total.shape[0], step):
        span = slice(start, start + step)
        values = token_ref[span, :].astype(f32)
        centered = values - jnp.mean(values, axis=1, keepdims=True)
        rstd = lax.rsqrt(jnp.mean(centered * centered, axis=1, keepdims=True) + epsilon)
        normal = centered * rstd
        part = total[span, :]
        part = (
            part
            - jnp.mean(part, axis=1, keepdims=True)
            - normal * jnp.mean(part * normal, axis=1, keepdims=True)
        )
        out_ref[span, :] = grad_ref[span, :].astype(f32) + rstd * part


def attention_kernel(
    joint,
    query_ref,
    key_ref,
    value_ref,
    grad_ref,
    begin_ref,
    place_ref,
    key_place_ref,
    q_cos_ref,
    q_sin_ref,
    k_cos_ref,
    k_sin_ref,
    rows_ref,
    *refs,
):
    keys_ref, dk_sum, dv_sum = (rows_ref, *refs) if joint else refs
    step = pl.program_id(0)
    scale = 1.0 / math.sqrt(HEAD)

    @pl.when(step == 0)
    def _():
        dk_sum[...] = jnp.zeros_like(dk_sum)
        dv_sum[...] = jnp.zeros_like(dv_sum)

    query = query_ref[...].reshape(-1, HEAD)
    key = key_ref[...].reshape(-1, HEAD)
    value = value_ref[...]
    grad = grad_ref[...]
    key_place = key_place_ref[...]
    allowed = (key_place >= begin_ref[...]) & (key_place <= place_ref[...])
    scores = jnp.where(allowed, times_t(query, key) * scale, masked_score)
    top = jnp.max(scores, axis=1, keepdims=True)
    weights = jnp.exp(scores - top)
    prob = weights * (1.0 / jnp.sum(weights, axis=1, keepdims=True))
    prob_low = prob.astype(bf16)
    part, block = query.shape[0], rows_ref.shape[2]
    shape = (part // block, block)
    own = pl.ds(step * shape[0], shape[0]) if joint else slice(None)
    rows_ref[own, 0] = product(prob_low, value).astype(bf16).reshape(shape + (HEAD,))
    prob_grad = times_t(grad, value)
    delta = jnp.sum(prob * prob_grad, axis=1, keepdims=True)
    score_grad = (prob * (prob_grad - delta)).astype(bf16)
    dq = product(score_grad, key) * scale
    first = turn_first(dq[:, :128], q_cos_ref[...], -q_sin_ref[...])
    rows_ref[own, 1, :, :128] = first.astype(bf16).reshape(shape + (128,))
    rows_ref[own, 1, :, 128:] = dq[:, 128:].astype(bf16).reshape(shape + (HEAD - 128,))
    dk_sum[...] += t_times(score_grad, query)
    dv_sum[...] += t_times(prob_low, grad)

    @pl.when(step == pl.num_programs(0) - 1)
    def _():
        base = 2 if joint else 0
        shape = keys_ref.shape[:1] + keys_ref.shape[2:3]
        dk = dk_sum[...] * scale
        first = turn_first(dk[:, :128], k_cos_ref[...], -k_sin_ref[...])
        keys_ref[:, base, :, :128] = first.astype(bf16).reshape(shape + (128,))
        keys_ref[:, base, :, 128:] = dk[:, 128:].astype(bf16).reshape(shape + (HEAD - 128,))
        keys_ref[:, base + 1] = dv_sum[...].astype(bf16).reshape(shape + (HEAD,))


def attend(query, key, value, grad, begin, place, key_place, q_tables, k_tables, block):
    rows = query.shape[0] * block
    keys = key.shape[0] * block
    part = min(256, rows)
    joint = rows == keys
    by_rows = lambda i: (i, 0)
    all_rows = lambda i: (0, 0)
    fixed = lambda i: (0, 0, 0, 0)
    if joint:
        shapes = [(keys // block, 4, block, HEAD)]
        out_specs = [pl.BlockSpec(shapes[0], fixed)]
    else:
        shapes = [(rows // block, 2, block, HEAD), (keys // block, 2, block, HEAD)]
        out_specs = [
            pl.BlockSpec((part // block, 2, block, HEAD), lambda i: (i, 0, 0, 0)),
            pl.BlockSpec(shapes[1], fixed),
        ]
    return pl.pallas_call(
        functools.partial(attention_kernel, joint),
        grid=(rows // part,),
        in_specs=[
            pl.BlockSpec((part // block, 1, block, HEAD), lambda i: (i, 1, 0, 0)),
            pl.BlockSpec((keys // block, 1, block, HEAD), fixed),
            pl.BlockSpec((keys, HEAD), all_rows),
            pl.BlockSpec((part, HEAD), by_rows),
            pl.BlockSpec((part, 1), by_rows),
            pl.BlockSpec((part, 1), by_rows),
            pl.BlockSpec((1, keys), all_rows),
            pl.BlockSpec((part, 128), by_rows),
            pl.BlockSpec((part, 128), by_rows),
            pl.BlockSpec((keys, 128), all_rows),
            pl.BlockSpec((keys, 128), all_rows),
        ],
        out_specs=out_specs,
        out_shape=[jax.ShapeDtypeStruct(shape, bf16) for shape in shapes],
        scratch_shapes=[pltpu.VMEM((keys, HEAD), f32), pltpu.VMEM((keys, HEAD), f32)],
        compiler_params=pltpu.CompilerParams(vmem_limit_bytes=VMEM_BYTES),
        cost_estimate=pl.CostEstimate(
            flops=14 * rows * keys * HEAD,
            bytes_accessed=16 * keys * HEAD,
            transcendentals=rows * keys,
        ),
    )(query, key, value, grad, begin, place, key_place, *q_tables, *k_tables)


def body(
    contexts,
    tokens,
    cotangent,
    deal,
    doc_lengths,
    doc_adapter,
    ln1_gain,
    ln1_bias,
    ln2_gain,
    ln2_bias,
    qkv_weight,
    qkv_bias,
    dense_weight,
    dense_bias,
    in_weight,
    in_bias,
    out_weight,
    out_bias,
    qkv_down,
    qkv_up,
    dense_down,
    dense_up,
    in_down,
    in_up,
    out_down,
    out_up,
):
    rows = tokens.shape[1]
    width = tokens.shape[2]
    wa = lax.axis_index("wa")
    ctx = lax.axis_index("ctx")
    total = WA * rows
    own_width = width // WA
    hidden_width = in_weight.shape[1] // WA
    part_cols = ADAPT_COLS // WA
    groups = contexts // PAIRS
    half = own_width // 2
    relative = [wa, wa ^ 1, wa ^ 2, wa ^ 3]
    index = jnp.stack(relative + [ctx % 2, ctx, wa * 0, wa * 0 + 1]).astype(jnp.int32)

    def columns(value, which, size):
        return lax.dynamic_slice_in_dim(value, which * size, size, axis=1)

    def part_rows(value, which, size):
        return lax.dynamic_slice_in_dim(value, which * size, size, axis=0)

    limit = 64
    numbers = jnp.concatenate(
        [doc_lengths // limit, doc_lengths % limit, doc_adapter], axis=1
    ).astype(bf16)
    numbers = jnp.pad(numbers, ((0, 15), (0, 128 - numbers.shape[1])))
    first_pack = pack_small(index, [tokens[0], qkv_down], qkv_up, [0, 1, 2], numbers)

    def gather_rows(weight, size, kinds, *earlier):
        cuts = cut_columns(index, weight, size, kinds, [(2, contexts, 5), (3, contexts, 5)])
        parts = [swap(cuts[0], 2), swap(cuts[1], 3)]
        part = after(jnp.concatenate(parts, axis=1), *earlier)
        return part, lax.all_gather(part, "ctx", axis=0, tiled=True)

    qkv_others_part, qkv_others = gather_rows(qkv_weight, own_width, [2, 1, 0], *first_pack)
    in_cuts = cut_columns(
        index,
        in_weight,
        hidden_width,
        [0],
        [(2, 2, 6), (2, 2, 7), (3, 2, 6), (3, 2, 7)],
        4,
    )
    in_parts = [swap(after(in_cuts[0], qkv_others_part), 2)]
    def hand_on(away, near, *earlier):
        peer = swap(after(away, *earlier), 2)
        return [swap(near, 1), peer, swap(peer, 1)]

    mate_cuts = cut_columns(index, qkv_weight, own_width, [2, 1, 0], [(1, 1, None)])[0]
    in_mate_cut = cut_columns(index, in_weight, hidden_width, [0], [(1, 1, None)], 2)[0]
    first_packs = hand_on(*first_pack)
    grad_pack = jnp.concatenate([cotangent[0], dense_up, out_up], axis=0)
    grad_packs = hand_on(grad_pack, grad_pack, first_packs[1])
    mate_weights = swap(after(mate_cuts, first_packs[0]), 1)
    feed_pack = pack_small(index, [in_down], in_up, [0], numbers)
    feed_packs = hand_on(*feed_pack, grad_packs[1])

    docs_per_pack = doc_lengths.shape[1]
    tables = [numbers] + [item[-16:] for item in first_packs]
    tables = jnp.stack(absolute([item[0] for item in tables], wa)).astype(jnp.int32)
    lengths = tables[:, :docs_per_pack] * limit + tables[:, docs_per_pack : 2 * docs_per_pack]
    adapters = tables[:, 2 * docs_per_pack : 3 * docs_per_pack]
    starts = jnp.cumsum(lengths, axis=1) - lengths

    def places(first, size):
        slots = first + jnp.arange(size, dtype=jnp.int32)
        blocks = slots // BLOCK
        table = jnp.arange(deal.shape[0], dtype=jnp.int32)
        block = jnp.sum(jnp.where(table[None, :] == blocks[:, None], deal[None, :], 0), axis=1)
        return block * BLOCK + slots % BLOCK

    place = places(ctx * rows, rows)
    inside = starts[:, None, :] <= place[None, :, None]
    docs = jnp.sum(inside.astype(jnp.int32), axis=2) - 1
    begin = jnp.max(jnp.where(inside, starts[:, None, :], 0), axis=2)
    offset = (place[None, :] - begin).reshape(total)
    doc_table = jnp.arange(docs_per_pack, dtype=jnp.int32)
    chosen = jnp.sum(
        jnp.where(docs[:, :, None] == doc_table, adapters[:, None, :], 0), axis=2
    ).reshape(total)
    adapter_of = jnp.arange(ADAPT_COLS, dtype=jnp.int32) // RANK
    mask = (adapter_of[None, :] == chosen[:, None]).astype(f32)
    cosine, sine = rotary_tables(offset)

    gains = [item[None, :] for item in (ln1_gain, ln1_bias, ln2_gain, ln2_bias)]
    first_norm, second_norm, first_inner = call(
        front_kernel,
        index,
        [whole(item) for item in [after(tokens[0], in_parts[0], *feed_pack), qkv_down] + first_packs + [mask] + gains],
        [
            ((total, width), bf16, None, None),
            ((total, width), bf16, None, None),
            ((total, ADAPT_COLS), bf16, None, None),
        ],
        flops=2 * total * width * ADAPT_COLS,
    )

    strip = strip_rows = part_cols * HEAD // 128
    ups_row = (tokens.size + qkv_down.size) // 128
    ups_size = 3 * own_width * part_cols // 128

    def project(last, kinds, turned):
        own_block = lambda i, head, ref: (0, ((last - i) * WA + ref[0]) * 2 + head)
        items = [whole(first_norm), (qkv_weight, (own_width, HEAD), own_block)]
        for item, first in ((mate_weights, 0), (qkv_others, 0), (qkv_others, 3)):
            first = (first + 2 - last) * 2
            items.append(
                (
                    item,
                    (own_width, HEAD),
                    lambda i, head, ref, first=first: (0, first + 2 * i + head),
                )
            )
        items.append((qkv_up, (part_cols, HEAD), own_block))
        for r, item in zip((1, 2, 3), first_packs):
            row = (ups_row + (r == 3) * ups_size) // strip + last * 2
            items.append(
                (item, (strip, 128), lambda i, head, ref, row=row: (row - 2 * i + head, 0))
            )
        items += [
            whole(first_inner),
            (qkv_bias[None, :], (1, HEAD), own_block),
            whole(cosine),
            whole(sine),
        ]
        out = call(
            functools.partial(qkv_kernel, turned),
            index,
            items,
            [
                (
                    (WA, 2, kinds, rows, HEAD),
                    bf16,
                    (WA, 1, 1, rows, HEAD),
                    lambda i, head, ref: (0, head, i, 0, 0),
                )
            ],
            grid=(kinds, 2),
            scratch=[pltpu.VMEM((ADAPT_COLS, HEAD), bf16)],
            flops=2 * total * width * own_width * kinds,
        )[0]
        return out.reshape(PAIRS, kinds, rows, HEAD)

    def to_pairs(item):
        if groups == 1:
            return lax.all_to_all(item, "ctx", 0, 0, tiled=True)
        names = [[g * PAIRS + j for j in range(PAIRS)] for g in range(groups)]
        return lax.all_to_all(item, "ctx", 0, 0, axis_index_groups=names, tiled=True)

    grad, dense_inner_grad, out_inner_grad, attended_grad, all_ups = call(
        grad_kernel,
        index,
        [
            whole(item)
            for item in [after(grad_pack, first_inner)] + grad_packs + [mask, dense_weight, dense_down]
        ],
        [
            ((total, width), bf16, None, None),
            ((total, ADAPT_COLS), bf16, None, None),
            ((total, ADAPT_COLS), bf16, None, None),
            ((WA, 2, rows, HEAD), bf16, None, None),
            ((2, ADAPT_COLS, width), bf16, None, None),
        ],
        scratch=[pltpu.VMEM((ADAPT_COLS, width), bf16), pltpu.VMEM((ADAPT_COLS, width), bf16)],
        flops=2 * total * width * (own_width + 2 * ADAPT_COLS),
    )
    attended_grad = to_pairs(attended_grad.reshape(PAIRS, rows, HEAD))
    in_parts.append(swap(after(in_cuts[1], grad_packs[1]), 2))
    qkv_others = after(qkv_others, first_norm, grad)
    value = to_pairs(after(project(2, 1, False), attended_grad))
    in_parts.append(swap(after(in_cuts[2], in_parts[1]), 3))
    pair_own = after(project(1, 2, True), value, in_parts[2])
    pair = to_pairs(pair_own)
    in_parts.append(swap(after(in_cuts[3], in_parts[2]), 3))

    tile = min(512, hidden_width)
    tiles = hidden_width // tile
    in_downs = [whole(in_down)] + [
        (item, (own_width, ADAPT_COLS), lambda *_: (0, 0)) for item in feed_packs
    ]

    in_mate = swap(after(in_mate_cut, pair_own), 1)

    def feed(part, known, norm, *earlier):
        count = tiles
        first = part * count
        own_tile = lambda t, ref: (0, ref[0] * tiles + first + t)
        strip = part_cols * tile // 128
        items = [whole(after(norm, *earlier)), whole(grad)]
        items += [
            (in_weight, (own_width, tile), own_tile),
            (in_mate, (own_width, tile), lambda t, ref: (0, first + t)),
        ]
        items += [
            (item, (own_width // 2, tile), lambda t, ref: (0, first + t)) for item in in_parts
        ]
        items.append((in_up, (part_cols, tile), own_tile))
        for r, item in zip((1, 2, 3), feed_packs):
            row = (own_width + (r == 3) * part_cols * hidden_width // 128) // strip + first
            items.append((item, (strip, 128), lambda t, ref, row=row: (row + t, 0)))
        items += in_downs + [whole(mask)] if known is None else [whole(known)]
        items += [
            (in_bias[None, :], (1, tile), own_tile),
            whole(gains[2]),
            (out_weight, (tile, width), lambda t, ref: (first + t, 0)),
            (out_down, (tile, ADAPT_COLS), lambda t, ref: (first + t, 0)),
            whole(out_inner_grad),
        ]
        size = count * tile
        return call(
            functools.partial(feed_kernel, known is None, True),
            index,
            items,
            [
                ((total, width), f32, None, None),
                ((total, width), f32, None, None),
                ((total, ADAPT_COLS), f32, None, None),
                ((total, ADAPT_COLS), f32, None, None),
                ((size, ADAPT_COLS), bf16, (tile, ADAPT_COLS), lambda t, ref: (t, 0)),
                ((ADAPT_COLS, size), bf16, (ADAPT_COLS, tile), lambda t, ref: (0, t)),
                ((total, ADAPT_COLS), bf16, None, None),
            ],
            grid=(count,),
            scratch=[pltpu.VMEM((ADAPT_COLS, tile), bf16)],
            flops=8 * total * width * size,
        )

    (
        branch_sum,
        norm_grad,
        out_inner,
        second_inner_grad,
        out_down_grad,
        in_up_grad,
        second_inner,
    ) = feed(0, None, second_norm, pair)

    pair_rows = PAIRS * rows
    group = ctx // PAIRS
    own_pack = (ctx % PAIRS) // 2
    own_starts = jnp.sum(
        jnp.where(jnp.arange(WA)[:, None] == own_pack, starts, 0), axis=0
    )
    all_places = places(0, groups * pair_rows)
    all_inside = own_starts[None, :] <= all_places[:, None]
    all_begins = jnp.max(jnp.where(all_inside, own_starts[None, :], 0), axis=1)
    k_tables = rotary_tables(all_places - all_begins)
    if groups == 1:
        q_place, q_begin, q_tables = all_places, all_begins, k_tables
    else:
        q_place = part_rows(all_places, group, pair_rows)
        q_begin = part_rows(all_begins, group, pair_rows)
        q_tables = [part_rows(item, group, pair_rows) for item in k_tables]
    value, attended_grad = [item.reshape(pair_rows, HEAD) for item in (value, attended_grad)]
    key = pair
    sets = [[g * PAIRS + j for g in range(groups)] for j in range(PAIRS)]
    if groups > 1:
        key, value = [
            lax.all_gather(item, "ctx", axis=0, axis_index_groups=sets, tiled=True)
            for item in (pair[:, :1], value)
        ]
    both = attend(
        after(pair, in_parts[3], in_mate, *feed_packs),
        key,
        value,
        attended_grad,
        q_begin[:, None],
        q_place[:, None],
        all_places[None, :],
        q_tables,
        k_tables,
        rows,
    )
    if groups > 1:
        dkv = lax.psum_scatter(
            both[1], "ctx", scatter_dimension=0, axis_index_groups=sets, tiled=True
        )
        both = [jnp.concatenate([both[0], dkv], axis=1)]
    both = to_pairs(both[0]).reshape(WA, 2, 4, rows, HEAD)
    both = after(both, branch_sum)
    odq, dkv = both, both

    def sum_inner(partial):
        partial = (partial + swap(partial, 1)).astype(bf16)
        partial = partial.astype(f32) + swap(partial, 2).astype(f32)
        return (partial * mask).astype(bf16)

    def spread_rows(value):
        return [part_rows(value, wa, part_cols)] + [
            swap(part_rows(value, wa ^ r, part_cols), r) for r in (1, 2, 3)
        ]

    def exchange_sum(value):
        parts = value.reshape(contexts, -1, ADAPT_COLS)
        parts = lax.all_to_all(parts, "ctx", 0, 0, tiled=True)
        return jnp.sum(parts.astype(f32), axis=0).astype(bf16)

    def pack_grads(down_grad, norm, norm_grad, inner, ups):
        items = [whole(down_grad), (norm, (total, own_width), lambda _, ref: (0, ref[0]))]
        items += [whole(item) for item in [norm_grad, inner, grad] + ups]
        size = down_grad.size + own_width * ADAPT_COLS + part_cols * width
        size += sum(item.size for item in ups)
        return call(
            pack_grads_kernel,
            index,
            items,
            [((size // ADAPT_COLS, ADAPT_COLS), bf16, None, None)],
            scratch=[pltpu.VMEM((ADAPT_COLS, width), f32)],
        )[0]

    in_up_parts = spread_rows(in_up_grad)
    out_inner = sum_inner(out_inner)
    second_inner_grad = sum_inner(second_inner_grad)
    feed_packed = pack_grads(
        out_down_grad, second_norm, second_inner_grad, out_inner, in_up_parts
    )
    feed_sum = exchange_sum(after(feed_packed, both))
    odq = dkv = after(both, feed_packed)

    mixed_grads = [odq, dkv]
    up_items = []
    for kind in range(3):
        up_items.append(
            (qkv_up, (part_cols, own_width), lambda _, ref, kind=kind: (0, kind * WA + ref[0]))
        )
        for r, item in zip((1, 2, 3), first_packs):
            row = (ups_row + (r == 3) * ups_size) // (2 * strip_rows) + kind
            up_items.append(
                (item, (2 * strip_rows, 128), lambda _, ref, row=row: (row, 0))
            )
    mixed_inner, qkv_up_grad = call(
        mix_kernel,
        index,
        [whole(item) for item in mixed_grads] + up_items + [whole(first_inner)],
        [
            ((total, ADAPT_COLS), f32, None, None),
            ((ADAPT_COLS, 3 * own_width), bf16, None, None),
        ],
        scratch=[pltpu.VMEM((3, ADAPT_COLS, own_width), bf16)],
        flops=4 * total * ADAPT_COLS * 3 * own_width,
    )
    first_inner_grad = sum_inner(mixed_inner)
    up_parts = spread_rows(qkv_up_grad)
    dense_items = [after(odq, mixed_inner), branch_sum, dense_weight, dense_down, dense_inner_grad]
    reduced = [
        ((2, rows, width), f32, None, None),
        ((2, rows, width), bf16, None, None),
    ]
    keep, send, dense_inner, dense_down_grad = call(
        dense_kernel,
        index,
        [whole(item) for item in dense_items],
        reduced
        + [
            ((total, ADAPT_COLS), f32, None, None),
            ((own_width, ADAPT_COLS), bf16, None, None),
        ],
        scratch=[pltpu.VMEM((total, width), f32)],
        flops=2 * total * width * own_width,
    )
    dense_inner = sum_inner(dense_inner)
    near = swap(send, 1)
    away = swap((keep[1] + near[1].astype(f32)).astype(bf16), 2)
    output = (
        keep[0]
        + near[0].astype(f32)
        + away.astype(f32)
        + product(part_rows(dense_inner, wa, rows), all_ups[0])
        + product(part_rows(out_inner, wa, rows), all_ups[1])
        + dense_bias
        + out_bias
        + tokens[0].astype(f32)
    ).astype(bf16)[None]

    weight_items = []
    for kind in range(3):
        weight_items.append(
            (
                qkv_weight,
                (own_width, own_width),
                lambda _, ref, kind=kind: (0, kind * WA + ref[0]),
            )
        )
        for item, first in ((mate_weights, 2), (qkv_others, 2), (qkv_others, 5)):
            weight_items.append(
                (item, (own_width, own_width), lambda _, ref, at=first - kind: (0, at))
            )
    keep, send = call(
        norm_grad_kernel,
        index,
        [whole(item) for item in mixed_grads]
        + weight_items
        + [whole(item) for item in [after(gains[0], keep), norm_grad]],
        reduced,
        scratch=[pltpu.VMEM((total, width), f32)],
        flops=2 * total * width * 3 * own_width,
    )
    near = swap(send, 1)
    combined = (keep[1] + near[1].astype(f32)).astype(bf16)
    away = swap(combined, 2)
    down_at = rows * width // 128 // own_width
    down_block = lambda *_: (down_at, 0)
    tokens_grad = call(
        finish_kernel,
        index,
        [
            whole(item)
            for item in [
                keep,
                near,
                away,
                part_rows(first_inner_grad, wa, rows),
                part_rows(second_inner_grad, wa, rows),
            ]
        ]
        + [whole(qkv_down)]
        + [(item, (own_width, ADAPT_COLS), down_block) for item in first_packs]
        + in_downs
        + [whole(item) for item in [gains[0], gains[2], tokens[0], cotangent[0]]],
        [((rows, width), f32, None, None)],
        scratch=[pltpu.VMEM((rows, width), f32)],
    )[0][None]

    packed = pack_grads(dense_down_grad, first_norm, first_inner_grad, dense_inner, up_parts)
    packed = exchange_sum(after(packed, feed_sum))
    packed = jnp.concatenate([feed_sum, packed], axis=0)
    packed = lax.all_gather(packed, "ctx", axis=0)
    packed = after(packed, tokens_grad, output)
    down_shape = ((own_width, ADAPT_COLS), f32, None, None)
    up_shape = ((part_cols, width), f32, None, None)
    (
        out_down_grad,
        in_down_grad,
        out_up_grad,
        in_up_grad,
        dense_down_grad,
        qkv_down_grad,
        dense_up_grad,
        qkv_up_grad,
    ) = call(
        functools.partial(unpack_grads_kernel, feed_sum.shape[0]),
        index,
        [whole(packed)],
        [
            ((hidden_width, ADAPT_COLS), f32, None, None),
            down_shape,
            up_shape,
            ((part_cols, WA * hidden_width), f32, None, None),
            down_shape,
            down_shape,
            up_shape,
            ((part_cols, 3 * width), f32, None, None),
        ],
    )
    return (
        output,
        tokens_grad,
        qkv_down_grad,
        qkv_up_grad,
        dense_down_grad,
        dense_up_grad,
        in_down_grad,
        in_up_grad,
        out_down_grad,
        out_up_grad,
    )


def solution(mesh):
    rows = P("wa", "ctx", None)
    shard = P("wa", None)
    in_specs = (
        (rows, rows, P(), shard, shard)
        + (P(),) * 4
        + (shard, P()) * 4
        + (shard,) * 8
    )
    out_specs = (rows, rows) + (shard,) * 8
    return jax.shard_map(
        functools.partial(body, mesh.shape["ctx"]),
        mesh=mesh,
        in_specs=in_specs,
        out_specs=out_specs,
        check_vma=False,
    )
```

```python
import functools
import math

import jax
import jax.numpy as jnp
from jax import lax
from jax.experimental import pallas as pl
from jax.experimental.pallas import tpu as pltpu
from jax.sharding import PartitionSpec as P

HEADS = 8
HEAD = 256
ROT = 64
RANK = 16
BLOCK = 64
ADAPT_COLS = 128
WA = 4
PAIRS = 8
VMEM_BYTES = 58 * 1024 * 1024

epsilon = 1e-05
masked_score = -1e30
f32 = jnp.float32
bf16 = jnp.bfloat16


def product(left, right):
    return jnp.dot(left, right, preferred_element_type=f32)


def times_t(left, right):
    return lax.dot_general(left, right, (((1,), (1,)), ((), ())), preferred_element_type=f32)


def t_times(left, right):
    return lax.dot_general(left, right, (((0,), (0,)), ((), ())), preferred_element_type=f32)


def swap(value, bits):
    return lax.ppermute(value, "wa", [(i, i ^ bits) for i in range(WA)])


def after(value, *earlier):
    return lax.optimization_barrier((value, *earlier))[0]


def absolute(pieces, wa):
    low = wa % 2 == 1
    high = wa >= 2
    p = [
        jnp.where(low, pieces[1], pieces[0]),
        jnp.where(low, pieces[0], pieces[1]),
        jnp.where(low, pieces[3], pieces[2]),
        jnp.where(low, pieces[2], pieces[3]),
    ]
    return [
        jnp.where(high, p[2], p[0]),
        jnp.where(high, p[3], p[1]),
        jnp.where(high, p[0], p[2]),
        jnp.where(high, p[1], p[3]),
    ]


def rotary_tables(offset):
    half = ROT // 2
    lane = jnp.arange(128, dtype=jnp.int32)
    freq = 10000.0 ** (-2.0 * (lane % half).astype(f32) / ROT)
    freq = jnp.where(lane < ROT, freq, 0.0)
    angle = offset.astype(f32)[:, None] * freq[None, :]
    sign = jnp.where(lane < half, -1.0, 1.0)
    return jnp.cos(angle), jnp.sin(angle) * sign[None, :]


def turn_first(values, cosine, sine):
    lane = lax.broadcasted_iota(jnp.int32, values.shape, 1)
    partner = jnp.where(
        lane < ROT // 2, pltpu.roll(values, 128 - ROT // 2, 1), pltpu.roll(values, ROT // 2, 1)
    )
    return values * cosine + partner * sine


def call(kernel, index, inputs, outputs, grid=(1,), scratch=(), flops=0, name=None):
    def spec(shape, block, where):
        if where is None:
            zeros = (0,) * len(shape)
            return pl.BlockSpec(shape, lambda *_: zeros)
        return pl.BlockSpec(block, where)

    size = sum(a.size * a.dtype.itemsize if w is None else math.prod(i or 1 for i in b) * 2 * math.prod(grid)
               for a, b, w in inputs)
    return pl.pallas_call(
        kernel,
        grid_spec=pltpu.PrefetchScalarGridSpec(
            num_scalar_prefetch=1,
            grid=grid,
            in_specs=[spec(a.shape, b, w) for a, b, w in inputs],
            out_specs=[spec(s, b, w) for s, _, b, w in outputs],
            scratch_shapes=list(scratch),
        ),
        out_shape=[jax.ShapeDtypeStruct(s, d) for s, d, _, _ in outputs],
        compiler_params=pltpu.CompilerParams(vmem_limit_bytes=VMEM_BYTES),
        cost_estimate=pl.CostEstimate(flops=flops, bytes_accessed=size, transcendentals=0),
    )(index, *[a for a, _, _ in inputs])


def whole(array):
    return (array, None, None)


def copy_kernel(index_ref, *refs):
    count = len(refs) // 2
    for source, target in zip(refs[:count], refs[count:]):
        target[...] = source[...].reshape(target.shape)


def cut_columns(index, weight, size, kinds, cuts, parts=1):
    rows = weight.shape[0]
    part = size // parts
    inputs, outputs = [], []
    for r, division, number in cuts:
        height = rows // division

        def where(slot, t, ref, r=r, number=number):
            kind = sum(kind * (slot == i) for i, kind in enumerate(kinds))
            return (0 if number is None else ref[number], (kind * WA + ref[r]) * parts + t)

        inputs.append((weight, (height, part), where))
        outputs.append(
            (
                (height, len(kinds) * size),
                weight.dtype,
                (height, part),
                lambda slot, t, ref: (0, slot * parts + t),
            )
        )
    return call(copy_kernel, index, inputs, outputs, grid=(len(kinds), parts))


def strips(value):
    return [value[:, i : i + 128] for i in range(0, value.shape[1], 128)]


def store_strips(target, first, value):
    for item in strips(value):
        target[first : first + item.shape[0], :] = item
        first += item.shape[0]
    return first


def pack_kernel(index_ref, *refs):
    plain, last_ref = refs[:-6], refs[-6]
    (ups_mate, ups_peer, ups_far), (away_ref, near_ref) = refs[-5:-2], refs[-2:]
    first = 0
    for ref in plain:
        store_strips(away_ref, first, ref)
        first = store_strips(near_ref, first, ref)
    blank = ups_peer.shape[0] * ups_peer.shape[1] // 128
    store_strips(near_ref, first, ups_mate)
    store_strips(near_ref, first + blank, ups_mate)
    store_strips(away_ref, first, ups_peer)
    store_strips(away_ref, first + blank, ups_far)
    store_strips(near_ref, first + 2 * blank, last_ref)
    store_strips(away_ref, first + 2 * blank, last_ref)


def pack_small(index, plain, up, kinds, last):
    block = up.shape[1] // len(kinds) // WA
    items = [whole(item) for item in plain + [last]]
    size = sum(item.size for item in plain) // 128
    ups = up.shape[0] * block * len(kinds) // 128
    cut = jnp.concatenate if len(kinds) > 1 else (lambda v, axis: v[0])
    for r in (1, 2, 3):
        items.append(
            whole(
                cut(
                    [
                        lax.dynamic_slice_in_dim(up, (kind * WA + index[r]) * block, block, axis=1)
                        for kind in kinds
                    ],
                    axis=1,
                )
            )
        )
    shape = (size + 2 * ups + last.shape[0], 128)
    return call(pack_kernel, index, items, [(shape, bf16, None, None)] * 2)


def front_kernel(index_ref, *refs):
    token_ref, down_ref = refs[:2]
    packs = refs[2:5]
    mask_ref, g1, b1, g2, b2, first_ref, second_ref, inner_ref = refs[5:]
    rows, width = token_ref.shape
    wide = down_ref.shape[0]
    step = 32
    for r in range(WA):
        base = pl.multiple_of(index_ref[r] * rows, rows)
        for start in range(0, rows, step):
            if r == 0:
                values = token_ref[start : start + step, :]
            else:
                values = jnp.concatenate(
                    [
                        packs[r - 1][i * rows + start : i * rows + start + step, :]
                        for i in range(width // 128)
                    ],
                    axis=1,
                )
            values = values.astype(f32)
            centered = values - jnp.mean(values, axis=1, keepdims=True)
            spread = jnp.mean(centered * centered, axis=1, keepdims=True)
            normal = centered * lax.rsqrt(spread + epsilon)
            first_ref[pl.ds(base + start, step), :] = (normal * g1[...] + b1[...]).astype(bf16)
            second_ref[pl.ds(base + start, step), :] = (normal * g2[...] + b2[...]).astype(bf16)
    total = 0.0
    first = rows * width // 128
    for r in range(WA):
        columns = pl.ds(pl.multiple_of(index_ref[r] * wide, wide), wide)
        down = down_ref[...] if r == 0 else packs[r - 1][first : first + wide, :]
        total += product(first_ref[:, columns], down)
    inner_ref[...] = (total * mask_ref[...]).astype(bf16)


def pieces_of(index_ref, refs):
    wide = refs[0].shape[0]
    pieces = []
    for r, ref in enumerate(refs):
        size = ref.shape[0]
        first = index_ref[r] * wide
        if len(refs) > WA and r >= 2:
            first = index_ref[2 + (r - 2) // 2] * wide + (r % 2) * size
        pieces.append((pl.ds(pl.multiple_of(first, size), size), ref))
    return pieces


def read(ref):
    return ref[...].reshape(ref.shape[-2:])


def join_ups(index_ref, ups, joined):
    size = ADAPT_COLS // WA
    for r, ref in enumerate(ups):
        first = pl.multiple_of(index_ref[r] * size, size)
        if ref.shape[-1] == joined.shape[-1]:
            joined[pl.ds(first, size), :] = read(ref)
        else:
            for i in range(joined.shape[-1] // 128):
                joined[pl.ds(first, size), i * 128 : (i + 1) * 128] = ref[
                    i * size : (i + 1) * size, :
                ]


def qkv_kernel(turned, index_ref, hidden_ref, *refs):
    weights, ups = refs[:4], refs[4:8]
    inner_ref, bias_ref, cos_ref, sin_ref, out_ref, joined = refs[8:]
    join_ups(index_ref, ups, joined)
    total = product(inner_ref[...], joined[...]) + bias_ref[...]
    for columns, ref in pieces_of(index_ref, weights):
        total += product(hidden_ref[:, columns], read(ref))
    shape = out_ref.shape
    if turned:
        first = turn_first(total[:, :128], cos_ref[...], sin_ref[...])
        out_ref[..., :128] = first.astype(bf16).reshape(shape[:-1] + (128,))
        out_ref[..., 128:] = total[:, 128:].astype(bf16).reshape(shape[:-1] + (HEAD - 128,))
    else:
        out_ref[...] = total.astype(bf16).reshape(shape)


def grad_kernel(index_ref, *refs):
    parts = refs[:WA]
    mask_ref, weight_ref, down_ref = refs[WA : WA + 3]
    grad_ref, dense_ref, out_ref, heads_ref, ups_ref, dense_joined, out_joined = refs[WA + 3 :]
    size = ADAPT_COLS // WA
    rows = parts[0].shape[0] - 2 * size
    for r in range(WA):
        first = pl.ds(pl.multiple_of(index_ref[r] * size, size), size)
        dense_joined[first, :] = parts[r][rows : rows + size, :]
        out_joined[first, :] = parts[r][rows + size :, :]
        grad_ref[pl.ds(pl.multiple_of(index_ref[r] * rows, rows), rows), :] = parts[r][:rows, :]
    ups_ref[0] = dense_joined[...]
    ups_ref[1] = out_joined[...]
    grad = grad_ref[...]
    dense = (times_t(grad, dense_joined[...]) * mask_ref[...]).astype(bf16)
    dense_ref[...] = dense
    out_ref[...] = (times_t(grad, out_joined[...]) * mask_ref[...]).astype(bf16)
    for head in range(2):
        span = slice(head * HEAD, (head + 1) * HEAD)
        total = times_t(grad, weight_ref[span, :]) + times_t(dense, down_ref[span, :])
        heads_ref[:, head] = total.astype(bf16).reshape(WA, rows, HEAD)


def gelu_parts(values):
    bell = jnp.exp(-0.5 * values * values)
    t = 1.0 / (1.0 + (0.3275911 * math.sqrt(0.5)) * jnp.abs(values))
    series = 1.061405429 * 0.5
    for factor in (-1.453152027, 1.421413741, -0.284496736, 0.254829592):
        series = series * t + 0.5 * factor
    tail = series * t * bell
    below = jnp.where(values > 0, 1.0 - tail, tail)
    return values * below, below + values * bell * (1.0 / math.sqrt(2.0 * math.pi))


def feed_kernel(starts, ends, index_ref, hidden_ref, grad_ref, *refs):
    weights, ups, refs = refs[:6], refs[6:10], refs[10:]
    if starts:
        downs, mask_ref, refs = refs[:4], refs[4], refs[5:]
    else:
        known_ref, refs = refs[0], refs[1:]
    bias_ref, gain_ref, out_w_ref, out_down_ref, out_inner_grad_ref = refs[:5]
    (
        out_ref,
        norm_grad_ref,
        out_inner_ref,
        inner_grad_ref,
        out_down_grad_ref,
        in_up_grad_ref,
        inner_ref,
        joined,
    ) = refs[5:]
    step = pl.program_id(0)

    @pl.when(step == 0)
    def _():
        if starts:
            wide = downs[0].shape[0]
            total = 0.0
            for r in range(WA):
                columns = pl.ds(pl.multiple_of(index_ref[r] * wide, wide), wide)
                total += product(hidden_ref[:, columns], downs[r][...])
            inner_ref[...] = (total * mask_ref[...]).astype(bf16)
        else:
            inner_ref[...] = known_ref[...]
        out_ref[...] = jnp.zeros_like(out_ref)
        norm_grad_ref[...] = jnp.zeros_like(norm_grad_ref)
        out_inner_ref[...] = jnp.zeros_like(out_inner_ref)
        inner_grad_ref[...] = jnp.zeros_like(inner_grad_ref)

    join_ups(index_ref, ups, joined)
    pre = product(inner_ref[...], joined[...]) + bias_ref[...]
    for columns, ref in pieces_of(index_ref, weights):
        pre += product(hidden_ref[:, columns], read(ref))
    units, slope = gelu_parts(pre)
    units = units.astype(bf16)
    pre_grad = times_t(grad_ref[...], out_w_ref[...]) + times_t(
        out_inner_grad_ref[...], out_down_ref[...]
    )
    pre_grad = (pre_grad * slope).astype(bf16)
    out_ref[...] += product(units, out_w_ref[...])
    for columns, ref in pieces_of(index_ref, weights):
        norm_grad_ref[:, columns] += times_t(pre_grad, read(ref))
    out_inner_ref[...] += product(units, out_down_ref[...])
    inner_grad_ref[...] += times_t(pre_grad, joined[...])
    out_down_grad_ref[...] = t_times(units, out_inner_grad_ref[...]).astype(bf16)
    in_up_grad_ref[...] = t_times(inner_ref[...], pre_grad).astype(bf16)

    @pl.when(step == pl.num_programs(0) - 1)
    def _():
        norm_grad_ref[...] = norm_grad_ref[...] * gain_ref[...]


def scatter_rows(index_ref, total_ref, keep_ref, send_ref):
    rows = keep_ref.shape[1]
    for r, (ref, slot) in enumerate(((keep_ref, 0), (send_ref, 0), (keep_ref, 1), (send_ref, 1))):
        part = total_ref[pl.ds(pl.multiple_of(index_ref[r] * rows, rows), rows), :]
        ref[slot] = part.astype(ref.dtype)


def head_rows(ref, head):
    return ref[:, head, 0].reshape(-1, HEAD)


def dense_kernel(
    index_ref,
    heads_ref,
    sum_ref,
    weight_ref,
    down_ref,
    inner_grad_ref,
    keep_ref,
    send_ref,
    inner_ref,
    down_grad_ref,
    total,
):
    result = sum_ref[...]
    inner = 0.0
    for head in range(2):
        span = slice(head * HEAD, (head + 1) * HEAD)
        heads = head_rows(heads_ref, head)
        result += product(heads, weight_ref[span, :])
        inner += product(heads, down_ref[span, :])
        down_grad_ref[span, :] = t_times(heads, inner_grad_ref[...]).astype(bf16)
    inner_ref[...] = inner
    total[...] = result
    scatter_rows(index_ref, total, keep_ref, send_ref)


def mixed_rows(query_grad_ref, key_grad_ref, kind, head):
    if kind == 0:
        return query_grad_ref[:, head, 1].reshape(-1, HEAD)
    return key_grad_ref[:, head, kind + 1].reshape(-1, HEAD)


def mix_kernel(index_ref, *refs):
    grads, ups = refs[:2], refs[2 : 2 + 3 * WA]
    inner_ref, inner_grad_ref, up_grad_ref, joined = refs[2 + 3 * WA :]
    width = 2 * HEAD
    for kind in range(3):
        for r in range(WA):
            size = ADAPT_COLS // WA
            first = pl.multiple_of(index_ref[r] * size, size)
            ref = ups[kind * WA + r]
            if r == 0:
                joined[kind, pl.ds(first, size), :] = ref[...]
            else:
                for i in range(width // 128):
                    joined[kind, pl.ds(first, size), i * 128 : (i + 1) * 128] = ref[
                        i * size : (i + 1) * size, :
                    ]
    total = 0.0
    for kind in range(3):
        for head in range(2):
            span = slice(head * HEAD, (head + 1) * HEAD)
            rows = mixed_rows(*grads, kind, head)
            total += times_t(rows, joined[kind, :, span])
            out = slice(kind * width + head * HEAD, kind * width + (head + 1) * HEAD)
            up_grad_ref[:, out] = t_times(inner_ref[...], rows).astype(bf16)
    inner_grad_ref[...] = total


def norm_grad_kernel(index_ref, *refs):
    grads, weights = refs[:2], refs[2:14]
    gain_ref, sum_ref, keep_ref, send_ref, total = refs[14:]
    sets = [pieces_of(index_ref, weights[WA * kind : WA * kind + WA]) for kind in range(3)]
    rows = [[mixed_rows(*grads, kind, head) for head in range(2)] for kind in range(3)]
    for piece in range(WA):
        columns = sets[0][piece][0]
        part = 0.0
        for kind in range(3):
            weight = read(sets[kind][piece][1])
            for head in range(2):
                part += times_t(rows[kind][head], weight[:, head * HEAD : (head + 1) * HEAD])
        total[:, columns] = part * gain_ref[:, columns] + sum_ref[:, columns]
    scatter_rows(index_ref, total, keep_ref, send_ref)


def own_rows_of(inner, grad, index_ref, total):
    size = ADAPT_COLS // WA
    total[...] = t_times(inner, grad)
    return total[pl.ds(pl.multiple_of(index_ref[0] * size, size), size), :].astype(bf16)


def pack_grads_kernel(index_ref, *refs):
    down_ref, norm_ref, norm_grad_ref, inner_ref, grad_ref = refs[:5]
    ups, (packed_ref, total) = refs[5:9], refs[9:]
    at = down_ref.shape[0]
    packed_ref[:at, :] = down_ref[...]
    part = t_times(norm_ref[...], norm_grad_ref[...]).astype(bf16)
    packed_ref[at : at + part.shape[0], :] = part
    at += part.shape[0]
    at = store_strips(packed_ref, at, own_rows_of(inner_ref[...], grad_ref[...], index_ref, total))
    for ref in ups:
        at = store_strips(packed_ref, at, ref)


def unpack_grads_kernel(feed_size, index_ref, source_ref, *refs):
    packed = source_ref[...]
    size = ADAPT_COLS // WA
    for outs, start, end in ((refs[:4], 0, feed_size), (refs[4:], feed_size, packed.shape[1])):
        part = packed[:, start:end].reshape(-1, ADAPT_COLS)
        down_ref, norm_ref, inner_ref, up_ref = outs
        at = 0
        for ref in (down_ref, norm_ref):
            ref[...] = part[at : at + ref.shape[0], :].astype(f32)
            at += ref.shape[0]
        for i in range(inner_ref.shape[1] // 128):
            inner_ref[:, i * 128 : (i + 1) * 128] = part[at : at + size, :].astype(f32)
            at += size
        kinds = 3 if start else 1
        width = up_ref.shape[1] // kinds
        block = width // WA
        for r in range(WA):
            for kind in range(kinds):
                for i in range(block // 128):
                    first = kind * width + index_ref[r] * block + i * 128
                    columns = pl.ds(pl.multiple_of(first, 128), 128)
                    up_ref[:, columns] = part[at : at + size, :].astype(f32)
                    at += size


def finish_kernel(index_ref, *refs):
    keep_ref, near_ref, away_ref, first_ref, second_ref = refs[:5]
    first_downs, second_downs = refs[5:9], refs[9:13]
    g1, g2, token_ref, grad_ref, out_ref, total = refs[13:]
    total[...] = keep_ref[0] + near_ref[0].astype(f32) + away_ref[...].astype(f32)
    wide = first_downs[0].shape[0]
    for r in range(WA):
        columns = pl.ds(pl.multiple_of(index_ref[r] * wide, wide), wide)
        total[:, columns] += (
            times_t(first_ref[...], first_downs[r][...]) * g1[:, columns]
            + times_t(second_ref[...], second_downs[r][...]) * g2[:, columns]
        )
    step = 32
    for start in range(0, total.shape[0], step):
        span = slice(start, start + step)
        values = token_ref[span, :].astype(f32)
        centered = values - jnp.mean(values, axis=1, keepdims=True)
        rstd = lax.rsqrt(jnp.mean(centered * centered, axis=1, keepdims=True) + epsilon)
        normal = centered * rstd
        part = total[span, :]
        part = (
            part
            - jnp.mean(part, axis=1, keepdims=True)
            - normal * jnp.mean(part * normal, axis=1, keepdims=True)
        )
        out_ref[span, :] = grad_ref[span, :].astype(f32) + rstd * part


def attention_kernel(
    joint,
    query_ref,
    key_ref,
    value_ref,
    grad_ref,
    begin_ref,
    place_ref,
    key_place_ref,
    q_cos_ref,
    q_sin_ref,
    k_cos_ref,
    k_sin_ref,
    rows_ref,
    *refs,
):
    keys_ref, dk_sum, dv_sum = (rows_ref, *refs) if joint else refs
    step = pl.program_id(0)
    scale = 1.0 / math.sqrt(HEAD)

    @pl.when(step == 0)
    def _():
        dk_sum[...] = jnp.zeros_like(dk_sum)
        dv_sum[...] = jnp.zeros_like(dv_sum)

    query = query_ref[...].reshape(-1, HEAD)
    key = key_ref[...].reshape(-1, HEAD)
    value = value_ref[...]
    grad = grad_ref[...]
    key_place = key_place_ref[...]
    allowed = (key_place >= begin_ref[...]) & (key_place <= place_ref[...])
    scores = jnp.where(allowed, times_t(query, key) * scale, masked_score)
    top = jnp.max(scores, axis=1, keepdims=True)
    weights = jnp.exp(scores - top)
    prob = weights * (1.0 / jnp.sum(weights, axis=1, keepdims=True))
    prob_low = prob.astype(bf16)
    part, block = query.shape[0], rows_ref.shape[2]
    shape = (part // block, block)
    own = pl.ds(step * shape[0], shape[0]) if joint else slice(None)
    rows_ref[own, 0] = product(prob_low, value).astype(bf16).reshape(shape + (HEAD,))
    prob_grad = times_t(grad, value)
    delta = jnp.sum(prob * prob_grad, axis=1, keepdims=True)
    score_grad = (prob * (prob_grad - delta)).astype(bf16)
    dq = product(score_grad, key) * scale
    first = turn_first(dq[:, :128], q_cos_ref[...], -q_sin_ref[...])
    rows_ref[own, 1, :, :128] = first.astype(bf16).reshape(shape + (128,))
    rows_ref[own, 1, :, 128:] = dq[:, 128:].astype(bf16).reshape(shape + (HEAD - 128,))
    dk_sum[...] += t_times(score_grad, query)
    dv_sum[...] += t_times(prob_low, grad)

    @pl.when(step == pl.num_programs(0) - 1)
    def _():
        base = 2 if joint else 0
        shape = keys_ref.shape[:1] + keys_ref.shape[2:3]
        dk = dk_sum[...] * scale
        first = turn_first(dk[:, :128], k_cos_ref[...], -k_sin_ref[...])
        keys_ref[:, base, :, :128] = first.astype(bf16).reshape(shape + (128,))
        keys_ref[:, base, :, 128:] = dk[:, 128:].astype(bf16).reshape(shape + (HEAD - 128,))
        keys_ref[:, base + 1] = dv_sum[...].astype(bf16).reshape(shape + (HEAD,))


def attend(query, key, value, grad, begin, place, key_place, q_tables, k_tables, block):
    rows = query.shape[0] * block
    keys = key.shape[0] * block
    part = min(256, rows)
    joint = rows == keys
    by_rows = lambda i: (i, 0)
    all_rows = lambda i: (0, 0)
    fixed = lambda i: (0, 0, 0, 0)
    if joint:
        shapes = [(keys // block, 4, block, HEAD)]
        out_specs = [pl.BlockSpec(shapes[0], fixed)]
    else:
        shapes = [(rows // block, 2, block, HEAD), (keys // block, 2, block, HEAD)]
        out_specs = [
            pl.BlockSpec((part // block, 2, block, HEAD), lambda i: (i, 0, 0, 0)),
            pl.BlockSpec(shapes[1], fixed),
        ]
    return pl.pallas_call(
        functools.partial(attention_kernel, joint),
        grid=(rows // part,),
        in_specs=[
            pl.BlockSpec((part // block, 1, block, HEAD), lambda i: (i, 1, 0, 0)),
            pl.BlockSpec((keys // block, 1, block, HEAD), fixed),
            pl.BlockSpec((keys, HEAD), all_rows),
            pl.BlockSpec((part, HEAD), by_rows),
            pl.BlockSpec((part, 1), by_rows),
            pl.BlockSpec((part, 1), by_rows),
            pl.BlockSpec((1, keys), all_rows),
            pl.BlockSpec((part, 128), by_rows),
            pl.BlockSpec((part, 128), by_rows),
            pl.BlockSpec((keys, 128), all_rows),
            pl.BlockSpec((keys, 128), all_rows),
        ],
        out_specs=out_specs,
        out_shape=[jax.ShapeDtypeStruct(shape, bf16) for shape in shapes],
        scratch_shapes=[pltpu.VMEM((keys, HEAD), f32), pltpu.VMEM((keys, HEAD), f32)],
        compiler_params=pltpu.CompilerParams(vmem_limit_bytes=VMEM_BYTES),
        cost_estimate=pl.CostEstimate(
            flops=14 * rows * keys * HEAD,
            bytes_accessed=16 * keys * HEAD,
            transcendentals=rows * keys,
        ),
    )(query, key, value, grad, begin, place, key_place, *q_tables, *k_tables)


def body(
    contexts,
    tokens,
    cotangent,
    deal,
    doc_lengths,
    doc_adapter,
    ln1_gain,
    ln1_bias,
    ln2_gain,
    ln2_bias,
    qkv_weight,
    qkv_bias,
    dense_weight,
    dense_bias,
    in_weight,
    in_bias,
    out_weight,
    out_bias,
    qkv_down,
    qkv_up,
    dense_down,
    dense_up,
    in_down,
    in_up,
    out_down,
    out_up,
):
    rows = tokens.shape[1]
    width = tokens.shape[2]
    wa = lax.axis_index("wa")
    ctx = lax.axis_index("ctx")
    total = WA * rows
    own_width = width // WA
    hidden_width = in_weight.shape[1] // WA
    part_cols = ADAPT_COLS // WA
    groups = contexts // PAIRS
    half = own_width // 2
    relative = [wa, wa ^ 1, wa ^ 2, wa ^ 3]
    index = jnp.stack(relative + [ctx % 2, ctx, wa * 0, wa * 0 + 1]).astype(jnp.int32)

    def columns(value, which, size):
        return lax.dynamic_slice_in_dim(value, which * size, size, axis=1)

    def part_rows(value, which, size):
        return lax.dynamic_slice_in_dim(value, which * size, size, axis=0)

    limit = 64
    numbers = jnp.concatenate(
        [doc_lengths // limit, doc_lengths % limit, doc_adapter], axis=1
    ).astype(bf16)
    numbers = jnp.pad(numbers, ((0, 15), (0, 128 - numbers.shape[1])))
    first_pack = pack_small(index, [tokens[0], qkv_down], qkv_up, [0, 1, 2], numbers)

    def gather_rows(weight, size, kinds, *earlier):
        cuts = cut_columns(index, weight, size, kinds, [(2, contexts, 5), (3, contexts, 5)])
        parts = [swap(cuts[0], 2), swap(cuts[1], 3)]
        part = after(jnp.concatenate(parts, axis=1), *earlier)
        return part, lax.all_gather(part, "ctx", axis=0, tiled=True)

    qkv_others_part, qkv_others = gather_rows(qkv_weight, own_width, [2, 1, 0], *first_pack)
    in_cuts = cut_columns(
        index,
        in_weight,
        hidden_width,
        [0],
        [(2, 2, 6), (2, 2, 7), (3, 2, 6), (3, 2, 7)],
        4,
    )
    in_parts = [swap(after(in_cuts[0], qkv_others_part), 2)]
    def hand_on(away, near, *earlier):
        peer = swap(after(away, *earlier), 2)
        return [swap(near, 1), peer, swap(peer, 1)]

    mate_cuts = cut_columns(index, qkv_weight, own_width, [2, 1, 0], [(1, 1, None)])[0]
    in_mate_cut = cut_columns(index, in_weight, hidden_width, [0], [(1, 1, None)], 2)[0]
    first_packs = hand_on(*first_pack)
    grad_pack = jnp.concatenate([cotangent[0], dense_up, out_up], axis=0)
    grad_packs = hand_on(grad_pack, grad_pack, first_packs[1])
    mate_weights = swap(after(mate_cuts, first_packs[0]), 1)
    feed_pack = pack_small(index, [in_down], in_up, [0], numbers)
    feed_packs = hand_on(*feed_pack, grad_packs[1])

    docs_per_pack = doc_lengths.shape[1]
    tables = [numbers] + [item[-16:] for item in first_packs]
    tables = jnp.stack(absolute([item[0] for item in tables], wa)).astype(jnp.int32)
    lengths = tables[:, :docs_per_pack] * limit + tables[:, docs_per_pack : 2 * docs_per_pack]
    adapters = tables[:, 2 * docs_per_pack : 3 * docs_per_pack]
    starts = jnp.cumsum(lengths, axis=1) - lengths

    def places(first, size):
        slots = first + jnp.arange(size, dtype=jnp.int32)
        blocks = slots // BLOCK
        table = jnp.arange(deal.shape[0], dtype=jnp.int32)
        block = jnp.sum(jnp.where(table[None, :] == blocks[:, None], deal[None, :], 0), axis=1)
        return block * BLOCK + slots % BLOCK

    place = places(ctx * rows, rows)
    inside = starts[:, None, :] <= place[None, :, None]
    docs = jnp.sum(inside.astype(jnp.int32), axis=2) - 1
    begin = jnp.max(jnp.where(inside, starts[:, None, :], 0), axis=2)
    offset = (place[None, :] - begin).reshape(total)
    doc_table = jnp.arange(docs_per_pack, dtype=jnp.int32)
    chosen = jnp.sum(
        jnp.where(docs[:, :, None] == doc_table, adapters[:, None, :], 0), axis=2
    ).reshape(total)
    adapter_of = jnp.arange(ADAPT_COLS, dtype=jnp.int32) // RANK
    mask = (adapter_of[None, :] == chosen[:, None]).astype(f32)
    cosine, sine = rotary_tables(offset)

    gains = [item[None, :] for item in (ln1_gain, ln1_bias, ln2_gain, ln2_bias)]
    first_norm, second_norm, first_inner = call(
        front_kernel,
        index,
        [whole(item) for item in [after(tokens[0], in_parts[0], *feed_pack), qkv_down] + first_packs + [mask] + gains],
        [
            ((total, width), bf16, None, None),
            ((total, width), bf16, None, None),
            ((total, ADAPT_COLS), bf16, None, None),
        ],
        flops=2 * total * width * ADAPT_COLS,
    )

    strip = strip_rows = part_cols * HEAD // 128
    ups_row = (tokens.size + qkv_down.size) // 128
    ups_size = 3 * own_width * part_cols // 128

    def project(last, kinds, turned):
        own_block = lambda i, head, ref: (0, ((last - i) * WA + ref[0]) * 2 + head)
        items = [whole(first_norm), (qkv_weight, (own_width, HEAD), own_block)]
        for item, first in ((mate_weights, 0), (qkv_others, 0), (qkv_others, 3)):
            first = (first + 2 - last) * 2
            items.append(
                (
                    item,
                    (own_width, HEAD),
                    lambda i, head, ref, first=first: (0, first + 2 * i + head),
                )
            )
        items.append((qkv_up, (part_cols, HEAD), own_block))
        for r, item in zip((1, 2, 3), first_packs):
            row = (ups_row + (r == 3) * ups_size) // strip + last * 2
            items.append(
                (item, (strip, 128), lambda i, head, ref, row=row: (row - 2 * i + head, 0))
            )
        items += [
            whole(first_inner),
            (qkv_bias[None, :], (1, HEAD), own_block),
            whole(cosine),
            whole(sine),
        ]
        out = call(
            functools.partial(qkv_kernel, turned),
            index,
            items,
            [
                (
                    (WA, 2, kinds, rows, HEAD),
                    bf16,
                    (WA, 1, 1, rows, HEAD),
                    lambda i, head, ref: (0, head, i, 0, 0),
                )
            ],
            grid=(kinds, 2),
            scratch=[pltpu.VMEM((ADAPT_COLS, HEAD), bf16)],
            flops=2 * total * width * own_width * kinds,
        )[0]
        return out.reshape(PAIRS, kinds, rows, HEAD)

    def to_pairs(item):
        if groups == 1:
            return lax.all_to_all(item, "ctx", 0, 0, tiled=True)
        names = [[g * PAIRS + j for j in range(PAIRS)] for g in range(groups)]
        return lax.all_to_all(item, "ctx", 0, 0, axis_index_groups=names, tiled=True)

    grad, dense_inner_grad, out_inner_grad, attended_grad, all_ups = call(
        grad_kernel,
        index,
        [
            whole(item)
            for item in [after(grad_pack, first_inner)] + grad_packs + [mask, dense_weight, dense_down]
        ],
        [
            ((total, width), bf16, None, None),
            ((total, ADAPT_COLS), bf16, None, None),
            ((total, ADAPT_COLS), bf16, None, None),
            ((WA, 2, rows, HEAD), bf16, None, None),
            ((2, ADAPT_COLS, width), bf16, None, None),
        ],
        scratch=[pltpu.VMEM((ADAPT_COLS, width), bf16), pltpu.VMEM((ADAPT_COLS, width), bf16)],
        flops=2 * total * width * (own_width + 2 * ADAPT_COLS),
    )
    attended_grad = to_pairs(attended_grad.reshape(PAIRS, rows, HEAD))
    in_parts.append(swap(after(in_cuts[1], grad_packs[1]), 2))
    qkv_others = after(qkv_others, first_norm, grad)
    value = to_pairs(after(project(2, 1, False), attended_grad))
    in_parts.append(swap(after(in_cuts[2], in_parts[1]), 3))
    pair_own = after(project(1, 2, True), value, in_parts[2])
    pair = to_pairs(pair_own)
    in_parts.append(swap(after(in_cuts[3], in_parts[2]), 3))

    tile = min(512, hidden_width)
    tiles = hidden_width // tile
    in_downs = [whole(in_down)] + [
        (item, (own_width, ADAPT_COLS), lambda *_: (0, 0)) for item in feed_packs
    ]

    in_mate = swap(after(in_mate_cut, pair_own), 1)

    def feed(part, known, norm, *earlier):
        count = tiles
        first = part * count
        own_tile = lambda t, ref: (0, ref[0] * tiles + first + t)
        strip = part_cols * tile // 128
        items = [whole(after(norm, *earlier)), whole(grad)]
        items += [
            (in_weight, (own_width, tile), own_tile),
            (in_mate, (own_width, tile), lambda t, ref: (0, first + t)),
        ]
        items += [
            (item, (own_width // 2, tile), lambda t, ref: (0, first + t)) for item in in_parts
        ]
        items.append((in_up, (part_cols, tile), own_tile))
        for r, item in zip((1, 2, 3), feed_packs):
            row = (own_width + (r == 3) * part_cols * hidden_width // 128) // strip + first
            items.append((item, (strip, 128), lambda t, ref, row=row: (row + t, 0)))
        items += in_downs + [whole(mask)] if known is None else [whole(known)]
        items += [
            (in_bias[None, :], (1, tile), own_tile),
            whole(gains[2]),
            (out_weight, (tile, width), lambda t, ref: (first + t, 0)),
            (out_down, (tile, ADAPT_COLS), lambda t, ref: (first + t, 0)),
            whole(out_inner_grad),
        ]
        size = count * tile
        return call(
            functools.partial(feed_kernel, known is None, True),
            index,
            items,
            [
                ((total, width), f32, None, None),
                ((total, width), f32, None, None),
                ((total, ADAPT_COLS), f32, None, None),
                ((total, ADAPT_COLS), f32, None, None),
                ((size, ADAPT_COLS), bf16, (tile, ADAPT_COLS), lambda t, ref: (t, 0)),
                ((ADAPT_COLS, size), bf16, (ADAPT_COLS, tile), lambda t, ref: (0, t)),
                ((total, ADAPT_COLS), bf16, None, None),
            ],
            grid=(count,),
            scratch=[pltpu.VMEM((ADAPT_COLS, tile), bf16)],
            flops=8 * total * width * size,
        )

    (
        branch_sum,
        norm_grad,
        out_inner,
        second_inner_grad,
        out_down_grad,
        in_up_grad,
        second_inner,
    ) = feed(0, None, second_norm, pair)

    pair_rows = PAIRS * rows
    group = ctx // PAIRS
    own_pack = (ctx % PAIRS) // 2
    own_starts = jnp.sum(
        jnp.where(jnp.arange(WA)[:, None] == own_pack, starts, 0), axis=0
    )
    all_places = places(0, groups * pair_rows)
    all_inside = own_starts[None, :] <= all_places[:, None]
    all_begins = jnp.max(jnp.where(all_inside, own_starts[None, :], 0), axis=1)
    k_tables = rotary_tables(all_places - all_begins)
    if groups == 1:
        q_place, q_begin, q_tables = all_places, all_begins, k_tables
    else:
        q_place = part_rows(all_places, group, pair_rows)
        q_begin = part_rows(all_begins, group, pair_rows)
        q_tables = [part_rows(item, group, pair_rows) for item in k_tables]
    value, attended_grad = [item.reshape(pair_rows, HEAD) for item in (value, attended_grad)]
    key = pair
    sets = [[g * PAIRS + j for g in range(groups)] for j in range(PAIRS)]
    if groups > 1:
        key, value = [
            lax.all_gather(item, "ctx", axis=0, axis_index_groups=sets, tiled=True)
            for item in (pair[:, :1], value)
        ]
    both = attend(
        after(pair, in_mate, *feed_packs),
        key,
        value,
        attended_grad,
        q_begin[:, None],
        q_place[:, None],
        all_places[None, :],
        q_tables,
        k_tables,
        rows,
    )
    if groups > 1:
        dkv = lax.psum_scatter(
            both[1], "ctx", scatter_dimension=0, axis_index_groups=sets, tiled=True
        )
        both = [jnp.concatenate([both[0], dkv], axis=1)]
    both = to_pairs(after(both[0], in_parts[3])).reshape(WA, 2, 4, rows, HEAD)
    both = after(both, branch_sum)
    odq, dkv = both, both

    def sum_inner(partial):
        partial = (partial + swap(partial, 1)).astype(bf16)
        partial = partial.astype(f32) + swap(partial, 2).astype(f32)
        return (partial * mask).astype(bf16)

    def spread_rows(value):
        return [part_rows(value, wa, part_cols)] + [
            swap(part_rows(value, wa ^ r, part_cols), r) for r in (1, 2, 3)
        ]

    def exchange_sum(value):
        parts = value.reshape(contexts, -1, ADAPT_COLS)
        parts = lax.all_to_all(parts, "ctx", 0, 0, tiled=True)
        return jnp.sum(parts.astype(f32), axis=0).astype(bf16)

    def pack_grads(down_grad, norm, norm_grad, inner, ups):
        items = [whole(down_grad), (norm, (total, own_width), lambda _, ref: (0, ref[0]))]
        items += [whole(item) for item in [norm_grad, inner, grad] + ups]
        size = down_grad.size + own_width * ADAPT_COLS + part_cols * width
        size += sum(item.size for item in ups)
        return call(
            pack_grads_kernel,
            index,
            items,
            [((size // ADAPT_COLS, ADAPT_COLS), bf16, None, None)],
            scratch=[pltpu.VMEM((ADAPT_COLS, width), f32)],
        )[0]

    in_up_parts = spread_rows(in_up_grad)
    out_inner = sum_inner(out_inner)
    second_inner_grad = sum_inner(second_inner_grad)
    feed_packed = pack_grads(
        out_down_grad, second_norm, second_inner_grad, out_inner, in_up_parts
    )
    feed_sum = exchange_sum(after(feed_packed, both))
    odq = dkv = after(both, feed_packed)

    mixed_grads = [odq, dkv]
    up_items = []
    for kind in range(3):
        up_items.append(
            (qkv_up, (part_cols, own_width), lambda _, ref, kind=kind: (0, kind * WA + ref[0]))
        )
        for r, item in zip((1, 2, 3), first_packs):
            row = (ups_row + (r == 3) * ups_size) // (2 * strip_rows) + kind
            up_items.append(
                (item, (2 * strip_rows, 128), lambda _, ref, row=row: (row, 0))
            )
    mixed_inner, qkv_up_grad = call(
        mix_kernel,
        index,
        [whole(item) for item in mixed_grads] + up_items + [whole(first_inner)],
        [
            ((total, ADAPT_COLS), f32, None, None),
            ((ADAPT_COLS, 3 * own_width), bf16, None, None),
        ],
        scratch=[pltpu.VMEM((3, ADAPT_COLS, own_width), bf16)],
        flops=4 * total * ADAPT_COLS * 3 * own_width,
    )
    first_inner_grad = sum_inner(mixed_inner)
    up_parts = spread_rows(qkv_up_grad)
    dense_items = [after(odq, mixed_inner), branch_sum, dense_weight, dense_down, dense_inner_grad]
    reduced = [
        ((2, rows, width), f32, None, None),
        ((2, rows, width), bf16, None, None),
    ]
    keep, send, dense_inner, dense_down_grad = call(
        dense_kernel,
        index,
        [whole(item) for item in dense_items],
        reduced
        + [
            ((total, ADAPT_COLS), f32, None, None),
            ((own_width, ADAPT_COLS), bf16, None, None),
        ],
        scratch=[pltpu.VMEM((total, width), f32)],
        flops=2 * total * width * own_width,
    )
    dense_inner = sum_inner(dense_inner)
    near = swap(send, 1)
    away = swap((keep[1] + near[1].astype(f32)).astype(bf16), 2)
    output = (
        keep[0]
        + near[0].astype(f32)
        + away.astype(f32)
        + product(part_rows(dense_inner, wa, rows), all_ups[0])
        + product(part_rows(out_inner, wa, rows), all_ups[1])
        + dense_bias
        + out_bias
        + tokens[0].astype(f32)
    ).astype(bf16)[None]

    weight_items = []
    for kind in range(3):
        weight_items.append(
            (
                qkv_weight,
                (own_width, own_width),
                lambda _, ref, kind=kind: (0, kind * WA + ref[0]),
            )
        )
        for item, first in ((mate_weights, 2), (qkv_others, 2), (qkv_others, 5)):
            weight_items.append(
                (item, (own_width, own_width), lambda _, ref, at=first - kind: (0, at))
            )
    keep, send = call(
        norm_grad_kernel,
        index,
        [whole(item) for item in mixed_grads]
        + weight_items
        + [whole(item) for item in [after(gains[0], keep), norm_grad]],
        reduced,
        scratch=[pltpu.VMEM((total, width), f32)],
        flops=2 * total * width * 3 * own_width,
    )
    near = swap(send, 1)
    combined = (keep[1] + near[1].astype(f32)).astype(bf16)
    away = swap(combined, 2)
    down_at = rows * width // 128 // own_width
    down_block = lambda *_: (down_at, 0)
    tokens_grad = call(
        finish_kernel,
        index,
        [
            whole(item)
            for item in [
                keep,
                near,
                away,
                part_rows(first_inner_grad, wa, rows),
                part_rows(second_inner_grad, wa, rows),
            ]
        ]
        + [whole(qkv_down)]
        + [(item, (own_width, ADAPT_COLS), down_block) for item in first_packs]
        + in_downs
        + [whole(item) for item in [gains[0], gains[2], tokens[0], cotangent[0]]],
        [((rows, width), f32, None, None)],
        scratch=[pltpu.VMEM((rows, width), f32)],
    )[0][None]

    packed = pack_grads(dense_down_grad, first_norm, first_inner_grad, dense_inner, up_parts)
    packed = exchange_sum(after(packed, feed_sum))
    packed = jnp.concatenate([feed_sum, packed], axis=0)
    packed = lax.all_gather(packed, "ctx", axis=0)
    packed = after(packed, tokens_grad, output)
    down_shape = ((own_width, ADAPT_COLS), f32, None, None)
    up_shape = ((part_cols, width), f32, None, None)
    (
        out_down_grad,
        in_down_grad,
        out_up_grad,
        in_up_grad,
        dense_down_grad,
        qkv_down_grad,
        dense_up_grad,
        qkv_up_grad,
    ) = call(
        functools.partial(unpack_grads_kernel, feed_sum.shape[0]),
        index,
        [whole(packed)],
        [
            ((hidden_width, ADAPT_COLS), f32, None, None),
            down_shape,
            up_shape,
            ((part_cols, WA * hidden_width), f32, None, None),
            down_shape,
            down_shape,
            up_shape,
            ((part_cols, 3 * width), f32, None, None),
        ],
    )
    return (
        output,
        tokens_grad,
        qkv_down_grad,
        qkv_up_grad,
        dense_down_grad,
        dense_up_grad,
        in_down_grad,
        in_up_grad,
        out_down_grad,
        out_up_grad,
    )


def solution(mesh):
    rows = P("wa", "ctx", None)
    shard = P("wa", None)
    in_specs = (
        (rows, rows, P(), shard, shard)
        + (P(),) * 4
        + (shard, P()) * 4
        + (shard,) * 8
    )
    out_specs = (rows, rows) + (shard,) * 8
    return jax.shard_map(
        functools.partial(body, mesh.shape["ctx"]),
        mesh=mesh,
        in_specs=in_specs,
        out_specs=out_specs,
        check_vma=False,
    )
```

```python
import functools
import math

import jax
import jax.numpy as jnp
from jax import lax
from jax.experimental import pallas as pl
from jax.experimental.pallas import tpu as pltpu
from jax.sharding import PartitionSpec as P

HEADS = 8
HEAD = 256
ROT = 64
RANK = 16
BLOCK = 64
ADAPT_COLS = 128
WA = 4
PAIRS = 8
VMEM_BYTES = 58 * 1024 * 1024

epsilon = 1e-05
masked_score = -1e30
f32 = jnp.float32
bf16 = jnp.bfloat16


def product(left, right):
    return jnp.dot(left, right, preferred_element_type=f32)


def times_t(left, right):
    return lax.dot_general(left, right, (((1,), (1,)), ((), ())), preferred_element_type=f32)


def t_times(left, right):
    return lax.dot_general(left, right, (((0,), (0,)), ((), ())), preferred_element_type=f32)


def swap(value, bits):
    return lax.ppermute(value, "wa", [(i, i ^ bits) for i in range(WA)])


def after(value, *earlier):
    return lax.optimization_barrier((value, *earlier))[0]


def absolute(pieces, wa):
    low = wa % 2 == 1
    high = wa >= 2
    p = [
        jnp.where(low, pieces[1], pieces[0]),
        jnp.where(low, pieces[0], pieces[1]),
        jnp.where(low, pieces[3], pieces[2]),
        jnp.where(low, pieces[2], pieces[3]),
    ]
    return [
        jnp.where(high, p[2], p[0]),
        jnp.where(high, p[3], p[1]),
        jnp.where(high, p[0], p[2]),
        jnp.where(high, p[1], p[3]),
    ]


def rotary_tables(offset):
    half = ROT // 2
    lane = jnp.arange(128, dtype=jnp.int32)
    freq = 10000.0 ** (-2.0 * (lane % half).astype(f32) / ROT)
    freq = jnp.where(lane < ROT, freq, 0.0)
    angle = offset.astype(f32)[:, None] * freq[None, :]
    sign = jnp.where(lane < half, -1.0, 1.0)
    return jnp.cos(angle), jnp.sin(angle) * sign[None, :]


def turn_first(values, cosine, sine):
    lane = lax.broadcasted_iota(jnp.int32, values.shape, 1)
    partner = jnp.where(
        lane < ROT // 2, pltpu.roll(values, 128 - ROT // 2, 1), pltpu.roll(values, ROT // 2, 1)
    )
    return values * cosine + partner * sine


def call(kernel, index, inputs, outputs, grid=(1,), scratch=(), flops=0, name=None):
    def spec(shape, block, where):
        if where is None:
            zeros = (0,) * len(shape)
            return pl.BlockSpec(shape, lambda *_: zeros)
        return pl.BlockSpec(block, where)

    size = sum(a.size * a.dtype.itemsize if w is None else math.prod(i or 1 for i in b) * 2 * math.prod(grid)
               for a, b, w in inputs)
    return pl.pallas_call(
        kernel,
        grid_spec=pltpu.PrefetchScalarGridSpec(
            num_scalar_prefetch=1,
            grid=grid,
            in_specs=[spec(a.shape, b, w) for a, b, w in inputs],
            out_specs=[spec(s, b, w) for s, _, b, w in outputs],
            scratch_shapes=list(scratch),
        ),
        out_shape=[jax.ShapeDtypeStruct(s, d) for s, d, _, _ in outputs],
        compiler_params=pltpu.CompilerParams(vmem_limit_bytes=VMEM_BYTES),
        cost_estimate=pl.CostEstimate(flops=flops, bytes_accessed=size, transcendentals=0),
    )(index, *[a for a, _, _ in inputs])


def whole(array):
    return (array, None, None)


def copy_kernel(index_ref, *refs):
    count = len(refs) // 2
    for source, target in zip(refs[:count], refs[count:]):
        target[...] = source[...].reshape(target.shape)


def cut_columns(index, weight, size, kinds, cuts, parts=1):
    rows = weight.shape[0]
    part = size // parts
    inputs, outputs = [], []
    for r, division, number in cuts:
        height = rows // division

        def where(slot, t, ref, r=r, number=number):
            kind = sum(kind * (slot == i) for i, kind in enumerate(kinds))
            return (0 if number is None else ref[number], (kind * WA + ref[r]) * parts + t)

        inputs.append((weight, (height, part), where))
        outputs.append(
            (
                (height, len(kinds) * size),
                weight.dtype,
                (height, part),
                lambda slot, t, ref: (0, slot * parts + t),
            )
        )
    return call(copy_kernel, index, inputs, outputs, grid=(len(kinds), parts))


def strips(value):
    return [value[:, i : i + 128] for i in range(0, value.shape[1], 128)]


def store_strips(target, first, value):
    for item in strips(value):
        target[first : first + item.shape[0], :] = item
        first += item.shape[0]
    return first


def pack_kernel(index_ref, *refs):
    plain, last_ref = refs[:-6], refs[-6]
    (ups_mate, ups_peer, ups_far), (away_ref, near_ref) = refs[-5:-2], refs[-2:]
    first = 0
    for ref in plain:
        store_strips(away_ref, first, ref)
        first = store_strips(near_ref, first, ref)
    blank = ups_peer.shape[0] * ups_peer.shape[1] // 128
    store_strips(near_ref, first, ups_mate)
    store_strips(near_ref, first + blank, ups_mate)
    store_strips(away_ref, first, ups_peer)
    store_strips(away_ref, first + blank, ups_far)
    store_strips(near_ref, first + 2 * blank, last_ref)
    store_strips(away_ref, first + 2 * blank, last_ref)


def pack_small(index, plain, up, kinds, last):
    block = up.shape[1] // len(kinds) // WA
    items = [whole(item) for item in plain + [last]]
    size = sum(item.size for item in plain) // 128
    ups = up.shape[0] * block * len(kinds) // 128
    cut = jnp.concatenate if len(kinds) > 1 else (lambda v, axis: v[0])
    for r in (1, 2, 3):
        items.append(
            whole(
                cut(
                    [
                        lax.dynamic_slice_in_dim(up, (kind * WA + index[r]) * block, block, axis=1)
                        for kind in kinds
                    ],
                    axis=1,
                )
            )
        )
    shape = (size + 2 * ups + last.shape[0], 128)
    return call(pack_kernel, index, items, [(shape, bf16, None, None)] * 2)


def front_kernel(index_ref, *refs):
    token_ref, down_ref = refs[:2]
    packs = refs[2:5]
    mask_ref, g1, b1, g2, b2, first_ref, second_ref, inner_ref = refs[5:]
    rows, width = token_ref.shape
    wide = down_ref.shape[0]
    step = 32
    for r in range(WA):
        base = pl.multiple_of(index_ref[r] * rows, rows)
        for start in range(0, rows, step):
            if r == 0:
                values = token_ref[start : start + step, :]
            else:
                values = jnp.concatenate(
                    [
                        packs[r - 1][i * rows + start : i * rows + start + step, :]
                        for i in range(width // 128)
                    ],
                    axis=1,
                )
            values = values.astype(f32)
            centered = values - jnp.mean(values, axis=1, keepdims=True)
            spread = jnp.mean(centered * centered, axis=1, keepdims=True)
            normal = centered * lax.rsqrt(spread + epsilon)
            first_ref[pl.ds(base + start, step), :] = (normal * g1[...] + b1[...]).astype(bf16)
            second_ref[pl.ds(base + start, step), :] = (normal * g2[...] + b2[...]).astype(bf16)
    total = 0.0
    first = rows * width // 128
    for r in range(WA):
        columns = pl.ds(pl.multiple_of(index_ref[r] * wide, wide), wide)
        down = down_ref[...] if r == 0 else packs[r - 1][first : first + wide, :]
        total += product(first_ref[:, columns], down)
    inner_ref[...] = (total * mask_ref[...]).astype(bf16)


def pieces_of(index_ref, refs):
    wide = refs[0].shape[0]
    pieces = []
    for r, ref in enumerate(refs):
        size = ref.shape[0]
        first = index_ref[r] * wide
        if len(refs) > WA and r >= 2:
            first = index_ref[2 + (r - 2) // 2] * wide + (r % 2) * size
        pieces.append((pl.ds(pl.multiple_of(first, size), size), ref))
    return pieces


def read(ref):
    return ref[...].reshape(ref.shape[-2:])


def join_ups(index_ref, ups, joined):
    size = ADAPT_COLS // WA
    for r, ref in enumerate(ups):
        first = pl.multiple_of(index_ref[r] * size, size)
        if ref.shape[-1] == joined.shape[-1]:
            joined[pl.ds(first, size), :] = read(ref)
        else:
            for i in range(joined.shape[-1] // 128):
                joined[pl.ds(first, size), i * 128 : (i + 1) * 128] = ref[
                    i * size : (i + 1) * size, :
                ]


def qkv_kernel(turned, index_ref, hidden_ref, *refs):
    weights, ups = refs[:4], refs[4:8]
    inner_ref, bias_ref, cos_ref, sin_ref, out_ref, joined = refs[8:]
    join_ups(index_ref, ups, joined)
    total = product(inner_ref[...], joined[...]) + bias_ref[...]
    for columns, ref in pieces_of(index_ref, weights):
        total += product(hidden_ref[:, columns], read(ref))
    shape = out_ref.shape
    if turned:
        first = turn_first(total[:, :128], cos_ref[...], sin_ref[...])
        out_ref[..., :128] = first.astype(bf16).reshape(shape[:-1] + (128,))
        out_ref[..., 128:] = total[:, 128:].astype(bf16).reshape(shape[:-1] + (HEAD - 128,))
    else:
        out_ref[...] = total.astype(bf16).reshape(shape)


def grad_kernel(index_ref, *refs):
    parts = refs[:WA]
    mask_ref, weight_ref, down_ref = refs[WA : WA + 3]
    grad_ref, dense_ref, out_ref, heads_ref, ups_ref, dense_joined, out_joined = refs[WA + 3 :]
    size = ADAPT_COLS // WA
    rows = parts[0].shape[0] - 2 * size
    for r in range(WA):
        first = pl.ds(pl.multiple_of(index_ref[r] * size, size), size)
        dense_joined[first, :] = parts[r][rows : rows + size, :]
        out_joined[first, :] = parts[r][rows + size :, :]
        grad_ref[pl.ds(pl.multiple_of(index_ref[r] * rows, rows), rows), :] = parts[r][:rows, :]
    ups_ref[0] = dense_joined[...]
    ups_ref[1] = out_joined[...]
    grad = grad_ref[...]
    dense = (times_t(grad, dense_joined[...]) * mask_ref[...]).astype(bf16)
    dense_ref[...] = dense
    out_ref[...] = (times_t(grad, out_joined[...]) * mask_ref[...]).astype(bf16)
    for head in range(2):
        span = slice(head * HEAD, (head + 1) * HEAD)
        total = times_t(grad, weight_ref[span, :]) + times_t(dense, down_ref[span, :])
        heads_ref[:, head] = total.astype(bf16).reshape(WA, rows, HEAD)


def gelu_parts(values):
    bell = jnp.exp(-0.5 * values * values)
    t = 1.0 / (1.0 + (0.3275911 * math.sqrt(0.5)) * jnp.abs(values))
    series = 1.061405429 * 0.5
    for factor in (-1.453152027, 1.421413741, -0.284496736, 0.254829592):
        series = series * t + 0.5 * factor
    tail = series * t * bell
    below = jnp.where(values > 0, 1.0 - tail, tail)
    return values * below, below + values * bell * (1.0 / math.sqrt(2.0 * math.pi))


def feed_kernel(starts, ends, index_ref, hidden_ref, grad_ref, *refs):
    weights, ups, refs = refs[:6], refs[6:10], refs[10:]
    if starts:
        downs, mask_ref, refs = refs[:4], refs[4], refs[5:]
    else:
        known_ref, refs = refs[0], refs[1:]
    bias_ref, gain_ref, out_w_ref, out_down_ref, out_inner_grad_ref = refs[:5]
    (
        out_ref,
        norm_grad_ref,
        out_inner_ref,
        inner_grad_ref,
        out_down_grad_ref,
        *in_up_grad_refs,
        inner_ref,
        joined,
        up_grad,
    ) = refs[5:]
    step = pl.program_id(0)

    @pl.when(step == 0)
    def _():
        if starts:
            wide = downs[0].shape[0]
            total = 0.0
            for r in range(WA):
                columns = pl.ds(pl.multiple_of(index_ref[r] * wide, wide), wide)
                total += product(hidden_ref[:, columns], downs[r][...])
            inner_ref[...] = (total * mask_ref[...]).astype(bf16)
        else:
            inner_ref[...] = known_ref[...]
        out_ref[...] = jnp.zeros_like(out_ref)
        norm_grad_ref[...] = jnp.zeros_like(norm_grad_ref)
        out_inner_ref[...] = jnp.zeros_like(out_inner_ref)
        inner_grad_ref[...] = jnp.zeros_like(inner_grad_ref)

    join_ups(index_ref, ups, joined)
    pre = product(inner_ref[...], joined[...]) + bias_ref[...]
    for columns, ref in pieces_of(index_ref, weights):
        pre += product(hidden_ref[:, columns], read(ref))
    units, slope = gelu_parts(pre)
    units = units.astype(bf16)
    pre_grad = times_t(grad_ref[...], out_w_ref[...]) + times_t(
        out_inner_grad_ref[...], out_down_ref[...]
    )
    pre_grad = (pre_grad * slope).astype(bf16)
    out_ref[...] += product(units, out_w_ref[...])
    for columns, ref in pieces_of(index_ref, weights):
        norm_grad_ref[:, columns] += times_t(pre_grad, read(ref))
    out_inner_ref[...] += product(units, out_down_ref[...])
    inner_grad_ref[...] += times_t(pre_grad, joined[...])
    out_down_grad_ref[...] = t_times(units, out_inner_grad_ref[...]).astype(bf16)
    up_grad[...] = t_times(inner_ref[...], pre_grad)
    size = ADAPT_COLS // WA
    for r, ref in enumerate(in_up_grad_refs):
        first = pl.multiple_of(index_ref[r] * size, size)
        ref[...] = up_grad[pl.ds(first, size), :].astype(bf16)

    @pl.when(step == pl.num_programs(0) - 1)
    def _():
        norm_grad_ref[...] = norm_grad_ref[...] * gain_ref[...]


def scatter_rows(index_ref, total_ref, keep_ref, send_ref):
    rows = keep_ref.shape[1]
    for r, (ref, slot) in enumerate(((keep_ref, 0), (send_ref, 0), (keep_ref, 1), (send_ref, 1))):
        part = total_ref[pl.ds(pl.multiple_of(index_ref[r] * rows, rows), rows), :]
        ref[slot] = part.astype(ref.dtype)


def head_rows(ref, head):
    return ref[:, head, 0].reshape(-1, HEAD)


def dense_kernel(
    index_ref,
    heads_ref,
    sum_ref,
    weight_ref,
    down_ref,
    inner_grad_ref,
    keep_ref,
    send_ref,
    inner_ref,
    down_grad_ref,
    total,
):
    result = sum_ref[...]
    inner = 0.0
    for head in range(2):
        span = slice(head * HEAD, (head + 1) * HEAD)
        heads = head_rows(heads_ref, head)
        result += product(heads, weight_ref[span, :])
        inner += product(heads, down_ref[span, :])
        down_grad_ref[span, :] = t_times(heads, inner_grad_ref[...]).astype(bf16)
    inner_ref[...] = inner
    total[...] = result
    scatter_rows(index_ref, total, keep_ref, send_ref)


def mixed_rows(query_grad_ref, key_grad_ref, kind, head):
    if kind == 0:
        return query_grad_ref[:, head, 1].reshape(-1, HEAD)
    return key_grad_ref[:, head, kind + 1].reshape(-1, HEAD)


def mix_kernel(index_ref, *refs):
    grads, ups = refs[:2], refs[2 : 2 + 3 * WA]
    inner_ref, inner_grad_ref, up_grad_ref, joined = refs[2 + 3 * WA :]
    width = 2 * HEAD
    for kind in range(3):
        for r in range(WA):
            size = ADAPT_COLS // WA
            first = pl.multiple_of(index_ref[r] * size, size)
            ref = ups[kind * WA + r]
            if r == 0:
                joined[kind, pl.ds(first, size), :] = ref[...]
            else:
                for i in range(width // 128):
                    joined[kind, pl.ds(first, size), i * 128 : (i + 1) * 128] = ref[
                        i * size : (i + 1) * size, :
                    ]
    total = 0.0
    for kind in range(3):
        for head in range(2):
            span = slice(head * HEAD, (head + 1) * HEAD)
            rows = mixed_rows(*grads, kind, head)
            total += times_t(rows, joined[kind, :, span])
            out = slice(kind * width + head * HEAD, kind * width + (head + 1) * HEAD)
            up_grad_ref[:, out] = t_times(inner_ref[...], rows).astype(bf16)
    inner_grad_ref[...] = total


def norm_grad_kernel(index_ref, *refs):
    grads, weights = refs[:2], refs[2:14]
    gain_ref, sum_ref, keep_ref, send_ref, total = refs[14:]
    sets = [pieces_of(index_ref, weights[WA * kind : WA * kind + WA]) for kind in range(3)]
    rows = [[mixed_rows(*grads, kind, head) for head in range(2)] for kind in range(3)]
    for piece in range(WA):
        columns = sets[0][piece][0]
        part = 0.0
        for kind in range(3):
            weight = read(sets[kind][piece][1])
            for head in range(2):
                part += times_t(rows[kind][head], weight[:, head * HEAD : (head + 1) * HEAD])
        total[:, columns] = part * gain_ref[:, columns] + sum_ref[:, columns]
    scatter_rows(index_ref, total, keep_ref, send_ref)


def own_rows_of(inner, grad, index_ref, total):
    size = ADAPT_COLS // WA
    total[...] = t_times(inner, grad)
    return total[pl.ds(pl.multiple_of(index_ref[0] * size, size), size), :].astype(bf16)


def pack_grads_kernel(index_ref, *refs):
    down_ref, norm_ref, norm_grad_ref, inner_ref, grad_ref = refs[:5]
    ups, (packed_ref, total) = refs[5:9], refs[9:]
    at = down_ref.shape[0]
    packed_ref[:at, :] = down_ref[...]
    part = t_times(norm_ref[...], norm_grad_ref[...]).astype(bf16)
    packed_ref[at : at + part.shape[0], :] = part
    at += part.shape[0]
    at = store_strips(packed_ref, at, own_rows_of(inner_ref[...], grad_ref[...], index_ref, total))
    for ref in ups:
        at = store_strips(packed_ref, at, ref)


def unpack_grads_kernel(feed_size, index_ref, source_ref, *refs):
    packed = source_ref[...]
    size = ADAPT_COLS // WA
    for outs, start, end in ((refs[:4], 0, feed_size), (refs[4:], feed_size, packed.shape[1])):
        part = packed[:, start:end].reshape(-1, ADAPT_COLS)
        down_ref, norm_ref, inner_ref, up_ref = outs
        at = 0
        for ref in (down_ref, norm_ref):
            ref[...] = part[at : at + ref.shape[0], :].astype(f32)
            at += ref.shape[0]
        for i in range(inner_ref.shape[1] // 128):
            inner_ref[:, i * 128 : (i + 1) * 128] = part[at : at + size, :].astype(f32)
            at += size
        kinds = 3 if start else 1
        width = up_ref.shape[1] // kinds
        block = width // WA
        for r in range(WA):
            for kind in range(kinds):
                for i in range(block // 128):
                    first = kind * width + index_ref[r] * block + i * 128
                    columns = pl.ds(pl.multiple_of(first, 128), 128)
                    up_ref[:, columns] = part[at : at + size, :].astype(f32)
                    at += size


def finish_kernel(index_ref, *refs):
    keep_ref, near_ref, away_ref, first_ref, second_ref = refs[:5]
    first_downs, second_downs = refs[5:9], refs[9:13]
    g1, g2, token_ref, grad_ref, out_ref, total = refs[13:]
    total[...] = keep_ref[0] + near_ref[0].astype(f32) + away_ref[...].astype(f32)
    wide = first_downs[0].shape[0]
    for r in range(WA):
        columns = pl.ds(pl.multiple_of(index_ref[r] * wide, wide), wide)
        total[:, columns] += (
            times_t(first_ref[...], first_downs[r][...]) * g1[:, columns]
            + times_t(second_ref[...], second_downs[r][...]) * g2[:, columns]
        )
    step = 32
    for start in range(0, total.shape[0], step):
        span = slice(start, start + step)
        values = token_ref[span, :].astype(f32)
        centered = values - jnp.mean(values, axis=1, keepdims=True)
        rstd = lax.rsqrt(jnp.mean(centered * centered, axis=1, keepdims=True) + epsilon)
        normal = centered * rstd
        part = total[span, :]
        part = (
            part
            - jnp.mean(part, axis=1, keepdims=True)
            - normal * jnp.mean(part * normal, axis=1, keepdims=True)
        )
        out_ref[span, :] = grad_ref[span, :].astype(f32) + rstd * part


def attention_kernel(
    joint,
    query_ref,
    key_ref,
    value_ref,
    grad_ref,
    begin_ref,
    place_ref,
    key_place_ref,
    q_cos_ref,
    q_sin_ref,
    k_cos_ref,
    k_sin_ref,
    rows_ref,
    *refs,
):
    keys_ref, dk_sum, dv_sum = (rows_ref, *refs) if joint else refs
    step = pl.program_id(0)
    scale = 1.0 / math.sqrt(HEAD)

    @pl.when(step == 0)
    def _():
        dk_sum[...] = jnp.zeros_like(dk_sum)
        dv_sum[...] = jnp.zeros_like(dv_sum)

    query = query_ref[...].reshape(-1, HEAD)
    key = key_ref[...].reshape(-1, HEAD)
    value = value_ref[...]
    grad = grad_ref[...]
    key_place = key_place_ref[...]
    allowed = (key_place >= begin_ref[...]) & (key_place <= place_ref[...])
    scores = jnp.where(allowed, times_t(query, key) * scale, masked_score)
    top = jnp.max(scores, axis=1, keepdims=True)
    weights = jnp.exp(scores - top)
    prob = weights * (1.0 / jnp.sum(weights, axis=1, keepdims=True))
    prob_low = prob.astype(bf16)
    part, block = query.shape[0], rows_ref.shape[2]
    shape = (part // block, block)
    own = pl.ds(step * shape[0], shape[0]) if joint else slice(None)
    rows_ref[own, 0] = product(prob_low, value).astype(bf16).reshape(shape + (HEAD,))
    prob_grad = times_t(grad, value)
    delta = jnp.sum(prob * prob_grad, axis=1, keepdims=True)
    score_grad = (prob * (prob_grad - delta)).astype(bf16)
    dq = product(score_grad, key) * scale
    first = turn_first(dq[:, :128], q_cos_ref[...], -q_sin_ref[...])
    rows_ref[own, 1, :, :128] = first.astype(bf16).reshape(shape + (128,))
    rows_ref[own, 1, :, 128:] = dq[:, 128:].astype(bf16).reshape(shape + (HEAD - 128,))
    dk_sum[...] += t_times(score_grad, query)
    dv_sum[...] += t_times(prob_low, grad)

    @pl.when(step == pl.num_programs(0) - 1)
    def _():
        base = 2 if joint else 0
        shape = keys_ref.shape[:1] + keys_ref.shape[2:3]
        dk = dk_sum[...] * scale
        first = turn_first(dk[:, :128], k_cos_ref[...], -k_sin_ref[...])
        keys_ref[:, base, :, :128] = first.astype(bf16).reshape(shape + (128,))
        keys_ref[:, base, :, 128:] = dk[:, 128:].astype(bf16).reshape(shape + (HEAD - 128,))
        keys_ref[:, base + 1] = dv_sum[...].astype(bf16).reshape(shape + (HEAD,))


def attend(query, key, value, grad, begin, place, key_place, q_tables, k_tables, block):
    rows = query.shape[0] * block
    keys = key.shape[0] * block
    part = min(256, rows)
    joint = rows == keys
    by_rows = lambda i: (i, 0)
    all_rows = lambda i: (0, 0)
    fixed = lambda i: (0, 0, 0, 0)
    if joint:
        shapes = [(keys // block, 4, block, HEAD)]
        out_specs = [pl.BlockSpec(shapes[0], fixed)]
    else:
        shapes = [(rows // block, 2, block, HEAD), (keys // block, 2, block, HEAD)]
        out_specs = [
            pl.BlockSpec((part // block, 2, block, HEAD), lambda i: (i, 0, 0, 0)),
            pl.BlockSpec(shapes[1], fixed),
        ]
    return pl.pallas_call(
        functools.partial(attention_kernel, joint),
        grid=(rows // part,),
        in_specs=[
            pl.BlockSpec((part // block, 1, block, HEAD), lambda i: (i, 1, 0, 0)),
            pl.BlockSpec((keys // block, 1, block, HEAD), fixed),
            pl.BlockSpec((keys, HEAD), all_rows),
            pl.BlockSpec((part, HEAD), by_rows),
            pl.BlockSpec((part, 1), by_rows),
            pl.BlockSpec((part, 1), by_rows),
            pl.BlockSpec((1, keys), all_rows),
            pl.BlockSpec((part, 128), by_rows),
            pl.BlockSpec((part, 128), by_rows),
            pl.BlockSpec((keys, 128), all_rows),
            pl.BlockSpec((keys, 128), all_rows),
        ],
        out_specs=out_specs,
        out_shape=[jax.ShapeDtypeStruct(shape, bf16) for shape in shapes],
        scratch_shapes=[pltpu.VMEM((keys, HEAD), f32), pltpu.VMEM((keys, HEAD), f32)],
        compiler_params=pltpu.CompilerParams(vmem_limit_bytes=VMEM_BYTES),
        cost_estimate=pl.CostEstimate(
            flops=14 * rows * keys * HEAD,
            bytes_accessed=16 * keys * HEAD,
            transcendentals=rows * keys,
        ),
    )(query, key, value, grad, begin, place, key_place, *q_tables, *k_tables)


def body(
    contexts,
    tokens,
    cotangent,
    deal,
    doc_lengths,
    doc_adapter,
    ln1_gain,
    ln1_bias,
    ln2_gain,
    ln2_bias,
    qkv_weight,
    qkv_bias,
    dense_weight,
    dense_bias,
    in_weight,
    in_bias,
    out_weight,
    out_bias,
    qkv_down,
    qkv_up,
    dense_down,
    dense_up,
    in_down,
    in_up,
    out_down,
    out_up,
):
    rows = tokens.shape[1]
    width = tokens.shape[2]
    wa = lax.axis_index("wa")
    ctx = lax.axis_index("ctx")
    total = WA * rows
    own_width = width // WA
    hidden_width = in_weight.shape[1] // WA
    part_cols = ADAPT_COLS // WA
    groups = contexts // PAIRS
    half = own_width // 2
    relative = [wa, wa ^ 1, wa ^ 2, wa ^ 3]
    index = jnp.stack(relative + [ctx % 2, ctx, wa * 0, wa * 0 + 1]).astype(jnp.int32)

    def columns(value, which, size):
        return lax.dynamic_slice_in_dim(value, which * size, size, axis=1)

    def part_rows(value, which, size):
        return lax.dynamic_slice_in_dim(value, which * size, size, axis=0)

    limit = 64
    numbers = jnp.concatenate(
        [doc_lengths // limit, doc_lengths % limit, doc_adapter], axis=1
    ).astype(bf16)
    numbers = jnp.pad(numbers, ((0, 15), (0, 128 - numbers.shape[1])))
    first_pack = pack_small(index, [tokens[0], qkv_down], qkv_up, [0, 1, 2], numbers)

    def gather_rows(weight, size, kinds, *earlier):
        cuts = cut_columns(index, weight, size, kinds, [(2, contexts, 5), (3, contexts, 5)])
        parts = [swap(cuts[0], 2), swap(cuts[1], 3)]
        part = after(jnp.concatenate(parts, axis=1), *earlier)
        return part, lax.all_gather(part, "ctx", axis=0, tiled=True)

    qkv_others_part, qkv_others = gather_rows(qkv_weight, own_width, [2, 1, 0], *first_pack)
    in_cuts = cut_columns(
        index,
        in_weight,
        hidden_width,
        [0],
        [(2, 2, 6), (2, 2, 7), (3, 2, 6), (3, 2, 7)],
        4,
    )
    in_parts = [swap(after(in_cuts[0], qkv_others_part), 2)]
    def hand_on(away, near, *earlier):
        peer = swap(after(away, *earlier), 2)
        return [swap(near, 1), peer, swap(peer, 1)]

    mate_cuts = cut_columns(index, qkv_weight, own_width, [2, 1, 0], [(1, 1, None)])[0]
    in_mate_cut = cut_columns(index, in_weight, hidden_width, [0], [(1, 1, None)], 2)[0]
    first_packs = hand_on(*first_pack)
    grad_pack = jnp.concatenate([cotangent[0], dense_up, out_up], axis=0)
    grad_packs = hand_on(grad_pack, grad_pack, first_packs[1])
    mate_weights = swap(after(mate_cuts, first_packs[0]), 1)
    feed_pack = pack_small(index, [in_down], in_up, [0], numbers)
    feed_packs = hand_on(*feed_pack, grad_packs[1])

    docs_per_pack = doc_lengths.shape[1]
    tables = [numbers] + [item[-16:] for item in first_packs]
    tables = jnp.stack(absolute([item[0] for item in tables], wa)).astype(jnp.int32)
    lengths = tables[:, :docs_per_pack] * limit + tables[:, docs_per_pack : 2 * docs_per_pack]
    adapters = tables[:, 2 * docs_per_pack : 3 * docs_per_pack]
    starts = jnp.cumsum(lengths, axis=1) - lengths

    def places(first, size):
        slots = first + jnp.arange(size, dtype=jnp.int32)
        blocks = slots // BLOCK
        table = jnp.arange(deal.shape[0], dtype=jnp.int32)
        block = jnp.sum(jnp.where(table[None, :] == blocks[:, None], deal[None, :], 0), axis=1)
        return block * BLOCK + slots % BLOCK

    place = places(ctx * rows, rows)
    inside = starts[:, None, :] <= place[None, :, None]
    docs = jnp.sum(inside.astype(jnp.int32), axis=2) - 1
    begin = jnp.max(jnp.where(inside, starts[:, None, :], 0), axis=2)
    offset = (place[None, :] - begin).reshape(total)
    doc_table = jnp.arange(docs_per_pack, dtype=jnp.int32)
    chosen = jnp.sum(
        jnp.where(docs[:, :, None] == doc_table, adapters[:, None, :], 0), axis=2
    ).reshape(total)
    adapter_of = jnp.arange(ADAPT_COLS, dtype=jnp.int32) // RANK
    mask = (adapter_of[None, :] == chosen[:, None]).astype(f32)
    cosine, sine = rotary_tables(offset)

    gains = [item[None, :] for item in (ln1_gain, ln1_bias, ln2_gain, ln2_bias)]
    first_norm, second_norm, first_inner = call(
        front_kernel,
        index,
        [whole(item) for item in [after(tokens[0], in_parts[0], *feed_pack), qkv_down] + first_packs + [mask] + gains],
        [
            ((total, width), bf16, None, None),
            ((total, width), bf16, None, None),
            ((total, ADAPT_COLS), bf16, None, None),
        ],
        flops=2 * total * width * ADAPT_COLS,
    )

    strip = strip_rows = part_cols * HEAD // 128
    ups_row = (tokens.size + qkv_down.size) // 128
    ups_size = 3 * own_width * part_cols // 128

    def project(last, kinds, turned):
        own_block = lambda i, head, ref: (0, ((last - i) * WA + ref[0]) * 2 + head)
        items = [whole(first_norm), (qkv_weight, (own_width, HEAD), own_block)]
        for item, first in ((mate_weights, 0), (qkv_others, 0), (qkv_others, 3)):
            first = (first + 2 - last) * 2
            items.append(
                (
                    item,
                    (own_width, HEAD),
                    lambda i, head, ref, first=first: (0, first + 2 * i + head),
                )
            )
        items.append((qkv_up, (part_cols, HEAD), own_block))
        for r, item in zip((1, 2, 3), first_packs):
            row = (ups_row + (r == 3) * ups_size) // strip + last * 2
            items.append(
                (item, (strip, 128), lambda i, head, ref, row=row: (row - 2 * i + head, 0))
            )
        items += [
            whole(first_inner),
            (qkv_bias[None, :], (1, HEAD), own_block),
            whole(cosine),
            whole(sine),
        ]
        out = call(
            functools.partial(qkv_kernel, turned),
            index,
            items,
            [
                (
                    (WA, 2, kinds, rows, HEAD),
                    bf16,
                    (WA, 1, 1, rows, HEAD),
                    lambda i, head, ref: (0, head, i, 0, 0),
                )
            ],
            grid=(kinds, 2),
            scratch=[pltpu.VMEM((ADAPT_COLS, HEAD), bf16)],
            flops=2 * total * width * own_width * kinds,
        )[0]
        return out.reshape(PAIRS, kinds, rows, HEAD)

    def to_pairs(item):
        if groups == 1:
            return lax.all_to_all(item, "ctx", 0, 0, tiled=True)
        names = [[g * PAIRS + j for j in range(PAIRS)] for g in range(groups)]
        return lax.all_to_all(item, "ctx", 0, 0, axis_index_groups=names, tiled=True)

    grad, dense_inner_grad, out_inner_grad, attended_grad, all_ups = call(
        grad_kernel,
        index,
        [
            whole(item)
            for item in [after(grad_pack, first_inner)] + grad_packs + [mask, dense_weight, dense_down]
        ],
        [
            ((total, width), bf16, None, None),
            ((total, ADAPT_COLS), bf16, None, None),
            ((total, ADAPT_COLS), bf16, None, None),
            ((WA, 2, rows, HEAD), bf16, None, None),
            ((2, ADAPT_COLS, width), bf16, None, None),
        ],
        scratch=[pltpu.VMEM((ADAPT_COLS, width), bf16), pltpu.VMEM((ADAPT_COLS, width), bf16)],
        flops=2 * total * width * (own_width + 2 * ADAPT_COLS),
    )
    attended_grad = to_pairs(attended_grad.reshape(PAIRS, rows, HEAD))
    in_parts.append(swap(after(in_cuts[1], grad_packs[1]), 2))
    qkv_others = after(qkv_others, first_norm, grad)
    value = to_pairs(after(project(2, 1, False), attended_grad))
    in_parts.append(swap(after(in_cuts[2], in_parts[1]), 3))
    pair_own = after(project(1, 2, True), value, in_parts[2])
    pair = to_pairs(pair_own)
    in_parts.append(swap(after(in_cuts[3], in_parts[2]), 3))

    tile = min(512, hidden_width)
    tiles = hidden_width // tile
    in_downs = [whole(in_down)] + [
        (item, (own_width, ADAPT_COLS), lambda *_: (0, 0)) for item in feed_packs
    ]

    in_mate = swap(after(in_mate_cut, pair_own), 1)

    def feed(part, known, norm, *earlier):
        count = tiles
        first = part * count
        own_tile = lambda t, ref: (0, ref[0] * tiles + first + t)
        strip = part_cols * tile // 128
        items = [whole(after(norm, *earlier)), whole(grad)]
        items += [
            (in_weight, (own_width, tile), own_tile),
            (in_mate, (own_width, tile), lambda t, ref: (0, first + t)),
        ]
        items += [
            (item, (own_width // 2, tile), lambda t, ref: (0, first + t)) for item in in_parts
        ]
        items.append((in_up, (part_cols, tile), own_tile))
        for r, item in zip((1, 2, 3), feed_packs):
            row = (own_width + (r == 3) * part_cols * hidden_width // 128) // strip + first
            items.append((item, (strip, 128), lambda t, ref, row=row: (row + t, 0)))
        items += in_downs + [whole(mask)] if known is None else [whole(known)]
        items += [
            (in_bias[None, :], (1, tile), own_tile),
            whole(gains[2]),
            (out_weight, (tile, width), lambda t, ref: (first + t, 0)),
            (out_down, (tile, ADAPT_COLS), lambda t, ref: (first + t, 0)),
            whole(out_inner_grad),
        ]
        size = count * tile
        return call(
            functools.partial(feed_kernel, known is None, True),
            index,
            items,
            [
                ((total, width), f32, None, None),
                ((total, width), f32, None, None),
                ((total, ADAPT_COLS), f32, None, None),
                ((total, ADAPT_COLS), f32, None, None),
                ((size, ADAPT_COLS), bf16, (tile, ADAPT_COLS), lambda t, ref: (t, 0)),
            ]
            + [((part_cols, size), bf16, (part_cols, tile), lambda t, ref: (0, t))] * WA
            + [((total, ADAPT_COLS), bf16, None, None)],
            grid=(count,),
            scratch=[pltpu.VMEM((ADAPT_COLS, tile), bf16), pltpu.VMEM((ADAPT_COLS, tile), f32)],
            flops=8 * total * width * size,
        )

    (
        branch_sum,
        norm_grad,
        out_inner,
        second_inner_grad,
        out_down_grad,
        *in_up_grads,
        second_inner,
    ) = feed(0, None, second_norm, pair)

    pair_rows = PAIRS * rows
    group = ctx // PAIRS
    own_pack = (ctx % PAIRS) // 2
    own_starts = jnp.sum(
        jnp.where(jnp.arange(WA)[:, None] == own_pack, starts, 0), axis=0
    )
    all_places = places(0, groups * pair_rows)
    all_inside = own_starts[None, :] <= all_places[:, None]
    all_begins = jnp.max(jnp.where(all_inside, own_starts[None, :], 0), axis=1)
    k_tables = rotary_tables(all_places - all_begins)
    if groups == 1:
        q_place, q_begin, q_tables = all_places, all_begins, k_tables
    else:
        q_place = part_rows(all_places, group, pair_rows)
        q_begin = part_rows(all_begins, group, pair_rows)
        q_tables = [part_rows(item, group, pair_rows) for item in k_tables]
    value, attended_grad = [item.reshape(pair_rows, HEAD) for item in (value, attended_grad)]
    key = pair
    sets = [[g * PAIRS + j for g in range(groups)] for j in range(PAIRS)]
    if groups > 1:
        key, value = [
            lax.all_gather(item, "ctx", axis=0, axis_index_groups=sets, tiled=True)
            for item in (pair[:, :1], value)
        ]
    both = attend(
        after(pair, in_mate, *feed_packs),
        key,
        value,
        attended_grad,
        q_begin[:, None],
        q_place[:, None],
        all_places[None, :],
        q_tables,
        k_tables,
        rows,
    )
    if groups > 1:
        dkv = lax.psum_scatter(
            both[1], "ctx", scatter_dimension=0, axis_index_groups=sets, tiled=True
        )
        both = [jnp.concatenate([both[0], dkv], axis=1)]
    both = to_pairs(after(both[0], in_parts[3])).reshape(WA, 2, 4, rows, HEAD)
    both = after(both, branch_sum)
    odq, dkv = both, both

    def sum_inner(partial):
        partial = (partial + swap(partial, 1)).astype(bf16)
        partial = partial.astype(f32) + swap(partial, 2).astype(f32)
        return (partial * mask).astype(bf16)

    def spread_rows(value):
        return [part_rows(value, wa, part_cols)] + [
            swap(part_rows(value, wa ^ r, part_cols), r) for r in (1, 2, 3)
        ]

    def exchange_sum(value):
        parts = value.reshape(contexts, -1, ADAPT_COLS)
        parts = lax.all_to_all(parts, "ctx", 0, 0, tiled=True)
        return jnp.sum(parts.astype(f32), axis=0).astype(bf16)

    def pack_grads(down_grad, norm, norm_grad, inner, ups):
        items = [whole(down_grad), (norm, (total, own_width), lambda _, ref: (0, ref[0]))]
        items += [whole(item) for item in [norm_grad, inner, grad] + ups]
        size = down_grad.size + own_width * ADAPT_COLS + part_cols * width
        size += sum(item.size for item in ups)
        return call(
            pack_grads_kernel,
            index,
            items,
            [((size // ADAPT_COLS, ADAPT_COLS), bf16, None, None)],
            scratch=[pltpu.VMEM((ADAPT_COLS, width), f32)],
        )[0]

    in_up_parts = in_up_grads[:1] + [swap(in_up_grads[r], r) for r in (1, 2, 3)]
    out_inner = sum_inner(out_inner)
    second_inner_grad = sum_inner(second_inner_grad)
    feed_packed = pack_grads(
        out_down_grad, second_norm, second_inner_grad, out_inner, in_up_parts
    )
    feed_sum = exchange_sum(after(feed_packed, both))
    odq = dkv = after(both, feed_packed)

    mixed_grads = [odq, dkv]
    up_items = []
    for kind in range(3):
        up_items.append(
            (qkv_up, (part_cols, own_width), lambda _, ref, kind=kind: (0, kind * WA + ref[0]))
        )
        for r, item in zip((1, 2, 3), first_packs):
            row = (ups_row + (r == 3) * ups_size) // (2 * strip_rows) + kind
            up_items.append(
                (item, (2 * strip_rows, 128), lambda _, ref, row=row: (row, 0))
            )
    mixed_inner, qkv_up_grad = call(
        mix_kernel,
        index,
        [whole(item) for item in mixed_grads] + up_items + [whole(first_inner)],
        [
            ((total, ADAPT_COLS), f32, None, None),
            ((ADAPT_COLS, 3 * own_width), bf16, None, None),
        ],
        scratch=[pltpu.VMEM((3, ADAPT_COLS, own_width), bf16)],
        flops=4 * total * ADAPT_COLS * 3 * own_width,
    )
    first_inner_grad = sum_inner(mixed_inner)
    up_parts = spread_rows(qkv_up_grad)
    dense_items = [after(odq, mixed_inner), branch_sum, dense_weight, dense_down, dense_inner_grad]
    reduced = [
        ((2, rows, width), f32, None, None),
        ((2, rows, width), bf16, None, None),
    ]
    keep, send, dense_inner, dense_down_grad = call(
        dense_kernel,
        index,
        [whole(item) for item in dense_items],
        reduced
        + [
            ((total, ADAPT_COLS), f32, None, None),
            ((own_width, ADAPT_COLS), bf16, None, None),
        ],
        scratch=[pltpu.VMEM((total, width), f32)],
        flops=2 * total * width * own_width,
    )
    dense_inner = sum_inner(dense_inner)
    near = swap(send, 1)
    away = swap((keep[1] + near[1].astype(f32)).astype(bf16), 2)
    output = (
        keep[0]
        + near[0].astype(f32)
        + away.astype(f32)
        + product(part_rows(dense_inner, wa, rows), all_ups[0])
        + product(part_rows(out_inner, wa, rows), all_ups[1])
        + dense_bias
        + out_bias
        + tokens[0].astype(f32)
    ).astype(bf16)[None]

    weight_items = []
    for kind in range(3):
        weight_items.append(
            (
                qkv_weight,
                (own_width, own_width),
                lambda _, ref, kind=kind: (0, kind * WA + ref[0]),
            )
        )
        for item, first in ((mate_weights, 2), (qkv_others, 2), (qkv_others, 5)):
            weight_items.append(
                (item, (own_width, own_width), lambda _, ref, at=first - kind: (0, at))
            )
    keep, send = call(
        norm_grad_kernel,
        index,
        [whole(item) for item in mixed_grads]
        + weight_items
        + [whole(item) for item in [after(gains[0], keep), norm_grad]],
        reduced,
        scratch=[pltpu.VMEM((total, width), f32)],
        flops=2 * total * width * 3 * own_width,
    )
    near = swap(send, 1)
    combined = (keep[1] + near[1].astype(f32)).astype(bf16)
    away = swap(combined, 2)
    down_at = rows * width // 128 // own_width
    down_block = lambda *_: (down_at, 0)
    tokens_grad = call(
        finish_kernel,
        index,
        [
            whole(item)
            for item in [
                keep,
                near,
                away,
                part_rows(first_inner_grad, wa, rows),
                part_rows(second_inner_grad, wa, rows),
            ]
        ]
        + [whole(qkv_down)]
        + [(item, (own_width, ADAPT_COLS), down_block) for item in first_packs]
        + in_downs
        + [whole(item) for item in [gains[0], gains[2], tokens[0], cotangent[0]]],
        [((rows, width), f32, None, None)],
        scratch=[pltpu.VMEM((rows, width), f32)],
    )[0][None]

    packed = pack_grads(dense_down_grad, first_norm, first_inner_grad, dense_inner, up_parts)
    packed = exchange_sum(after(packed, feed_sum))
    packed = jnp.concatenate([feed_sum, packed], axis=0)
    packed = lax.all_gather(packed, "ctx", axis=0)
    packed = after(packed, tokens_grad, output)
    down_shape = ((own_width, ADAPT_COLS), f32, None, None)
    up_shape = ((part_cols, width), f32, None, None)
    (
        out_down_grad,
        in_down_grad,
        out_up_grad,
        in_up_grad,
        dense_down_grad,
        qkv_down_grad,
        dense_up_grad,
        qkv_up_grad,
    ) = call(
        functools.partial(unpack_grads_kernel, feed_sum.shape[0]),
        index,
        [whole(packed)],
        [
            ((hidden_width, ADAPT_COLS), f32, None, None),
            down_shape,
            up_shape,
            ((part_cols, WA * hidden_width), f32, None, None),
            down_shape,
            down_shape,
            up_shape,
            ((part_cols, 3 * width), f32, None, None),
        ],
    )
    return (
        output,
        tokens_grad,
        qkv_down_grad,
        qkv_up_grad,
        dense_down_grad,
        dense_up_grad,
        in_down_grad,
        in_up_grad,
        out_down_grad,
        out_up_grad,
    )


def solution(mesh):
    rows = P("wa", "ctx", None)
    shard = P("wa", None)
    in_specs = (
        (rows, rows, P(), shard, shard)
        + (P(),) * 4
        + (shard, P()) * 4
        + (shard,) * 8
    )
    out_specs = (rows, rows) + (shard,) * 8
    return jax.shard_map(
        functools.partial(body, mesh.shape["ctx"]),
        mesh=mesh,
        in_specs=in_specs,
        out_specs=out_specs,
        check_vma=False,
    )
```
